256 devices in a mesh: clus: 32 (over y, x, core), col: 8 (over z).
Axes of the slice: x: 4, y: 4, z: 8, core: 2. Of those that a mesh axis runs over, the one named last changes fastest.
Arguments:
- embeds: bfloat16 [98304, 1024], P('clus', 'col')
- cluster_ids: int32 [98304], P('clus'), may hold values from 0 to 31, as said below
- orders: int32 [98304], P('clus'), may hold values from 0 to 98303, each once
Outputs:
- maxima: float32 [98304], P('clus')
The draws below stay inside these ranges and needn't reach their ends.
Inputs may be any that keep to these rules, and one draw needn't show every extreme that they name: `cluster_ids`: within each device's block of 3072 rows no cluster is named more than 192 times, and one cluster, the same for every block, is named exactly 192 times in each block.
All inputs are finite; a program needn't handle non-finite values.
Results may differ from the reference program's by a relative error of at most 0.0003.
Values may be sent and summed in bfloat16 or wider, within the bound.
No kernel may reach another device: no remote copies, remote signals or barrier semaphores. Data moves between devices by JAX's collectives and lax.ppermute only.
A program may use at most 128 MiB of HBM per device.

```python
import jax
import jax.numpy as jnp
from jax import lax

D = 1024
ROWS_DEV = 3072
ROWS = 98304
CLUSTERS = 32
CAP = 192


def cluster_rows(key):
    key = jax.random.fold_in(key, 11)
    giant_key, block_key = jax.random.split(key)
    giant = jax.random.randint(giant_key, (), 0, CLUSTERS)

    def one_block(inner_key):
        first_key, second_key = jax.random.split(inner_key)
        others = (giant + 1 + jnp.arange(CLUSTERS - 1)) % CLUSTERS
        pool = jnp.repeat(others, CAP)
        pool = jax.random.permutation(first_key, pool)[:ROWS_DEV - CAP]
        whole = jnp.concatenate([jnp.full((CAP,), giant), pool])
        return jax.random.permutation(second_key, whole)
    block_keys = jax.random.split(block_key, ROWS // ROWS_DEV)
    return jax.vmap(one_block)(block_keys).reshape(ROWS).astype(jnp.int32)


def draw_cluster_ids(key, part):
    return cluster_rows(key)


def draw_embeds(key, part):
    members = cluster_rows(key)
    key = jax.random.fold_in(key, 7)
    center_key, weight_key, noise_key, scale_key = jax.random.split(key, 4)
    centers = jax.random.normal(center_key, (CLUSTERS, D), jnp.float32)
    weights = jax.random.uniform(weight_key, (CLUSTERS,), jnp.float32, 0.5, 1.5)
    noise = jax.random.normal(noise_key, (ROWS, D), jnp.float32)
    scales = jnp.exp(jax.random.uniform(scale_key, (ROWS, 1), jnp.float32, 0.0, 1.0))
    values = scales * (weights[members][:, None] * centers[members] + noise)
    return values.astype(jnp.bfloat16)


def setup_inputs(seed: int = 0) -> dict:
    keys = jax.random.split(jax.random.key(seed), 4)
    return {
        "embeds": draw_embeds(jax.random.fold_in(keys[3], 71), 0),
        "cluster_ids": draw_cluster_ids(jax.random.fold_in(keys[3], 71), 0),
        "orders": jax.random.permutation(keys[2], ROWS).astype(jnp.int32),
    }


never_order = 2 ** 30

def reference(embeds, cluster_ids, orders):
    member_count = 2 * ROWS_DEV
    widened = embeds.astype(jnp.float32)
    lengths = jnp.sqrt(lax.optimization_barrier(jnp.sum(widened * widened, axis=1)) + 1e-06)

    def per_cluster(cluster):
        chosen = cluster_ids == cluster
        total = jnp.sum(chosen.astype(jnp.int32))
        member_ids = jnp.nonzero(chosen, size=member_count, fill_value=0)[0].astype(jnp.int32)
        present = jnp.arange(member_count, dtype=jnp.int32) < total
        member_rows = embeds[member_ids]
        member_orders = jnp.where(present, orders[member_ids], never_order)
        member_lengths = lengths[member_ids]
        scores = jnp.dot(member_rows, member_rows.T, preferred_element_type=jnp.float32)
        similar = scores / (member_lengths[:, None] * member_lengths[None, :])
        earlier = member_orders[None, :] < member_orders[:, None]
        largest = lax.optimization_barrier(jnp.max(jnp.where(earlier, similar, jnp.float32(-1.0)), axis=1))
        return (largest, jnp.where(present, member_ids, ROWS))
    values, targets = lax.map(per_cluster, jnp.arange(CLUSTERS, dtype=jnp.int32))
    maxima = jnp.zeros((ROWS,), jnp.float32)
    return maxima.at[targets.reshape(-1)].set(values.reshape(-1), mode='drop')
```

```python
import functools

import jax
import jax.numpy as jnp
from jax import lax
from jax.experimental import pallas as pl
from jax.experimental.pallas import tpu as pltpu
from jax.sharding import Mesh, PartitionSpec as P

never_order = 2**30
low = -3e38
Y, X, C, Z = 4, 4, 2, 8
ROWS = 3072
GROUPS = 32
CAP = 192
WIDTH = 128
BLOCK = Y * CAP
HALF = BLOCK // 2
LINES = ROWS // 128
ALL = ("y", "x", "core", "z")
PARAMS = pltpu.CompilerParams(vmem_limit_bytes=40 * 2**20)
VMEM = pl.BlockSpec(memory_space=pltpu.VMEM)
SMEM = pl.BlockSpec(memory_space=pltpu.SMEM)


def routes(move):
    pairs = []
    for y in range(Y):
        for x in range(X):
            for c in range(C):
                for z in range(Z):
                    y2, x2, c2, z2 = move(y, x, c, z)
                    to = (((y2 % Y) * X + x2 % X) * C + c2 % C) * Z + z2 % Z
                    pairs.append((((y * X + x) * C + c) * Z + z, to))
    return pairs


def place_kernel(ids_ref, rows_ref, placed_ref, slot_ref, member_ref, wide_ref, out_ref, slot_sm, sem):
    r = lax.broadcasted_iota(jnp.int32, (128, 256), 0)
    c = lax.broadcasted_iota(jnp.int32, (128, 256), 1)
    weights = ((r < c) | (c >= 128)).astype(jnp.float32).astype(jnp.bfloat16)
    group = lax.broadcasted_iota(jnp.int32, (GROUPS, 128), 0)
    for i in range(LINES):
        hit = group == ids_ref[pl.ds(i, 1), :]
        member_ref[pl.ds(i * GROUPS, GROUPS), :] = hit.astype(jnp.float32).astype(jnp.bfloat16)
    counts = jnp.dot(member_ref[...], weights, preferred_element_type=jnp.float32)
    carry = jnp.zeros((GROUPS, 128), jnp.float32)
    for i in range(LINES):
        part = counts[i * GROUPS : (i + 1) * GROUPS]
        line = ids_ref[pl.ds(i, 1), :]
        within = jnp.sum(jnp.where(group == line, part[:, :128] + carry, 0.0), axis=0, keepdims=True)
        slot_ref[pl.ds(i, 1), :] = line * CAP + within.astype(jnp.int32)
        carry = carry + part[:, 128:]
    copy = pltpu.make_async_copy(slot_ref, slot_sm, sem)
    copy.start()
    wide_ref[...] = rows_ref[...].astype(jnp.float32)
    out_ref[...] = jnp.zeros_like(out_ref)
    copy.wait()

    @pl.loop(0, LINES)
    def _(i):
        for lane in range(128):
            slot = slot_sm[i, lane]
            out_ref[pl.ds(slot, 1), :] = wide_ref[pl.ds(i * 128 + lane, 1), :]

    placed_ref[...] = out_ref[...].astype(jnp.bfloat16)


def place(ids, rows):
    return pl.pallas_call(
        place_kernel,
        out_shape=(
            jax.ShapeDtypeStruct((GROUPS * CAP, WIDTH), jnp.bfloat16),
            jax.ShapeDtypeStruct((LINES, 128), jnp.int32),
        ),
        in_specs=[VMEM, VMEM],
        out_specs=(VMEM, VMEM),
        scratch_shapes=[
            pltpu.VMEM((LINES * GROUPS, 128), jnp.bfloat16),
            pltpu.VMEM((ROWS, WIDTH), jnp.float32),
            pltpu.VMEM((GROUPS * CAP, WIDTH), jnp.float32),
            pltpu.SMEM((LINES, 128), jnp.int32),
            pltpu.SemaphoreType.DMA,
        ],
        compiler_params=PARAMS,
        name="place",
    )(ids, rows)


def col_inverse(ref):
    pieces = []
    for i in range(BLOCK // 128):
        wide = ref[pl.ds(i * 128, 128), :].astype(jnp.float32)
        pieces.append(lax.rsqrt(jnp.sum(wide * wide, axis=1, keepdims=True) + 1e-06))
    return jnp.concatenate(pieces, axis=0)


def to_row(col):
    eye = lax.broadcasted_iota(jnp.int32, (128, 128), 0) == lax.broadcasted_iota(
        jnp.int32, (128, 128), 1
    )
    pieces = []
    for i in range(BLOCK // 128):
        piece = jnp.broadcast_to(col[i * 128 : (i + 1) * 128], (128, 128))
        pieces.append(jnp.max(jnp.where(eye, piece, low), axis=0, keepdims=True))
    return jnp.concatenate(pieces, axis=1)


def dot_rows(p, q):
    return lax.dot_general(p, q, (((1,), (1,)), ((), ())), preferred_element_type=jnp.float32)


def cross(p_ref, q_ref, inv_p, inv_q_ref, order_p, order_q_ref, flip, q_best_ref):
    p_parts = []
    for h in range(2):
        start = pl.multiple_of(jnp.where(flip == 0, h, 1 - h) * HALF, HALF)
        q = q_ref[pl.ds(start, HALF), :]
        inv_q = inv_q_ref[:, pl.ds(start, HALF)]
        order_q = order_q_ref[:, pl.ds(start, HALF)]
        q_best = jnp.full((1, HALF), low, jnp.float32)
        for t in range(HALF // 128):
            at = h * HALF + t * 128
            s = dot_rows(p_ref[pl.ds(at, 128), :], q)
            earlier = order_q < order_p[at : at + 128]
            inv = inv_p[at : at + 128]
            p_best = jnp.max(jnp.where(earlier, s * inv_q, low), axis=1, keepdims=True)
            p_parts.append(p_best * inv)
            q_best = jnp.maximum(
                q_best, jnp.max(jnp.where(earlier, low, s * inv), axis=0, keepdims=True)
            )
        q_best_ref[:, pl.ds(start, HALF)] = jnp.maximum(
            q_best_ref[:, pl.ds(start, HALF)], q_best * inv_q
        )
    return jnp.concatenate(p_parts, axis=0)


def first_kernel(place_ref, a0, e0, order_rows, order_cols, best, inv_rows, row_a, row_b):
    core = place_ref[1]
    inv_p = col_inverse(a0)
    inv_rows[...] = jnp.zeros_like(inv_rows)
    inv_rows[pl.ds(0, 1), :] = to_row(inv_p)
    row_a[pl.ds(0, 1), :] = to_row(col_inverse(e0))
    row_b[...] = jnp.full_like(row_b, low)
    order_p = order_cols[:, 0:1]
    order_q = order_rows[0:1, :]
    inv_q = inv_rows[0:1, :]
    parts = []
    for t in range(BLOCK // 128):
        s = dot_rows(a0[pl.ds(t * 128, 128), :], a0[...])
        earlier = order_q < order_p[t * 128 : (t + 1) * 128]
        p_best = jnp.max(jnp.where(earlier, s * inv_q, low), axis=1, keepdims=True)
        parts.append(p_best * inv_p[t * 128 : (t + 1) * 128])
    own = jnp.concatenate(parts, axis=0)
    other = cross(
        a0, e0, inv_p, row_a.at[pl.ds(0, 1)], order_p, order_rows.at[pl.ds(3, 1)], core,
        row_b.at[pl.ds(0, 1)],
    )
    best[...] = jnp.full_like(best, -1.0)
    best[pl.ds(0, 1), :] = to_row(jnp.maximum(own, other))
    best[pl.ds(3, 1), :] = row_b[pl.ds(0, 1), :]


def second_kernel(
    place_ref, a0, a1, e1, order_rows, order_cols, before, inv_before, best, inv_rows, inv_e1, row_b
):
    core = place_ref[1]
    inv_p = col_inverse(a0)
    inv_rows[...] = inv_before[...]
    inv_rows[pl.ds(1, 1), :] = to_row(col_inverse(a1))
    inv_e = col_inverse(e1)
    inv_e1[...] = jnp.broadcast_to(inv_e, inv_e1.shape)
    row_b[...] = jnp.full_like(row_b, low)
    order_p = order_cols[:, 0:1]
    order_e = order_cols[:, 4:5]
    own = cross(
        a0, a1, inv_p, inv_rows.at[pl.ds(1, 1)], order_p, order_rows.at[pl.ds(1, 1)], 0,
        row_b.at[pl.ds(1, 1)],
    )
    own_b = cross(
        a0, a1, inv_p, inv_rows.at[pl.ds(1, 1)], order_p, order_rows.at[pl.ds(1, 1)], 1,
        row_b.at[pl.ds(1, 1)],
    )
    other = cross(
        e1, a0, inv_e, inv_rows.at[pl.ds(0, 1)], order_e, order_rows.at[pl.ds(0, 1)], core,
        row_b.at[pl.ds(0, 1)],
    )
    other_b = cross(
        e1, a1, inv_e, inv_rows.at[pl.ds(1, 1)], order_e, order_rows.at[pl.ds(1, 1)], core,
        row_b.at[pl.ds(1, 1)],
    )
    best[...] = before[...]
    best[pl.ds(0, 1), :] = jnp.maximum(
        jnp.maximum(before[pl.ds(0, 1), :], row_b[pl.ds(0, 1), :]), to_row(jnp.maximum(own, own_b))
    )
    best[pl.ds(1, 1), :] = jnp.maximum(before[pl.ds(1, 1), :], row_b[pl.ds(1, 1), :])
    best[pl.ds(4, 1), :] = jnp.maximum(
        before[pl.ds(4, 1), :], to_row(jnp.maximum(other, other_b))
    )


def third_kernel(
    place_ref, a0, a2, e1, order_rows, order_cols, before, inv_rows, inv_e1, best, row_a, row_b
):
    core = place_ref[1]
    far = place_ref[2]
    row_a[pl.ds(0, 1), :] = to_row(col_inverse(a2))
    row_b[...] = jnp.full_like(row_b, low)
    inv_p = col_inverse(a0)
    own = cross(
        a0, a2, inv_p, row_a.at[pl.ds(0, 1)], order_cols[:, 0:1], order_rows.at[pl.ds(2, 1)], far,
        row_b.at[pl.ds(0, 1)],
    )
    other = cross(
        e1, a2, inv_e1[:, 0:1], row_a.at[pl.ds(0, 1)], order_cols[:, 4:5],
        order_rows.at[pl.ds(2, 1)], core, row_b.at[pl.ds(0, 1)],
    )
    best[...] = jnp.full_like(best, -1.0)
    best[pl.ds(place_ref[3], 1), :] = jnp.maximum(before[pl.ds(0, 1), :], to_row(own))
    best[pl.ds(place_ref[4], 1), :] = before[pl.ds(1, 1), :]
    best[pl.ds(place_ref[5], 1), :] = jnp.maximum(before[pl.ds(2, 1), :], row_b[pl.ds(0, 1), :])
    best[pl.ds(place_ref[6], 1), :] = before[pl.ds(3, 1), :]
    best[pl.ds(place_ref[7], 1), :] = jnp.maximum(before[pl.ds(4, 1), :], to_row(other))


def shape(*dims):
    return jax.ShapeDtypeStruct(dims, jnp.float32)


def scores_call(kernel, units, inputs, outs, scratch, name):
    return pl.pallas_call(
        kernel,
        out_shape=outs,
        in_specs=[SMEM] + [VMEM] * (len(inputs) - 1),
        out_specs=jax.tree.map(lambda _: VMEM, outs),
        scratch_shapes=scratch,
        compiler_params=PARAMS,
        cost_estimate=pl.CostEstimate(
            flops=int(units * 2 * BLOCK * BLOCK * 1024), bytes_accessed=4 * 2**20, transcendentals=0
        ),
        name=name,
    )(*inputs)


def answer_kernel(ids_ref, slot_ref, table_ref, out_ref):
    table = table_ref[...]
    high = table.astype(jnp.bfloat16)
    rest = table - high.astype(jnp.float32)
    middle = rest.astype(jnp.bfloat16)
    small = (rest - middle.astype(jnp.float32)).astype(jnp.bfloat16)
    pieces = jnp.concatenate([high, middle, small], axis=0)
    group = lax.broadcasted_iota(jnp.int32, (3 * GROUPS, 128), 0) & (GROUPS - 1)
    place_in = lax.broadcasted_iota(jnp.int32, (CAP, 128), 0)
    for i in range(LINES):
        ids = ids_ref[pl.ds(i, 1), :]
        within = slot_ref[pl.ds(i, 1), :] - ids * CAP
        where = (ids & (Z - 1)) * Y + (ids >> 3)
        member = (group == where).astype(jnp.float32).astype(jnp.bfloat16)
        found = lax.dot_general(
            pieces, member, (((0,), (0,)), ((), ())), preferred_element_type=jnp.float32
        )
        out_ref[pl.ds(i, 1), :] = jnp.sum(
            jnp.where(place_in == within, found, 0.0), axis=0, keepdims=True
        )


def answer(ids, slots, table):
    return pl.pallas_call(
        answer_kernel,
        out_shape=jax.ShapeDtypeStruct((LINES, 128), jnp.float32),
        in_specs=[VMEM] * 3,
        out_specs=VMEM,
        compiler_params=PARAMS,
        name="answer",
    )(ids, slots, table)


def shards(embeds, cluster_ids, orders):
    x, core, z = lax.axis_index("x"), lax.axis_index("core"), lax.axis_index("z")
    ids = cluster_ids.reshape(LINES, 128)
    placed, slots = place(ids, embeds)
    arrived = lax.all_to_all(
        placed.reshape(GROUPS, CAP, WIDTH), ("y", "z"), split_axis=0, concat_axis=0, tiled=True
    )
    a0 = arrived.reshape(Y, Z, CAP, WIDTH).transpose(0, 2, 1, 3).reshape(BLOCK, Z * WIDTH)

    order_slots = jnp.full((GROUPS * CAP,), never_order, jnp.int32).at[slots.reshape(ROWS)].set(orders)
    order_slots = order_slots.reshape(Y, Z, CAP)
    mine = lax.dynamic_slice_in_dim(order_slots, z, 1, 1).reshape(1, Y, CAP)
    spread = jnp.broadcast_to(mine, (X * C, Y, CAP)).reshape(GROUPS, CAP)
    member_orders = lax.all_to_all(
        spread, ("x", "core", "y"), split_axis=0, concat_axis=0, tiled=True
    ).reshape(X * C, BLOCK)
    step = jnp.where(core == 0, -1, 1)
    spots = jnp.stack(
        [
            x * 2 + core,
            ((x + step) % X) * 2 + core,
            ((x + 2) % X) * 2 + core,
            x * 2 + 1 - core,
            ((x - step) % X) * 2 + 1 - core,
        ]
    )
    place_in = jnp.concatenate([jnp.stack([x, core, x // 2]), spots]).astype(jnp.int32)
    order_rows = member_orders.astype(jnp.float32)[spots]
    order_rows = jnp.concatenate([order_rows, jnp.zeros((3, BLOCK), jnp.float32)])
    order_cols = order_rows.T

    swap = routes(lambda y, x, c, z: (y, x, 1 - c, z))
    ring = routes(lambda y, x, c, z: (y, x + (1 if c == 0 else -1), c, z))
    a1 = lax.ppermute(a0, ALL, ring)
    e0 = lax.ppermute(a0, ALL, swap)
    a2 = lax.ppermute(a1, ALL, ring)
    e1 = lax.ppermute(a1, ALL, swap)
    vector = pltpu.VMEM((8, BLOCK), jnp.float32)
    best, inv_rows = scores_call(
        first_kernel, 1.5, (place_in, a0, e0, order_rows, order_cols),
        (shape(8, BLOCK), shape(8, BLOCK)), [vector, vector], "first",
    )
    best, inv_rows, inv_e1 = scores_call(
        second_kernel, 2, (place_in, a0, a1, e1, order_rows, order_cols, best, inv_rows),
        (shape(8, BLOCK), shape(8, BLOCK), shape(BLOCK, 128)), [vector], "second",
    )
    best = scores_call(
        third_kernel, 1, (place_in, a0, a2, e1, order_rows, order_cols, best, inv_rows, inv_e1),
        shape(8, BLOCK), [vector, vector], "third",
    )
    back = lax.all_to_all(
        best.reshape(GROUPS, CAP), ("x", "core", "y"), split_axis=0, concat_axis=0, tiled=True
    )
    merged = jnp.max(back.reshape(X * C, Y, CAP), axis=0)
    table = lax.all_to_all(
        jnp.broadcast_to(merged[None], (Z, Y, CAP)), "z", split_axis=0, concat_axis=0, tiled=True
    )
    return answer(ids, slots, table.reshape(GROUPS, CAP)).reshape(ROWS)


def solution(mesh):
    fine = Mesh(mesh.devices.reshape(Y, X, C, Z), ALL)
    clus = ("y", "x", "core")
    return jax.shard_map(
        shards,
        mesh=fine,
        in_specs=(P(clus, "z"), P(clus), P(clus)),
        out_specs=P(clus),
        check_vma=False,
    )
```

```python
import functools

import jax
import jax.numpy as jnp
from jax import lax
from jax.experimental import pallas as pl
from jax.experimental.pallas import tpu as pltpu
from jax.sharding import Mesh, PartitionSpec as P

never_order = 2**30
low = -3e38
Y, X, C, Z = 4, 4, 2, 8
ROWS = 3072
GROUPS = 32
CAP = 192
WIDTH = 128
BLOCK = Y * CAP
HALF = BLOCK // 2
LINES = ROWS // 128
ALL = ("y", "x", "core", "z")
PARAMS = pltpu.CompilerParams(vmem_limit_bytes=40 * 2**20)
VMEM = pl.BlockSpec(memory_space=pltpu.VMEM)
SMEM = pl.BlockSpec(memory_space=pltpu.SMEM)


def routes(move):
    pairs = []
    for y in range(Y):
        for x in range(X):
            for c in range(C):
                for z in range(Z):
                    y2, x2, c2, z2 = move(y, x, c, z)
                    to = (((y2 % Y) * X + x2 % X) * C + c2 % C) * Z + z2 % Z
                    pairs.append((((y * X + x) * C + c) * Z + z, to))
    return pairs


def place_kernel(ids_ref, rows_ref, placed_ref, slot_ref, member_ref, wide_ref, out_ref, slot_sm, sem):
    r = lax.broadcasted_iota(jnp.int32, (128, 256), 0)
    c = lax.broadcasted_iota(jnp.int32, (128, 256), 1)
    weights = ((r < c) | (c >= 128)).astype(jnp.float32).astype(jnp.bfloat16)
    group = lax.broadcasted_iota(jnp.int32, (GROUPS, 128), 0)
    for i in range(LINES):
        hit = group == ids_ref[pl.ds(i, 1), :]
        member_ref[pl.ds(i * GROUPS, GROUPS), :] = hit.astype(jnp.float32).astype(jnp.bfloat16)
    counts = jnp.dot(member_ref[...], weights, preferred_element_type=jnp.float32)
    carry = jnp.zeros((GROUPS, 128), jnp.float32)
    for i in range(LINES):
        part = counts[i * GROUPS : (i + 1) * GROUPS]
        line = ids_ref[pl.ds(i, 1), :]
        within = jnp.sum(jnp.where(group == line, part[:, :128] + carry, 0.0), axis=0, keepdims=True)
        slot_ref[pl.ds(i, 1), :] = line * CAP + within.astype(jnp.int32)
        carry = carry + part[:, 128:]
    copy = pltpu.make_async_copy(slot_ref, slot_sm, sem)
    copy.start()
    wide_ref[...] = rows_ref[...].astype(jnp.float32)
    out_ref[...] = jnp.zeros_like(out_ref)
    copy.wait()

    @pl.loop(0, LINES)
    def _(i):
        for lane in range(128):
            slot = slot_sm[i, lane]
            out_ref[pl.ds(slot, 1), :] = wide_ref[pl.ds(i * 128 + lane, 1), :]

    placed_ref[...] = out_ref[...].astype(jnp.bfloat16)


def place(ids, rows):
    return pl.pallas_call(
        place_kernel,
        out_shape=(
            jax.ShapeDtypeStruct((GROUPS * CAP, WIDTH), jnp.bfloat16),
            jax.ShapeDtypeStruct((LINES, 128), jnp.int32),
        ),
        in_specs=[VMEM, VMEM],
        out_specs=(VMEM, VMEM),
        scratch_shapes=[
            pltpu.VMEM((LINES * GROUPS, 128), jnp.bfloat16),
            pltpu.VMEM((ROWS, WIDTH), jnp.float32),
            pltpu.VMEM((GROUPS * CAP, WIDTH), jnp.float32),
            pltpu.SMEM((LINES, 128), jnp.int32),
            pltpu.SemaphoreType.DMA,
        ],
        compiler_params=PARAMS,
        name="place",
    )(ids, rows)


def col_inverse(ref):
    pieces = []
    for i in range(BLOCK // 128):
        wide = ref[pl.ds(i * 128, 128), :].astype(jnp.float32)
        pieces.append(lax.rsqrt(jnp.sum(wide * wide, axis=1, keepdims=True) + 1e-06))
    return jnp.concatenate(pieces, axis=0)


def to_row(col):
    eye = lax.broadcasted_iota(jnp.int32, (128, 128), 0) == lax.broadcasted_iota(
        jnp.int32, (128, 128), 1
    )
    pieces = []
    for i in range(BLOCK // 128):
        piece = jnp.broadcast_to(col[i * 128 : (i + 1) * 128], (128, 128))
        pieces.append(jnp.max(jnp.where(eye, piece, low), axis=0, keepdims=True))
    return jnp.concatenate(pieces, axis=1)


def dot_rows(p, q):
    return lax.dot_general(p, q, (((1,), (1,)), ((), ())), preferred_element_type=jnp.float32)


def cross(p_ref, q_ref, inv_p, inv_q_ref, order_p, order_q_ref, flip, q_best_ref):
    p_parts = []
    for h in range(2):
        start = pl.multiple_of(jnp.where(flip == 0, h, 1 - h) * HALF, HALF)
        q = q_ref[pl.ds(start, HALF), :]
        inv_q = inv_q_ref[:, pl.ds(start, HALF)]
        order_q = order_q_ref[:, pl.ds(start, HALF)]
        q_best = jnp.full((1, HALF), low, jnp.float32)
        for t in range(HALF // 128):
            at = h * HALF + t * 128
            s = dot_rows(p_ref[pl.ds(at, 128), :], q)
            earlier = order_q < order_p[at : at + 128]
            inv = inv_p[at : at + 128]
            p_best = jnp.max(jnp.where(earlier, s * inv_q, low), axis=1, keepdims=True)
            p_parts.append(p_best * inv)
            q_best = jnp.maximum(
                q_best, jnp.max(jnp.where(earlier, low, s * inv), axis=0, keepdims=True)
            )
        q_best_ref[:, pl.ds(start, HALF)] = jnp.maximum(
            q_best_ref[:, pl.ds(start, HALF)], q_best * inv_q
        )
    return jnp.concatenate(p_parts, axis=0)


def first_kernel(place_ref, a0, e0, order_rows, order_cols, best, inv_rows, row_a, row_b):
    core = place_ref[1]
    inv_p = col_inverse(a0)
    inv_rows[...] = jnp.zeros_like(inv_rows)
    inv_rows[pl.ds(0, 1), :] = to_row(inv_p)
    row_a[pl.ds(0, 1), :] = to_row(col_inverse(e0))
    row_b[...] = jnp.full_like(row_b, low)
    order_p = order_cols[:, 0:1]
    order_q = order_rows[0:1, :]
    inv_q = inv_rows[0:1, :]
    parts = []
    for t in range(BLOCK // 128):
        s = dot_rows(a0[pl.ds(t * 128, 128), :], a0[...])
        earlier = order_q < order_p[t * 128 : (t + 1) * 128]
        p_best = jnp.max(jnp.where(earlier, s * inv_q, low), axis=1, keepdims=True)
        parts.append(p_best * inv_p[t * 128 : (t + 1) * 128])
    own = jnp.concatenate(parts, axis=0)
    other = cross(
        a0, e0, inv_p, row_a.at[pl.ds(0, 1)], order_p, order_rows.at[pl.ds(3, 1)], core,
        row_b.at[pl.ds(0, 1)],
    )
    best[...] = jnp.full_like(best, -1.0)
    best[pl.ds(0, 1), :] = to_row(jnp.maximum(own, other))
    best[pl.ds(3, 1), :] = row_b[pl.ds(0, 1), :]


def second_kernel(
    place_ref, a0, a1, e1, order_rows, order_cols, before, inv_before, best, inv_rows, inv_e1, row_b
):
    core = place_ref[1]
    inv_p = col_inverse(a0)
    inv_rows[...] = inv_before[...]
    inv_rows[pl.ds(1, 1), :] = to_row(col_inverse(a1))
    inv_e = col_inverse(e1)
    inv_e1[...] = jnp.broadcast_to(inv_e, inv_e1.shape)
    row_b[...] = jnp.full_like(row_b, low)
    order_p = order_cols[:, 0:1]
    order_e = order_cols[:, 4:5]
    own = cross(
        a0, a1, inv_p, inv_rows.at[pl.ds(1, 1)], order_p, order_rows.at[pl.ds(1, 1)], 0,
        row_b.at[pl.ds(1, 1)],
    )
    own_b = cross(
        a0, a1, inv_p, inv_rows.at[pl.ds(1, 1)], order_p, order_rows.at[pl.ds(1, 1)], 1,
        row_b.at[pl.ds(1, 1)],
    )
    other = cross(
        e1, a0, inv_e, inv_rows.at[pl.ds(0, 1)], order_e, order_rows.at[pl.ds(0, 1)], core,
        row_b.at[pl.ds(0, 1)],
    )
    other_b = cross(
        e1, a1, inv_e, inv_rows.at[pl.ds(1, 1)], order_e, order_rows.at[pl.ds(1, 1)], core,
        row_b.at[pl.ds(1, 1)],
    )
    best[...] = before[...]
    best[pl.ds(0, 1), :] = jnp.maximum(
        jnp.maximum(before[pl.ds(0, 1), :], row_b[pl.ds(0, 1), :]), to_row(jnp.maximum(own, own_b))
    )
    best[pl.ds(1, 1), :] = jnp.maximum(before[pl.ds(1, 1), :], row_b[pl.ds(1, 1), :])
    best[pl.ds(4, 1), :] = jnp.maximum(
        before[pl.ds(4, 1), :], to_row(jnp.maximum(other, other_b))
    )


def third_kernel(
    place_ref, a0, a2, e1, order_rows, order_cols, before, inv_rows, inv_e1, best, row_a, row_b
):
    core = place_ref[1]
    far = place_ref[2]
    row_a[pl.ds(0, 1), :] = to_row(col_inverse(a2))
    row_b[...] = jnp.full_like(row_b, low)
    inv_p = col_inverse(a0)
    own = cross(
        a0, a2, inv_p, row_a.at[pl.ds(0, 1)], order_cols[:, 0:1], order_rows.at[pl.ds(2, 1)], far,
        row_b.at[pl.ds(0, 1)],
    )
    other = cross(
        e1, a2, inv_e1[:, 0:1], row_a.at[pl.ds(0, 1)], order_cols[:, 4:5],
        order_rows.at[pl.ds(2, 1)], core, row_b.at[pl.ds(0, 1)],
    )
    best[...] = jnp.full_like(best, -1.0)
    best[pl.ds(place_ref[3], 1), :] = jnp.maximum(before[pl.ds(0, 1), :], to_row(own))
    best[pl.ds(place_ref[4], 1), :] = before[pl.ds(1, 1), :]
    best[pl.ds(place_ref[5], 1), :] = jnp.maximum(before[pl.ds(2, 1), :], row_b[pl.ds(0, 1), :])
    best[pl.ds(place_ref[6], 1), :] = before[pl.ds(3, 1), :]
    best[pl.ds(place_ref[7], 1), :] = jnp.maximum(before[pl.ds(4, 1), :], to_row(other))


def shape(*dims):
    return jax.ShapeDtypeStruct(dims, jnp.float32)


def scores_call(kernel, units, inputs, outs, scratch, name):
    return pl.pallas_call(
        kernel,
        out_shape=outs,
        in_specs=[SMEM] + [VMEM] * (len(inputs) - 1),
        out_specs=jax.tree.map(lambda _: VMEM, outs),
        scratch_shapes=scratch,
        compiler_params=PARAMS,
        cost_estimate=pl.CostEstimate(
            flops=int(units * 2 * BLOCK * BLOCK * 1024), bytes_accessed=4 * 2**20, transcendentals=0
        ),
        name=name,
    )(*inputs)


def answer_kernel(ids_ref, slot_ref, table_ref, out_ref):
    table = table_ref[...]
    high = table.astype(jnp.bfloat16)
    rest = table - high.astype(jnp.float32)
    middle = rest.astype(jnp.bfloat16)
    small = (rest - middle.astype(jnp.float32)).astype(jnp.bfloat16)
    pieces = jnp.concatenate([high, middle, small], axis=0)
    group = lax.broadcasted_iota(jnp.int32, (3 * GROUPS, 128), 0) & (GROUPS - 1)
    place_in = lax.broadcasted_iota(jnp.int32, (CAP, 128), 0)
    for i in range(LINES):
        ids = ids_ref[pl.ds(i, 1), :]
        within = slot_ref[pl.ds(i, 1), :] - ids * CAP
        where = (ids & (Z - 1)) * Y + (ids >> 3)
        member = (group == where).astype(jnp.float32).astype(jnp.bfloat16)
        found = lax.dot_general(
            pieces, member, (((0,), (0,)), ((), ())), preferred_element_type=jnp.float32
        )
        out_ref[pl.ds(i, 1), :] = jnp.sum(
            jnp.where(place_in == within, found, 0.0), axis=0, keepdims=True
        )


def answer(ids, slots, table):
    return pl.pallas_call(
        answer_kernel,
        out_shape=jax.ShapeDtypeStruct((LINES, 128), jnp.float32),
        in_specs=[VMEM] * 3,
        out_specs=VMEM,
        compiler_params=PARAMS,
        name="answer",
    )(ids, slots, table)


def shards(embeds, cluster_ids, orders):
    x, core, z = lax.axis_index("x"), lax.axis_index("core"), lax.axis_index("z")
    ids = cluster_ids.reshape(LINES, 128)
    placed, slots = place(ids, embeds)
    arrived = lax.all_to_all(
        placed.reshape(GROUPS, CAP, WIDTH), ("y", "z"), split_axis=0, concat_axis=0, tiled=True
    )
    order_slots = jnp.full((GROUPS * CAP,), never_order, jnp.int32).at[slots.reshape(ROWS)].set(orders)
    order_slots = order_slots.reshape(Y, Z, CAP)
    mine = lax.dynamic_slice_in_dim(order_slots, z, 1, 1).reshape(1, Y, CAP)
    spread = jnp.broadcast_to(mine, (X * C, Y, CAP)).reshape(GROUPS, CAP)
    member_orders = lax.all_to_all(
        spread, ("x", "core", "y"), split_axis=0, concat_axis=0, tiled=True
    ).reshape(X * C, BLOCK)
    step = jnp.where(core == 0, -1, 1)
    spots = jnp.stack(
        [
            x * 2 + core,
            ((x + step) % X) * 2 + core,
            ((x + 2) % X) * 2 + core,
            x * 2 + 1 - core,
            ((x - step) % X) * 2 + 1 - core,
        ]
    )
    place_in = jnp.concatenate([jnp.stack([x, core, x // 2]), spots]).astype(jnp.int32)
    order_rows = member_orders.astype(jnp.float32)[spots]
    order_rows = jnp.concatenate([order_rows, jnp.zeros((3, BLOCK), jnp.float32)])
    order_cols = order_rows.T
    arrived, order_rows, order_cols = lax.optimization_barrier((arrived, order_rows, order_cols))
    a0 = arrived.reshape(Y, Z, CAP, WIDTH).transpose(0, 2, 1, 3).reshape(BLOCK, Z * WIDTH)

    swap = routes(lambda y, x, c, z: (y, x, 1 - c, z))
    ring = routes(lambda y, x, c, z: (y, x + (1 if c == 0 else -1), c, z))
    a1 = lax.ppermute(a0, ALL, ring)
    e0 = lax.ppermute(a0, ALL, swap)
    a2 = lax.ppermute(a1, ALL, ring)
    e1 = lax.ppermute(a1, ALL, swap)
    vector = pltpu.VMEM((8, BLOCK), jnp.float32)
    best, inv_rows = scores_call(
        first_kernel, 1.5, (place_in, a0, e0, order_rows, order_cols),
        (shape(8, BLOCK), shape(8, BLOCK)), [vector, vector], "first",
    )
    best, inv_rows, inv_e1 = scores_call(
        second_kernel, 2, (place_in, a0, a1, e1, order_rows, order_cols, best, inv_rows),
        (shape(8, BLOCK), shape(8, BLOCK), shape(BLOCK, 128)), [vector], "second",
    )
    best = scores_call(
        third_kernel, 1, (place_in, a0, a2, e1, order_rows, order_cols, best, inv_rows, inv_e1),
        shape(8, BLOCK), [vector, vector], "third",
    )
    back = lax.all_to_all(
        best.reshape(GROUPS, CAP), ("x", "core", "y"), split_axis=0, concat_axis=0, tiled=True
    )
    merged = jnp.max(back.reshape(X * C, Y, CAP), axis=0)
    table = lax.all_to_all(
        jnp.broadcast_to(merged[None], (Z, Y, CAP)), "z", split_axis=0, concat_axis=0, tiled=True
    )
    return answer(ids, slots, table.reshape(GROUPS, CAP)).reshape(ROWS)


def solution(mesh):
    fine = Mesh(mesh.devices.reshape(Y, X, C, Z), ALL)
    clus = ("y", "x", "core")
    return jax.shard_map(
        shards,
        mesh=fine,
        in_specs=(P(clus, "z"), P(clus), P(clus)),
        out_specs=P(clus),
        check_vma=False,
    )
```

```python
import functools

import jax
import jax.numpy as jnp
from jax import lax
from jax.experimental import pallas as pl
from jax.experimental.pallas import tpu as pltpu
from jax.sharding import Mesh, PartitionSpec as P

never_order = 2.0**30
low = -3e38
Y, X, C, Z = 4, 4, 2, 8
ROWS = 3072
GROUPS = 32
CAP = 192
WIDTH = 128
BLOCK = Y * CAP
HALF = BLOCK // 2
LINES = ROWS // 128
ALL = ("y", "x", "core", "z")
PARAMS = pltpu.CompilerParams(vmem_limit_bytes=40 * 2**20)
VMEM = pl.BlockSpec(memory_space=pltpu.VMEM)
SMEM = pl.BlockSpec(memory_space=pltpu.SMEM)


def routes(move):
    pairs = []
    for y in range(Y):
        for x in range(X):
            for c in range(C):
                for z in range(Z):
                    y2, x2, c2, z2 = move(y, x, c, z)
                    to = (((y2 % Y) * X + x2 % X) * C + c2 % C) * Z + z2 % Z
                    pairs.append((((y * X + x) * C + c) * Z + z, to))
    return pairs


def place_kernel(ids_ref, rows_ref, placed_ref, slot_ref, member_ref, wide_ref, out_ref, slot_sm, sem):
    r = lax.broadcasted_iota(jnp.int32, (128, 256), 0)
    c = lax.broadcasted_iota(jnp.int32, (128, 256), 1)
    weights = ((r < c) | (c >= 128)).astype(jnp.float32).astype(jnp.bfloat16)
    group = lax.broadcasted_iota(jnp.int32, (GROUPS, 128), 0)
    for i in range(LINES):
        hit = group == ids_ref[pl.ds(i, 1), :]
        member_ref[pl.ds(i * GROUPS, GROUPS), :] = hit.astype(jnp.float32).astype(jnp.bfloat16)
    counts = jnp.dot(member_ref[...], weights, preferred_element_type=jnp.float32)
    carry = jnp.zeros((GROUPS, 128), jnp.float32)
    for i in range(LINES):
        part = counts[i * GROUPS : (i + 1) * GROUPS]
        line = ids_ref[pl.ds(i, 1), :]
        within = jnp.sum(jnp.where(group == line, part[:, :128] + carry, 0.0), axis=0, keepdims=True)
        slot_ref[pl.ds(i, 1), :] = line * CAP + within.astype(jnp.int32)
        carry = carry + part[:, 128:]
    copy = pltpu.make_async_copy(slot_ref, slot_sm, sem)
    copy.start()
    wide_ref[...] = rows_ref[...].astype(jnp.float32)
    out_ref[...] = jnp.zeros_like(out_ref)
    copy.wait()

    @pl.loop(0, LINES)
    def _(i):
        for lane in range(128):
            slot = slot_sm[i, lane]
            out_ref[pl.ds(slot, 1), :] = wide_ref[pl.ds(i * 128 + lane, 1), :]

    placed_ref[...] = out_ref[...].astype(jnp.bfloat16)


def place(ids, rows):
    return pl.pallas_call(
        place_kernel,
        out_shape=(
            jax.ShapeDtypeStruct((GROUPS * CAP, WIDTH), jnp.bfloat16),
            jax.ShapeDtypeStruct((LINES, 128), jnp.int32),
        ),
        in_specs=[VMEM, VMEM],
        out_specs=(VMEM, VMEM),
        scratch_shapes=[
            pltpu.VMEM((LINES * GROUPS, 128), jnp.bfloat16),
            pltpu.VMEM((ROWS, WIDTH), jnp.float32),
            pltpu.VMEM((GROUPS * CAP, WIDTH), jnp.float32),
            pltpu.SMEM((LINES, 128), jnp.int32),
            pltpu.SemaphoreType.DMA,
        ],
        compiler_params=PARAMS,
        name="place",
    )(ids, rows)


def ranks_kernel(ids_ref, slot_ref, orders_ref, table_ref):
    group = lax.broadcasted_iota(jnp.int32, (GROUPS, 128), 0)
    spot = lax.broadcasted_iota(jnp.int32, (CAP, 128), 0)
    total = jnp.zeros((3 * GROUPS, CAP), jnp.float32)
    for i in range(LINES):
        ids = ids_ref[pl.ds(i, 1), :]
        within = slot_ref[pl.ds(i, 1), :] - ids * CAP
        value = orders_ref[pl.ds(i, 1), :] + 1
        hit = group == ids
        digits = [
            jnp.where(hit, digit.astype(jnp.float32), 0.0)
            for digit in (value & 255, (value >> 8) & 255, value >> 16)
        ]
        left = jnp.concatenate(digits, axis=0).astype(jnp.bfloat16)
        right = (spot == within).astype(jnp.float32).astype(jnp.bfloat16)
        total = total + dot_rows(left, right)
    value = total[:GROUPS] + 256.0 * total[GROUPS : 2 * GROUPS] + 65536.0 * total[2 * GROUPS :]
    table_ref[...] = jnp.where(value > 0, value - 1.0, never_order)


def ranks(ids, slots, orders):
    return pl.pallas_call(
        ranks_kernel,
        out_shape=jax.ShapeDtypeStruct((GROUPS, CAP), jnp.float32),
        in_specs=[VMEM] * 3,
        out_specs=VMEM,
        compiler_params=PARAMS,
        name="ranks",
    )(ids, slots, orders)


def col_inverse(ref):
    pieces = []
    for i in range(BLOCK // 128):
        wide = ref[pl.ds(i * 128, 128), :].astype(jnp.float32)
        pieces.append(lax.rsqrt(jnp.sum(wide * wide, axis=1, keepdims=True) + 1e-06))
    return jnp.concatenate(pieces, axis=0)


def to_row(col):
    eye = lax.broadcasted_iota(jnp.int32, (128, 128), 0) == lax.broadcasted_iota(
        jnp.int32, (128, 128), 1
    )
    pieces = []
    for i in range(BLOCK // 128):
        piece = jnp.broadcast_to(col[i * 128 : (i + 1) * 128], (128, 128))
        pieces.append(jnp.max(jnp.where(eye, piece, low), axis=0, keepdims=True))
    return jnp.concatenate(pieces, axis=1)


def dot_rows(p, q):
    return lax.dot_general(p, q, (((1,), (1,)), ((), ())), preferred_element_type=jnp.float32)


def cross(p_ref, q_ref, inv_p, inv_q_ref, order_p, order_q_ref, flip, q_best_ref):
    p_parts = []
    for h in range(2):
        start = pl.multiple_of(jnp.where(flip == 0, h, 1 - h) * HALF, HALF)
        q = q_ref[pl.ds(start, HALF), :]
        inv_q = inv_q_ref[:, pl.ds(start, HALF)]
        order_q = order_q_ref[:, pl.ds(start, HALF)]
        q_best = jnp.full((1, HALF), low, jnp.float32)
        for t in range(HALF // 128):
            at = h * HALF + t * 128
            s = dot_rows(p_ref[pl.ds(at, 128), :], q)
            earlier = order_q < order_p[at : at + 128]
            inv = inv_p[at : at + 128]
            p_best = jnp.max(jnp.where(earlier, s * inv_q, low), axis=1, keepdims=True)
            p_parts.append(p_best * inv)
            q_best = jnp.maximum(
                q_best, jnp.max(jnp.where(earlier, low, s * inv), axis=0, keepdims=True)
            )
        q_best_ref[:, pl.ds(start, HALF)] = jnp.maximum(
            q_best_ref[:, pl.ds(start, HALF)], q_best * inv_q
        )
    return jnp.concatenate(p_parts, axis=0)


def first_kernel(place_ref, a0, e0, order_rows, order_cols, best, inv_rows, row_a, row_b):
    core = place_ref[1]
    inv_p = col_inverse(a0)
    inv_rows[...] = jnp.zeros_like(inv_rows)
    inv_rows[pl.ds(0, 1), :] = to_row(inv_p)
    row_a[pl.ds(0, 1), :] = to_row(col_inverse(e0))
    row_b[...] = jnp.full_like(row_b, low)
    order_p = order_cols[:, 0:1]
    order_q = order_rows[0:1, :]
    inv_q = inv_rows[0:1, :]
    parts = []
    for t in range(BLOCK // 128):
        s = dot_rows(a0[pl.ds(t * 128, 128), :], a0[...])
        earlier = order_q < order_p[t * 128 : (t + 1) * 128]
        p_best = jnp.max(jnp.where(earlier, s * inv_q, low), axis=1, keepdims=True)
        parts.append(p_best * inv_p[t * 128 : (t + 1) * 128])
    own = jnp.concatenate(parts, axis=0)
    other = cross(
        a0, e0, inv_p, row_a.at[pl.ds(0, 1)], order_p, order_rows.at[pl.ds(3, 1)], core,
        row_b.at[pl.ds(0, 1)],
    )
    best[...] = jnp.full_like(best, -1.0)
    best[pl.ds(0, 1), :] = to_row(jnp.maximum(own, other))
    best[pl.ds(3, 1), :] = row_b[pl.ds(0, 1), :]


def second_kernel(
    place_ref, a0, a1, e1, order_rows, order_cols, before, inv_before, best, inv_rows, inv_e1, row_b
):
    core = place_ref[1]
    inv_p = col_inverse(a0)
    inv_rows[...] = inv_before[...]
    inv_rows[pl.ds(1, 1), :] = to_row(col_inverse(a1))
    inv_e = col_inverse(e1)
    inv_e1[...] = jnp.broadcast_to(inv_e, inv_e1.shape)
    row_b[...] = jnp.full_like(row_b, low)
    order_p = order_cols[:, 0:1]
    order_e = order_cols[:, 4:5]
    own = cross(
        a0, a1, inv_p, inv_rows.at[pl.ds(1, 1)], order_p, order_rows.at[pl.ds(1, 1)], 0,
        row_b.at[pl.ds(1, 1)],
    )
    own_b = cross(
        a0, a1, inv_p, inv_rows.at[pl.ds(1, 1)], order_p, order_rows.at[pl.ds(1, 1)], 1,
        row_b.at[pl.ds(1, 1)],
    )
    other = cross(
        e1, a0, inv_e, inv_rows.at[pl.ds(0, 1)], order_e, order_rows.at[pl.ds(0, 1)], core,
        row_b.at[pl.ds(0, 1)],
    )
    other_b = cross(
        e1, a1, inv_e, inv_rows.at[pl.ds(1, 1)], order_e, order_rows.at[pl.ds(1, 1)], core,
        row_b.at[pl.ds(1, 1)],
    )
    best[...] = before[...]
    best[pl.ds(0, 1), :] = jnp.maximum(
        jnp.maximum(before[pl.ds(0, 1), :], row_b[pl.ds(0, 1), :]), to_row(jnp.maximum(own, own_b))
    )
    best[pl.ds(1, 1), :] = jnp.maximum(before[pl.ds(1, 1), :], row_b[pl.ds(1, 1), :])
    best[pl.ds(4, 1), :] = jnp.maximum(
        before[pl.ds(4, 1), :], to_row(jnp.maximum(other, other_b))
    )


def third_kernel(
    place_ref, a0, a2, e1, order_rows, order_cols, before, inv_rows, inv_e1, best, row_a, row_b
):
    core = place_ref[1]
    far = place_ref[2]
    row_a[pl.ds(0, 1), :] = to_row(col_inverse(a2))
    row_b[...] = jnp.full_like(row_b, low)
    inv_p = col_inverse(a0)
    own = cross(
        a0, a2, inv_p, row_a.at[pl.ds(0, 1)], order_cols[:, 0:1], order_rows.at[pl.ds(2, 1)], far,
        row_b.at[pl.ds(0, 1)],
    )
    other = cross(
        e1, a2, inv_e1[:, 0:1], row_a.at[pl.ds(0, 1)], order_cols[:, 4:5],
        order_rows.at[pl.ds(2, 1)], core, row_b.at[pl.ds(0, 1)],
    )
    best[...] = jnp.full_like(best, -1.0)
    best[pl.ds(place_ref[3], 1), :] = jnp.maximum(before[pl.ds(0, 1), :], to_row(own))
    best[pl.ds(place_ref[4], 1), :] = before[pl.ds(1, 1), :]
    best[pl.ds(place_ref[5], 1), :] = jnp.maximum(before[pl.ds(2, 1), :], row_b[pl.ds(0, 1), :])
    best[pl.ds(place_ref[6], 1), :] = before[pl.ds(3, 1), :]
    best[pl.ds(place_ref[7], 1), :] = jnp.maximum(before[pl.ds(4, 1), :], to_row(other))


def shape(*dims):
    return jax.ShapeDtypeStruct(dims, jnp.float32)


def scores_call(kernel, units, inputs, outs, scratch, name):
    return pl.pallas_call(
        kernel,
        out_shape=outs,
        in_specs=[SMEM] + [VMEM] * (len(inputs) - 1),
        out_specs=jax.tree.map(lambda _: VMEM, outs),
        scratch_shapes=scratch,
        compiler_params=PARAMS,
        cost_estimate=pl.CostEstimate(
            flops=int(units * 2 * BLOCK * BLOCK * 1024), bytes_accessed=4 * 2**20, transcendentals=0
        ),
        name=name,
    )(*inputs)


def answer_kernel(ids_ref, slot_ref, table_ref, out_ref):
    table = table_ref[...]
    high = table.astype(jnp.bfloat16)
    rest = table - high.astype(jnp.float32)
    middle = rest.astype(jnp.bfloat16)
    small = (rest - middle.astype(jnp.float32)).astype(jnp.bfloat16)
    pieces = jnp.concatenate([high, middle, small], axis=0)
    group = lax.broadcasted_iota(jnp.int32, (3 * GROUPS, 128), 0) & (GROUPS - 1)
    place_in = lax.broadcasted_iota(jnp.int32, (CAP, 128), 0)
    for i in range(LINES):
        ids = ids_ref[pl.ds(i, 1), :]
        within = slot_ref[pl.ds(i, 1), :] - ids * CAP
        where = (ids & (Z - 1)) * Y + (ids >> 3)
        member = (group == where).astype(jnp.float32).astype(jnp.bfloat16)
        found = lax.dot_general(
            pieces, member, (((0,), (0,)), ((), ())), preferred_element_type=jnp.float32
        )
        out_ref[pl.ds(i, 1), :] = jnp.sum(
            jnp.where(place_in == within, found, 0.0), axis=0, keepdims=True
        )


def answer(ids, slots, table):
    return pl.pallas_call(
        answer_kernel,
        out_shape=jax.ShapeDtypeStruct((LINES, 128), jnp.float32),
        in_specs=[VMEM] * 3,
        out_specs=VMEM,
        compiler_params=PARAMS,
        name="answer",
    )(ids, slots, table)


def shards(embeds, cluster_ids, orders):
    y, x, core, z = (lax.axis_index(name) for name in ALL)
    ids = cluster_ids.reshape(LINES, 128)
    placed, slots = place(ids, embeds)
    arrived = lax.all_to_all(
        placed.reshape(GROUPS, CAP, WIDTH), ("y", "z"), split_axis=0, concat_axis=0, tiled=True
    )
    tables = lax.all_gather(ranks(ids, slots, orders.reshape(LINES, 128)), ("y", "x", "core"))
    mine = lax.dynamic_index_in_dim(tables, y * Z + z, 1, keepdims=False)
    member_orders = mine.reshape(Y, X * C, CAP).transpose(1, 0, 2).reshape(X * C, BLOCK)
    step = jnp.where(core == 0, -1, 1)
    spots = jnp.stack(
        [
            x * 2 + core,
            ((x + step) % X) * 2 + core,
            ((x + 2) % X) * 2 + core,
            x * 2 + 1 - core,
            ((x - step) % X) * 2 + 1 - core,
        ]
    )
    place_in = jnp.concatenate([jnp.stack([x, core, x // 2]), spots]).astype(jnp.int32)
    order_rows = member_orders[spots]
    order_rows = jnp.concatenate([order_rows, jnp.zeros((3, BLOCK), jnp.float32)])
    order_cols = order_rows.T
    arrived, order_rows, order_cols = lax.optimization_barrier((arrived, order_rows, order_cols))
    a0 = arrived.reshape(Y, Z, CAP, WIDTH).transpose(0, 2, 1, 3).reshape(BLOCK, Z * WIDTH)

    swap = routes(lambda y, x, c, z: (y, x, 1 - c, z))
    ring = routes(lambda y, x, c, z: (y, x + (1 if c == 0 else -1), c, z))
    a1 = lax.ppermute(a0, ALL, ring)
    e0 = lax.ppermute(a0, ALL, swap)
    a2 = lax.ppermute(a1, ALL, ring)
    e1 = lax.ppermute(a1, ALL, swap)
    vector = pltpu.VMEM((8, BLOCK), jnp.float32)
    best, inv_rows = scores_call(
        first_kernel, 1.5, (place_in, a0, e0, order_rows, order_cols),
        (shape(8, BLOCK), shape(8, BLOCK)), [vector, vector], "first",
    )
    best, inv_rows, inv_e1 = scores_call(
        second_kernel, 2, (place_in, a0, a1, e1, order_rows, order_cols, best, inv_rows),
        (shape(8, BLOCK), shape(8, BLOCK), shape(BLOCK, 128)), [vector], "second",
    )
    best = scores_call(
        third_kernel, 1, (place_in, a0, a2, e1, order_rows, order_cols, best, inv_rows, inv_e1),
        shape(8, BLOCK), [vector, vector], "third",
    )
    back = lax.all_to_all(
        best.reshape(GROUPS, CAP), ("x", "core", "y"), split_axis=0, concat_axis=0, tiled=True
    )
    merged = jnp.max(back.reshape(X * C, Y, CAP), axis=0)
    table = lax.all_to_all(
        jnp.broadcast_to(merged[None], (Z, Y, CAP)), "z", split_axis=0, concat_axis=0, tiled=True
    )
    return answer(ids, slots, table.reshape(GROUPS, CAP)).reshape(ROWS)


def solution(mesh):
    fine = Mesh(mesh.devices.reshape(Y, X, C, Z), ALL)
    clus = ("y", "x", "core")
    return jax.shard_map(
        shards,
        mesh=fine,
        in_specs=(P(clus, "z"), P(clus), P(clus)),
        out_specs=P(clus),
        check_vma=False,
    )
```

```python
import functools

import jax
import jax.numpy as jnp
from jax import lax
from jax.experimental import pallas as pl
from jax.experimental.pallas import tpu as pltpu
from jax.sharding import Mesh, PartitionSpec as P

never_order = 2.0**30
low = -3e38
Y, X, C, Z = 4, 4, 2, 8
ROWS = 3072
GROUPS = 32
CAP = 192
WIDTH = 128
PARTS = (128, 64)
SIZES = (Y * 128, Y * 64)
META = 16
LINES = ROWS // 128
ALL = ("y", "x", "core", "z")
PARAMS = pltpu.CompilerParams(vmem_limit_bytes=40 * 2**20)
VMEM = pl.BlockSpec(memory_space=pltpu.VMEM)
SMEM = pl.BlockSpec(memory_space=pltpu.SMEM)


def routes(move):
    pairs = []
    for y in range(Y):
        for x in range(X):
            for c in range(C):
                for z in range(Z):
                    y2, x2, c2, z2 = move(y, x, c, z)
                    to = (((y2 % Y) * X + x2 % X) * C + c2 % C) * Z + z2 % Z
                    pairs.append((((y * X + x) * C + c) * Z + z, to))
    return pairs


def place_kernel(
    ids_any, rows_any, first_ref, second_ref, slot_ref,
    ids_ref, rows_ref, member_ref, wide_ref, out_ref, spot_ref, spot_sm, sems,
):
    ids_copy = pltpu.make_async_copy(ids_any, ids_ref, sems.at[0])
    rows_copy = pltpu.make_async_copy(rows_any, rows_ref, sems.at[1])
    ids_copy.start()
    rows_copy.start()
    out_ref[...] = jnp.zeros_like(out_ref)
    r = lax.broadcasted_iota(jnp.int32, (128, 256), 0)
    c = lax.broadcasted_iota(jnp.int32, (128, 256), 1)
    weights = ((r < c) | (c >= 128)).astype(jnp.float32).astype(jnp.bfloat16)
    group = lax.broadcasted_iota(jnp.int32, (GROUPS, 128), 0)
    ids_copy.wait()
    for i in range(LINES):
        hit = group == ids_ref[pl.ds(i, 1), :]
        member_ref[pl.ds(i * GROUPS, GROUPS), :] = hit.astype(jnp.float32).astype(jnp.bfloat16)
    counts = jnp.dot(member_ref[...], weights, preferred_element_type=jnp.float32)
    carry = jnp.zeros((GROUPS, 128), jnp.float32)
    for i in range(LINES):
        part = counts[i * GROUPS : (i + 1) * GROUPS]
        line = ids_ref[pl.ds(i, 1), :]
        within = jnp.sum(jnp.where(group == line, part[:, :128] + carry, 0.0), axis=0, keepdims=True)
        within = within.astype(jnp.int32)
        slot_ref[pl.ds(i, 1), :] = line * CAP + within
        spot_ref[pl.ds(i, 1), :] = jnp.where(
            within < PARTS[0],
            line * PARTS[0] + within,
            GROUPS * PARTS[0] + line * PARTS[1] + within - PARTS[0],
        )
        carry = carry + part[:, 128:]
    copy = pltpu.make_async_copy(spot_ref, spot_sm, sems.at[2])
    copy.start()
    rows_copy.wait()
    wide_ref[...] = rows_ref[...].astype(jnp.float32)
    copy.wait()

    @pl.loop(0, LINES)
    def _(i):
        for lane in range(128):
            spot = spot_sm[i, lane]
            out_ref[pl.ds(spot, 1), :] = wide_ref[pl.ds(i * 128 + lane, 1), :]

    split = GROUPS * PARTS[0]
    first_ref[...] = out_ref[pl.ds(0, split), :].astype(jnp.bfloat16)
    second_ref[...] = out_ref[pl.ds(split, GROUPS * PARTS[1]), :].astype(jnp.bfloat16)


def place(ids, rows):
    return pl.pallas_call(
        place_kernel,
        out_shape=(
            jax.ShapeDtypeStruct((GROUPS * PARTS[0], WIDTH), jnp.bfloat16),
            jax.ShapeDtypeStruct((GROUPS * PARTS[1], WIDTH), jnp.bfloat16),
            jax.ShapeDtypeStruct((LINES, 128), jnp.int32),
        ),
        in_specs=[pl.BlockSpec(memory_space=pl.ANY)] * 2,
        out_specs=(VMEM, VMEM, VMEM),
        scratch_shapes=[
            pltpu.VMEM((LINES, 128), jnp.int32),
            pltpu.VMEM((ROWS, WIDTH), jnp.bfloat16),
            pltpu.VMEM((LINES * GROUPS, 128), jnp.bfloat16),
            pltpu.VMEM((ROWS, WIDTH), jnp.float32),
            pltpu.VMEM((GROUPS * CAP, WIDTH), jnp.float32),
            pltpu.VMEM((LINES, 128), jnp.int32),
            pltpu.SMEM((LINES, 128), jnp.int32),
            pltpu.SemaphoreType.DMA((3,)),
        ],
        compiler_params=PARAMS,
        name="place",
    )(ids, rows)


def ranks_kernel(ids_ref, slot_ref, orders_ref, table_ref):
    group = lax.broadcasted_iota(jnp.int32, (GROUPS, 128), 0)
    spot = lax.broadcasted_iota(jnp.int32, (CAP, 128), 0)
    total = jnp.zeros((3 * GROUPS, CAP), jnp.float32)
    for i in range(LINES):
        ids = ids_ref[pl.ds(i, 1), :]
        within = slot_ref[pl.ds(i, 1), :] - ids * CAP
        value = orders_ref[pl.ds(i, 1), :] + 1
        hit = group == ids
        digits = [
            jnp.where(hit, digit.astype(jnp.float32), 0.0)
            for digit in (value & 255, (value >> 8) & 255, value >> 16)
        ]
        left = jnp.concatenate(digits, axis=0).astype(jnp.bfloat16)
        right = (spot == within).astype(jnp.float32).astype(jnp.bfloat16)
        total = total + dot_rows(left, right)
    value = total[:GROUPS] + 256.0 * total[GROUPS : 2 * GROUPS] + 65536.0 * total[2 * GROUPS :]
    table_ref[...] = value


def ranks(ids, slots, orders):
    return pl.pallas_call(
        ranks_kernel,
        out_shape=jax.ShapeDtypeStruct((GROUPS, CAP), jnp.float32),
        in_specs=[VMEM] * 3,
        out_specs=VMEM,
        compiler_params=PARAMS,
        name="ranks",
    )(ids, slots, orders)


def dot_rows(p, q):
    return lax.dot_general(p, q, (((1,), (1,)), ((), ())), preferred_element_type=jnp.float32)


def eye():
    r = lax.broadcasted_iota(jnp.int32, (128, 128), 0)
    return r == lax.broadcasted_iota(jnp.int32, (128, 128), 1)


def to_row(col):
    pieces = []
    for i in range(col.shape[0] // 128):
        piece = jnp.broadcast_to(col[i * 128 : (i + 1) * 128], (128, 128))
        pieces.append(jnp.max(jnp.where(eye(), piece, low), axis=0, keepdims=True))
    return jnp.concatenate(pieces, axis=1)


def to_col(row):
    pieces = []
    for i in range(row.shape[1] // 128):
        piece = jnp.broadcast_to(row[:, i * 128 : (i + 1) * 128], (128, 128))
        pieces.append(jnp.max(jnp.where(eye(), piece, low), axis=1, keepdims=True))
    return jnp.concatenate(pieces, axis=0)


def gather_kernel(size, in_ref, rank_ref, out_ref, meta_ref):
    part = size // Y
    cols = []
    for y in range(Y):
        total = jnp.zeros((part, WIDTH), jnp.float32)
        for z in range(Z):
            piece = in_ref[pl.ds((y * Z + z) * part, part), :]
            out_ref[pl.ds(y * part, part), pl.ds(z * WIDTH, WIDTH)] = piece
            wide = piece.astype(jnp.float32)
            total = total + wide * wide
        cols.append(lax.rsqrt(jnp.sum(total, axis=1, keepdims=True) + 1e-06))
    inverse = to_row(jnp.concatenate(cols, axis=0))
    high = inverse.astype(jnp.bfloat16).astype(jnp.float32)
    middle = (inverse - high).astype(jnp.bfloat16).astype(jnp.float32)
    rank = rank_ref[...].astype(jnp.int32)
    lines = (high, middle, inverse - high - middle, rank & 255, (rank >> 8) & 255, rank >> 16)
    meta_ref[...] = jnp.zeros_like(meta_ref)
    for i, line in enumerate(lines):
        meta_ref[pl.ds(i, 1), pl.ds(0, size)] = line.astype(jnp.float32)
    out_ref[pl.ds(size, META), :] = meta_ref[...].astype(jnp.bfloat16)


def gather(size, arrived, rank):
    return pl.pallas_call(
        functools.partial(gather_kernel, size),
        out_shape=jax.ShapeDtypeStruct((size + META, Z * WIDTH), jnp.bfloat16),
        in_specs=[VMEM] * 2,
        out_specs=VMEM,
        scratch_shapes=[pltpu.VMEM((META, Z * WIDTH), jnp.float32)],
        compiler_params=PARAMS,
        name="gather",
    )(arrived, rank)


def size_of(ref):
    return ref.shape[0] - META


def row_meta(ref):
    size = size_of(ref)
    meta = ref[pl.ds(size, META), pl.ds(0, size)].astype(jnp.float32)
    rank = meta[3:4] + 256.0 * meta[4:5] + 65536.0 * meta[5:6]
    return meta[0:1] + meta[1:2] + meta[2:3], jnp.where(rank > 0, rank, never_order)


def meet(best, p_name, p_ref, others):
    size = size_of(p_ref)
    inv_p, rank_p = (to_col(row) for row in row_meta(p_ref))
    p_best = jnp.full((size, 128), low, jnp.float32)
    for q_name, q_ref in others:
        inv_q, rank_q = row_meta(q_ref)
        q_best = []
        for j in range(0, size_of(q_ref), 256):
            s = dot_rows(p_ref[pl.ds(0, size), :], q_ref[pl.ds(j, 256), :])
            s = s * inv_p * inv_q[:, j : j + 256]
            earlier = rank_q[:, j : j + 256] < rank_p
            mine = jnp.where(earlier, s, low)
            p_best = jnp.maximum(p_best, jnp.maximum(mine[:, :128], mine[:, 128:]))
            if q_name != p_name:
                q_best.append(jnp.max(jnp.where(earlier, low, s), axis=0, keepdims=True))
        if q_best:
            record(best, q_name, jnp.concatenate(q_best, axis=1))
    record(best, p_name, to_row(jnp.max(p_best, axis=1, keepdims=True)))


def record(best, name, row):
    at = (pl.ds(name, 1), pl.ds(0, row.shape[1]))
    best[at] = jnp.maximum(best[at], row)


O1, O2, U1, U2, V1, V2, E1, E2, W1, W2 = range(10)


def first_kernel(spots, o1, u1, v1, e1, w1, best):
    best[...] = jnp.full_like(best, -1.0)
    meet(best, O1, o1, [(O1, o1), (U1, u1)])

    @pl.when(spots[0] == 0)
    def _():
        meet(best, E1, e1, [(V1, v1)])

    @pl.when(spots[0] != 0)
    def _():
        meet(best, E1, e1, [(U1, u1)])

    @pl.when(spots[1] != 0)
    def _():
        meet(best, U1, u1, [(V1, v1)])

    @pl.when(spots[1] == 0)
    def _():
        meet(best, U1, u1, [(W1, w1)])


def second_kernel(spots, o1, o2, u1, v1, e1, e2, before, best):
    best[...] = before[...]
    meet(best, O2, o2, [(O1, o1), (O2, o2), (U1, u1), (V1, v1)])
    meet(best, E2, e2, [(O1, o1), (U1, u1), (V1, v1)])

    @pl.when(spots[0] == 0)
    def _():
        meet(best, O1, o1, [(E1, e1)])

    @pl.when(spots[0] != 0)
    def _():
        meet(best, O2, o2, [(E2, e2)])


def third_kernel(spots, o2, u2, v2, e2, before, best):
    best[...] = before[...]
    meet(best, O2, o2, [(U2, u2)])

    @pl.when(spots[0] == 0)
    def _():
        meet(best, E2, e2, [(V2, v2)])

    @pl.when(spots[0] != 0)
    def _():
        meet(best, E2, e2, [(U2, u2)])


def fourth_kernel(spots, u1, u2, v1, v2, w1, w2, before, out, best, long, short):
    best[...] = before[...]

    @pl.when(spots[1] != 0)
    def _():
        meet(best, U1, u1, [(V2, v2)])
        meet(best, U2, u2, [(V1, v1), (V2, v2)])

    @pl.when(spots[1] == 0)
    def _():
        meet(best, U1, u1, [(W2, w2)])
        meet(best, U2, u2, [(W1, w1), (W2, w2)])

    long[...] = jnp.full_like(long, -1.0)
    short[...] = jnp.full_like(short, -1.0)
    for i in range(5):
        for y in range(Y):
            at = pl.ds(spots[2 + i] * Y + y, 1)
            long[at, :] = best[pl.ds(2 * i, 1), pl.ds(y * PARTS[0], PARTS[0])]
            pair = best[pl.ds(2 * i + 1, 1), pl.ds(y // 2 * 128, 128)]
            short[at, :] = pltpu.roll(pair, 64, 1) if y % 2 else pair
    out[:, pl.ds(0, PARTS[0])] = long[...]
    out[:, pl.ds(PARTS[0], PARTS[1])] = short[:, pl.ds(0, PARTS[1])]


def scores_call(kernel, units, inputs, out, scratch, name):
    return pl.pallas_call(
        kernel,
        out_shape=jax.ShapeDtypeStruct(out, jnp.float32),
        in_specs=[SMEM] + [VMEM] * (len(inputs) - 1),
        out_specs=VMEM,
        scratch_shapes=scratch,
        compiler_params=PARAMS,
        cost_estimate=pl.CostEstimate(
            flops=int(units * 2 * 256 * 256 * 1024), bytes_accessed=4 * 2**20, transcendentals=0
        ),
        name=name,
    )(*inputs)


def answer_kernel(ids_ref, slot_ref, table_ref, out_ref):
    table = table_ref[...]
    high = table.astype(jnp.bfloat16)
    rest = table - high.astype(jnp.float32)
    middle = rest.astype(jnp.bfloat16)
    small = (rest - middle.astype(jnp.float32)).astype(jnp.bfloat16)
    pieces = jnp.concatenate([high, middle, small], axis=0)
    group = lax.broadcasted_iota(jnp.int32, (3 * GROUPS, 128), 0) & (GROUPS - 1)
    place_in = lax.broadcasted_iota(jnp.int32, (CAP, 128), 0)
    for i in range(LINES):
        ids = ids_ref[pl.ds(i, 1), :]
        within = slot_ref[pl.ds(i, 1), :] - ids * CAP
        where = (ids & (Z - 1)) * Y + (ids >> 3)
        member = (group == where).astype(jnp.float32).astype(jnp.bfloat16)
        found = lax.dot_general(
            pieces, member, (((0,), (0,)), ((), ())), preferred_element_type=jnp.float32
        )
        out_ref[pl.ds(i, 1), :] = jnp.sum(
            jnp.where(place_in == within, found, 0.0), axis=0, keepdims=True
        )


def answer(ids, slots, table):
    return pl.pallas_call(
        answer_kernel,
        out_shape=jax.ShapeDtypeStruct((LINES, 128), jnp.float32),
        in_specs=[VMEM] * 3,
        out_specs=VMEM,
        compiler_params=PARAMS,
        name="answer",
    )(ids, slots, table)


def shards(embeds, cluster_ids, orders):
    y, x, core, z = (lax.axis_index(name) for name in ALL)
    ids = cluster_ids.reshape(LINES, 128)
    *placed, slots = place(ids, embeds)
    arrived = [
        lax.all_to_all(
            rows.reshape(GROUPS, part, WIDTH), ("y", "z"), split_axis=0, concat_axis=0, tiled=True
        ).reshape(GROUPS * part, WIDTH)
        for rows, part in zip(placed, PARTS)
    ]

    table = ranks(ids, slots, orders.reshape(LINES, 128)).reshape(Y, Z, CAP)
    table = lax.dynamic_index_in_dim(table, z, 1, keepdims=False)
    rank_parts = []
    for j in range(Y):
        row = lax.dynamic_slice_in_dim(table, (y + j) % Y, 1, 0)
        if j:
            row = lax.ppermute(row, ALL, routes(lambda y, x, c, z: (y + j, x, c, z)))
        rank_parts.append(row)
    member_ranks = jnp.concatenate(rank_parts)[(y - jnp.arange(Y)) % Y]
    rank1 = member_ranks[:, : PARTS[0]].reshape(1, SIZES[0])
    rank2 = member_ranks[:, PARTS[0] :].reshape(1, SIZES[1])

    step = 1 - 2 * core
    near, far = (x - step) % X, (x + step) % X
    spots = jnp.stack(
        [
            core,
            ((x < X // 2) == (core == 0)).astype(jnp.int32),
            x * C + core,
            near * C + core,
            far * C + core,
            x * C + 1 - core,
            far * C + 1 - core,
        ]
    ).astype(jnp.int32)

    swap = routes(lambda y, x, c, z: (y, x, 1 - c, z))
    ahead = routes(lambda y, x, c, z: (y, x + 1 - 2 * c, c, z))
    behind = routes(lambda y, x, c, z: (y, x - 1 + 2 * c, c, z))

    def share(own, after=()):
        u = lax.ppermute(own, ALL, ahead)
        v = lax.ppermute(own, ALL, behind)
        e = lax.ppermute(own, ALL, swap)
        u, *after = lax.optimization_barrier((u, *after))
        return (u, v, e, lax.ppermute(u, ALL, swap), *after)

    o1 = gather(SIZES[0], arrived[0], rank1)
    u1, v1, e1, w1, later = share(o1, (arrived[1],))
    o2 = gather(SIZES[1], later, rank2)
    u2, v2, e2, w2 = share(o2)
    best = scores_call(first_kernel, 16, (spots, o1, u1, v1, e1, w1), (16, SIZES[0]), [], "first")
    best = scores_call(
        second_kernel, 17, (spots, o1, o2, u1, v1, e1, e2, best), (16, SIZES[0]), [], "second"
    )
    best = scores_call(third_kernel, 2, (spots, o2, u2, v2, e2, best), (16, SIZES[0]), [], "third")
    best = scores_call(
        fourth_kernel, 5, (spots, u1, u2, v1, v2, w1, w2, best), (GROUPS, CAP),
        [pltpu.VMEM(size, jnp.float32) for size in ((16, SIZES[0]), (GROUPS, 128), (GROUPS, 128))],
        "fourth",
    )
    back = lax.all_to_all(best, ("x", "core", "y"), split_axis=0, concat_axis=0, tiled=True)
    merged = jnp.max(back.reshape(X * C, Y, CAP), axis=0)
    table = lax.all_to_all(
        jnp.broadcast_to(merged[None], (Z, Y, CAP)), "z", split_axis=0, concat_axis=0, tiled=True
    )
    return answer(ids, slots, table.reshape(GROUPS, CAP)).reshape(ROWS)


def solution(mesh):
    fine = Mesh(mesh.devices.reshape(Y, X, C, Z), ALL)
    clus = ("y", "x", "core")
    return jax.shard_map(
        shards,
        mesh=fine,
        in_specs=(P(clus, "z"), P(clus), P(clus)),
        out_specs=P(clus),
        check_vma=False,
    )
```

```python
import functools

import jax
import jax.numpy as jnp
from jax import lax
from jax.experimental import pallas as pl
from jax.experimental.pallas import tpu as pltpu
from jax.sharding import Mesh, PartitionSpec as P

never_order = 2.0**30
low = -3e38
Y, X, C, Z = 4, 4, 2, 8
ROWS = 3072
GROUPS = 32
CAP = 192
WIDTH = 128
PARTS = (128, 64)
SIZES = (Y * 128, Y * 64)
META = 16
LINES = ROWS // 128
ALL = ("y", "x", "core", "z")
PARAMS = pltpu.CompilerParams(vmem_limit_bytes=40 * 2**20)
VMEM = pl.BlockSpec(memory_space=pltpu.VMEM)
SMEM = pl.BlockSpec(memory_space=pltpu.SMEM)


def routes(move):
    pairs = []
    for y in range(Y):
        for x in range(X):
            for c in range(C):
                for z in range(Z):
                    y2, x2, c2, z2 = move(y, x, c, z)
                    to = (((y2 % Y) * X + x2 % X) * C + c2 % C) * Z + z2 % Z
                    pairs.append((((y * X + x) * C + c) * Z + z, to))
    return pairs


def place_kernel(
    ids_any, rows_any, first_ref, second_ref, slot_ref,
    ids_ref, rows_ref, member_ref, wide_ref, out_ref, spot_ref, spot_sm, sems,
):
    ids_copy = pltpu.make_async_copy(ids_any, ids_ref, sems.at[0])
    rows_copy = pltpu.make_async_copy(rows_any, rows_ref, sems.at[1])
    ids_copy.start()
    rows_copy.start()
    out_ref[...] = jnp.zeros_like(out_ref)
    r = lax.broadcasted_iota(jnp.int32, (128, 256), 0)
    c = lax.broadcasted_iota(jnp.int32, (128, 256), 1)
    weights = ((r < c) | (c >= 128)).astype(jnp.float32).astype(jnp.bfloat16)
    group = lax.broadcasted_iota(jnp.int32, (GROUPS, 128), 0)
    ids_copy.wait()
    for i in range(LINES):
        hit = group == ids_ref[pl.ds(i, 1), :]
        member_ref[pl.ds(i * GROUPS, GROUPS), :] = hit.astype(jnp.float32).astype(jnp.bfloat16)
    counts = jnp.dot(member_ref[...], weights, preferred_element_type=jnp.float32)
    carry = jnp.zeros((GROUPS, 128), jnp.float32)
    for i in range(LINES):
        part = counts[i * GROUPS : (i + 1) * GROUPS]
        line = ids_ref[pl.ds(i, 1), :]
        within = jnp.sum(jnp.where(group == line, part[:, :128] + carry, 0.0), axis=0, keepdims=True)
        within = within.astype(jnp.int32)
        slot_ref[pl.ds(i, 1), :] = line * CAP + within
        spot_ref[pl.ds(i, 1), :] = jnp.where(
            within < PARTS[0],
            line * PARTS[0] + within,
            GROUPS * PARTS[0] + line * PARTS[1] + within - PARTS[0],
        )
        carry = carry + part[:, 128:]
    copy = pltpu.make_async_copy(spot_ref, spot_sm, sems.at[2])
    copy.start()
    rows_copy.wait()
    wide_ref[...] = rows_ref[...].astype(jnp.float32)
    copy.wait()

    @pl.loop(0, LINES)
    def _(i):
        for lane in range(128):
            spot = spot_sm[i, lane]
            out_ref[pl.ds(spot, 1), :] = wide_ref[pl.ds(i * 128 + lane, 1), :]

    split = GROUPS * PARTS[0]
    first_ref[...] = out_ref[pl.ds(0, split), :].astype(jnp.bfloat16)
    second_ref[...] = out_ref[pl.ds(split, GROUPS * PARTS[1]), :].astype(jnp.bfloat16)


def place(ids, rows):
    return pl.pallas_call(
        place_kernel,
        out_shape=(
            jax.ShapeDtypeStruct((GROUPS * PARTS[0], WIDTH), jnp.bfloat16),
            jax.ShapeDtypeStruct((GROUPS * PARTS[1], WIDTH), jnp.bfloat16),
            jax.ShapeDtypeStruct((LINES, 128), jnp.int32),
        ),
        in_specs=[pl.BlockSpec(memory_space=pltpu.HBM)] * 2,
        out_specs=(VMEM, VMEM, VMEM),
        scratch_shapes=[
            pltpu.VMEM((LINES, 128), jnp.int32),
            pltpu.VMEM((ROWS, WIDTH), jnp.bfloat16),
            pltpu.VMEM((LINES * GROUPS, 128), jnp.bfloat16),
            pltpu.VMEM((ROWS, WIDTH), jnp.float32),
            pltpu.VMEM((GROUPS * CAP, WIDTH), jnp.float32),
            pltpu.VMEM((LINES, 128), jnp.int32),
            pltpu.SMEM((LINES, 128), jnp.int32),
            pltpu.SemaphoreType.DMA((3,)),
        ],
        compiler_params=PARAMS,
        name="place",
    )(ids, rows)


def ranks_kernel(ids_ref, slot_ref, orders_ref, table_ref):
    group = lax.broadcasted_iota(jnp.int32, (GROUPS, 128), 0)
    spot = lax.broadcasted_iota(jnp.int32, (CAP, 128), 0)
    total = jnp.zeros((3 * GROUPS, CAP), jnp.float32)
    for i in range(LINES):
        ids = ids_ref[pl.ds(i, 1), :]
        within = slot_ref[pl.ds(i, 1), :] - ids * CAP
        value = orders_ref[pl.ds(i, 1), :] + 1
        hit = group == ids
        digits = [
            jnp.where(hit, digit.astype(jnp.float32), 0.0)
            for digit in (value & 255, (value >> 8) & 255, value >> 16)
        ]
        left = jnp.concatenate(digits, axis=0).astype(jnp.bfloat16)
        right = (spot == within).astype(jnp.float32).astype(jnp.bfloat16)
        total = total + dot_rows(left, right)
    value = total[:GROUPS] + 256.0 * total[GROUPS : 2 * GROUPS] + 65536.0 * total[2 * GROUPS :]
    table_ref[...] = value


def ranks(ids, slots, orders):
    return pl.pallas_call(
        ranks_kernel,
        out_shape=jax.ShapeDtypeStruct((GROUPS, CAP), jnp.float32),
        in_specs=[VMEM] * 3,
        out_specs=VMEM,
        compiler_params=PARAMS,
        name="ranks",
    )(ids, slots, orders)


def dot_rows(p, q):
    return lax.dot_general(p, q, (((1,), (1,)), ((), ())), preferred_element_type=jnp.float32)


def eye():
    r = lax.broadcasted_iota(jnp.int32, (128, 128), 0)
    return r == lax.broadcasted_iota(jnp.int32, (128, 128), 1)


def to_row(col):
    pieces = []
    for i in range(col.shape[0] // 128):
        piece = jnp.broadcast_to(col[i * 128 : (i + 1) * 128], (128, 128))
        pieces.append(jnp.max(jnp.where(eye(), piece, low), axis=0, keepdims=True))
    return jnp.concatenate(pieces, axis=1)


def to_col(row):
    pieces = []
    for i in range(row.shape[1] // 128):
        piece = jnp.broadcast_to(row[:, i * 128 : (i + 1) * 128], (128, 128))
        pieces.append(jnp.max(jnp.where(eye(), piece, low), axis=1, keepdims=True))
    return jnp.concatenate(pieces, axis=0)


def gather_kernel(size, in_ref, rank_ref, out_ref, meta_ref):
    part = size // Y
    cols = []
    for y in range(Y):
        total = jnp.zeros((part, WIDTH), jnp.float32)
        for z in range(Z):
            piece = in_ref[pl.ds((y * Z + z) * part, part), :]
            out_ref[pl.ds(y * part, part), pl.ds(z * WIDTH, WIDTH)] = piece
            wide = piece.astype(jnp.float32)
            total = total + wide * wide
        cols.append(lax.rsqrt(jnp.sum(total, axis=1, keepdims=True) + 1e-06))
    inverse = to_row(jnp.concatenate(cols, axis=0))
    high = inverse.astype(jnp.bfloat16).astype(jnp.float32)
    middle = (inverse - high).astype(jnp.bfloat16).astype(jnp.float32)
    rank = rank_ref[...].astype(jnp.int32)
    lines = (high, middle, inverse - high - middle, rank & 255, (rank >> 8) & 255, rank >> 16)
    meta_ref[...] = jnp.zeros_like(meta_ref)
    for i, line in enumerate(lines):
        meta_ref[pl.ds(i, 1), pl.ds(0, size)] = line.astype(jnp.float32)
    out_ref[pl.ds(size, META), :] = meta_ref[...].astype(jnp.bfloat16)


def gather(size, arrived, rank):
    return pl.pallas_call(
        functools.partial(gather_kernel, size),
        out_shape=jax.ShapeDtypeStruct((size + META, Z * WIDTH), jnp.bfloat16),
        in_specs=[VMEM] * 2,
        out_specs=VMEM,
        scratch_shapes=[pltpu.VMEM((META, Z * WIDTH), jnp.float32)],
        compiler_params=PARAMS,
        name="gather",
    )(arrived, rank)


def size_of(ref):
    return ref.shape[0] - META


def row_meta(ref):
    size = size_of(ref)
    meta = ref[pl.ds(size, META), pl.ds(0, size)].astype(jnp.float32)
    rank = meta[3:4] + 256.0 * meta[4:5] + 65536.0 * meta[5:6]
    return meta[0:1] + meta[1:2] + meta[2:3], jnp.where(rank > 0, rank, never_order)


def meet(best, p_name, p_ref, others):
    size = size_of(p_ref)
    inv_p, rank_p = (to_col(row) for row in row_meta(p_ref))
    p_best = jnp.full((size, 128), low, jnp.float32)
    for q_name, q_ref in others:
        inv_q, rank_q = row_meta(q_ref)
        q_best = []
        for j in range(0, size_of(q_ref), 256):
            s = dot_rows(p_ref[pl.ds(0, size), :], q_ref[pl.ds(j, 256), :])
            s = s * inv_p * inv_q[:, j : j + 256]
            earlier = rank_q[:, j : j + 256] < rank_p
            mine = jnp.where(earlier, s, low)
            p_best = jnp.maximum(p_best, jnp.maximum(mine[:, :128], mine[:, 128:]))
            if q_name != p_name:
                q_best.append(jnp.max(jnp.where(earlier, low, s), axis=0, keepdims=True))
        if q_best:
            record(best, q_name, jnp.concatenate(q_best, axis=1))
    record(best, p_name, to_row(jnp.max(p_best, axis=1, keepdims=True)))


def record(best, name, row):
    at = (pl.ds(name, 1), pl.ds(0, row.shape[1]))
    best[at] = jnp.maximum(best[at], row)


O1, O2, U1, U2, V1, V2, E1, E2, W1, W2 = range(10)


def own_kernel(spots, o1, e1, best):
    best[...] = jnp.full_like(best, -1.0)
    meet(best, O1, o1, [(O1, o1)])

    @pl.when(spots[0] == 0)
    def _():
        meet(best, O1, o1, [(E1, e1)])


def first_kernel(spots, o1, u1, v1, e1, w1, before, best):
    best[...] = before[...]
    meet(best, O1, o1, [(U1, u1)])

    @pl.when(spots[0] == 0)
    def _():
        meet(best, E1, e1, [(V1, v1)])

    @pl.when(spots[0] != 0)
    def _():
        meet(best, E1, e1, [(U1, u1)])

    @pl.when(spots[1] != 0)
    def _():
        meet(best, U1, u1, [(V1, v1)])

    @pl.when(spots[1] == 0)
    def _():
        meet(best, U1, u1, [(W1, w1)])


def second_kernel(spots, o1, o2, u1, v1, e1, e2, before, best):
    best[...] = before[...]
    meet(best, O2, o2, [(O1, o1), (O2, o2), (U1, u1), (V1, v1)])
    meet(best, E2, e2, [(O1, o1), (U1, u1), (V1, v1)])

    @pl.when(spots[0] != 0)
    def _():
        meet(best, O2, o2, [(E2, e2)])


def third_kernel(spots, o2, u2, v2, e2, before, best):
    best[...] = before[...]
    meet(best, O2, o2, [(U2, u2)])

    @pl.when(spots[0] == 0)
    def _():
        meet(best, E2, e2, [(V2, v2)])

    @pl.when(spots[0] != 0)
    def _():
        meet(best, E2, e2, [(U2, u2)])


def fourth_kernel(spots, u1, u2, v1, v2, w1, w2, before, out, best, long, short):
    best[...] = before[...]

    @pl.when(spots[1] != 0)
    def _():
        meet(best, V2, v2, [(U1, u1)])
        meet(best, U2, u2, [(V1, v1), (V2, v2)])

    @pl.when(spots[1] == 0)
    def _():
        meet(best, W2, w2, [(U1, u1)])
        meet(best, U2, u2, [(W1, w1), (W2, w2)])

    long[...] = jnp.full_like(long, -1.0)
    short[...] = jnp.full_like(short, -1.0)
    for i in range(5):
        for y in range(Y):
            at = pl.ds(spots[2 + i] * Y + y, 1)
            long[at, :] = best[pl.ds(2 * i, 1), pl.ds(y * PARTS[0], PARTS[0])]
            pair = best[pl.ds(2 * i + 1, 1), pl.ds(y // 2 * 128, 128)]
            short[at, :] = pltpu.roll(pair, 64, 1) if y % 2 else pair
    out[:, pl.ds(0, PARTS[0])] = long[...]
    out[:, pl.ds(PARTS[0], PARTS[1])] = short[:, pl.ds(0, PARTS[1])]


def scores_call(kernel, units, inputs, out, scratch, name):
    return pl.pallas_call(
        kernel,
        out_shape=jax.ShapeDtypeStruct(out, jnp.float32),
        in_specs=[SMEM] + [VMEM] * (len(inputs) - 1),
        out_specs=VMEM,
        scratch_shapes=scratch,
        compiler_params=PARAMS,
        cost_estimate=pl.CostEstimate(
            flops=int(units * 2 * 256 * 256 * 1024), bytes_accessed=4 * 2**20, transcendentals=0
        ),
        name=name,
    )(*inputs)


def answer_kernel(ids_ref, slot_ref, table_ref, out_ref):
    table = table_ref[...]
    high = table.astype(jnp.bfloat16)
    rest = table - high.astype(jnp.float32)
    middle = rest.astype(jnp.bfloat16)
    small = (rest - middle.astype(jnp.float32)).astype(jnp.bfloat16)
    pieces = jnp.concatenate([high, middle, small], axis=0)
    group = lax.broadcasted_iota(jnp.int32, (3 * GROUPS, 128), 0) & (GROUPS - 1)
    place_in = lax.broadcasted_iota(jnp.int32, (CAP, 128), 0)
    for i in range(LINES):
        ids = ids_ref[pl.ds(i, 1), :]
        within = slot_ref[pl.ds(i, 1), :] - ids * CAP
        where = (ids & (Z - 1)) * Y + (ids >> 3)
        member = (group == where).astype(jnp.float32).astype(jnp.bfloat16)
        found = lax.dot_general(
            pieces, member, (((0,), (0,)), ((), ())), preferred_element_type=jnp.float32
        )
        out_ref[pl.ds(i, 1), :] = jnp.sum(
            jnp.where(place_in == within, found, 0.0), axis=0, keepdims=True
        )


def answer(ids, slots, table):
    return pl.pallas_call(
        answer_kernel,
        out_shape=jax.ShapeDtypeStruct((LINES, 128), jnp.float32),
        in_specs=[VMEM] * 3,
        out_specs=VMEM,
        compiler_params=PARAMS,
        name="answer",
    )(ids, slots, table)


def shards(embeds, cluster_ids, orders):
    y, x, core, z = (lax.axis_index(name) for name in ALL)
    ids = cluster_ids.reshape(LINES, 128)
    *placed, slots = place(ids, embeds)
    arrived = [
        lax.all_to_all(
            rows.reshape(GROUPS, part, WIDTH), ("y", "z"), split_axis=0, concat_axis=0, tiled=True
        ).reshape(GROUPS * part, WIDTH)
        for rows, part in zip(placed, PARTS)
    ]

    table = ranks(ids, slots, orders.reshape(LINES, 128)).reshape(Y, Z, CAP)
    table = lax.dynamic_index_in_dim(table, z, 1, keepdims=False)
    rank_parts = []
    for j in range(Y):
        row = lax.dynamic_slice_in_dim(table, (y + j) % Y, 1, 0)
        if j:
            row = lax.ppermute(row, ALL, routes(lambda y, x, c, z: (y + j, x, c, z)))
        rank_parts.append(row)
    member_ranks = jnp.concatenate(rank_parts)[(y - jnp.arange(Y)) % Y]
    rank1 = member_ranks[:, : PARTS[0]].reshape(1, SIZES[0])
    rank2 = member_ranks[:, PARTS[0] :].reshape(1, SIZES[1])

    step = 1 - 2 * core
    near, far = (x - step) % X, (x + step) % X
    spots = jnp.stack(
        [
            core,
            ((x < X // 2) == (core == 0)).astype(jnp.int32),
            x * C + core,
            near * C + core,
            far * C + core,
            x * C + 1 - core,
            far * C + 1 - core,
        ]
    ).astype(jnp.int32)

    swap = routes(lambda y, x, c, z: (y, x, 1 - c, z))
    ahead = routes(lambda y, x, c, z: (y, x + 1 - 2 * c, c, z))
    behind = routes(lambda y, x, c, z: (y, x - 1 + 2 * c, c, z))

    def share(own, after):
        u = lax.ppermute(own, ALL, ahead)
        v = lax.ppermute(own, ALL, behind)
        e = lax.ppermute(own, ALL, swap)
        u, *after = lax.optimization_barrier((u, *after(e)))
        return (u, v, e, lax.ppermute(u, ALL, swap), *after)

    wide = (16, SIZES[0])
    o1 = gather(SIZES[0], arrived[0], rank1)
    u1, v1, e1, w1, best, later = share(
        o1,
        lambda e: (scores_call(own_kernel, 8, (spots, o1, e), wide, [], "own"), arrived[1]),
    )
    o2 = gather(SIZES[1], later, rank2)
    u2, v2, e2, w2, best = share(
        o2,
        lambda e: (
            scores_call(first_kernel, 12, (spots, o1, u1, v1, e1, w1, best), wide, [], "first"),
        ),
    )
    best = scores_call(second_kernel, 14, (spots, o1, o2, u1, v1, e1, e2, best), wide, [], "second")
    best = scores_call(third_kernel, 2, (spots, o2, u2, v2, e2, best), wide, [], "third")
    best = scores_call(
        fourth_kernel, 5, (spots, u1, u2, v1, v2, w1, w2, best), (GROUPS, CAP),
        [pltpu.VMEM(size, jnp.float32) for size in (wide, (GROUPS, 128), (GROUPS, 128))],
        "fourth",
    )
    back = lax.all_to_all(best, ("x", "core", "y"), split_axis=0, concat_axis=0, tiled=True)
    merged = jnp.max(back.reshape(X * C, Y, CAP), axis=0)
    table = lax.all_to_all(
        jnp.broadcast_to(merged[None], (Z, Y, CAP)), "z", split_axis=0, concat_axis=0, tiled=True
    )
    return answer(ids, slots, table.reshape(GROUPS, CAP)).reshape(ROWS)


def solution(mesh):
    fine = Mesh(mesh.devices.reshape(Y, X, C, Z), ALL)
    clus = ("y", "x", "core")
    return jax.shard_map(
        shards,
        mesh=fine,
        in_specs=(P(clus, "z"), P(clus), P(clus)),
        out_specs=P(clus),
        check_vma=False,
    )
```

```python
import functools

import jax
import jax.numpy as jnp
from jax import lax
from jax.experimental import pallas as pl
from jax.experimental.pallas import tpu as pltpu
from jax.sharding import Mesh, PartitionSpec as P

never_order = 2.0**30
low = -3e38
Y, X, C, Z = 4, 4, 2, 8
ROWS = 3072
GROUPS = 32
CAP = 192
WIDTH = 128
PARTS = (128, 64)
SIZES = (Y * 128, Y * 64)
META = 16
LINES = ROWS // 128
ALL = ("y", "x", "core", "z")
PARAMS = pltpu.CompilerParams(vmem_limit_bytes=40 * 2**20)
VMEM = pl.BlockSpec(memory_space=pltpu.VMEM)
SMEM = pl.BlockSpec(memory_space=pltpu.SMEM)


def routes(move):
    pairs = []
    for y in range(Y):
        for x in range(X):
            for c in range(C):
                for z in range(Z):
                    y2, x2, c2, z2 = move(y, x, c, z)
                    to = (((y2 % Y) * X + x2 % X) * C + c2 % C) * Z + z2 % Z
                    pairs.append((((y * X + x) * C + c) * Z + z, to))
    return pairs


def place_kernel(
    ids_any, rows_any, first_ref, second_ref, slot_ref,
    ids_ref, rows_ref, member_ref, wide_ref, out_ref, spot_ref, spot_sm, sems,
):
    ids_copy = pltpu.make_async_copy(ids_any, ids_ref, sems.at[0])
    rows_copy = pltpu.make_async_copy(rows_any, rows_ref, sems.at[1])
    ids_copy.start()
    rows_copy.start()
    out_ref[...] = jnp.zeros_like(out_ref)
    r = lax.broadcasted_iota(jnp.int32, (128, 256), 0)
    c = lax.broadcasted_iota(jnp.int32, (128, 256), 1)
    weights = ((r < c) | (c >= 128)).astype(jnp.float32).astype(jnp.bfloat16)
    group = lax.broadcasted_iota(jnp.int32, (GROUPS, 128), 0)
    ids_copy.wait()
    for i in range(LINES):
        hit = group == ids_ref[pl.ds(i, 1), :]
        member_ref[pl.ds(i * GROUPS, GROUPS), :] = hit.astype(jnp.float32).astype(jnp.bfloat16)
    counts = jnp.dot(member_ref[...], weights, preferred_element_type=jnp.float32)
    carry = jnp.zeros((GROUPS, 128), jnp.float32)
    for i in range(LINES):
        part = counts[i * GROUPS : (i + 1) * GROUPS]
        line = ids_ref[pl.ds(i, 1), :]
        within = jnp.sum(jnp.where(group == line, part[:, :128] + carry, 0.0), axis=0, keepdims=True)
        within = within.astype(jnp.int32)
        slot_ref[pl.ds(i, 1), :] = line * CAP + within
        spot_ref[pl.ds(i, 1), :] = jnp.where(
            within < PARTS[0],
            line * PARTS[0] + within,
            GROUPS * PARTS[0] + line * PARTS[1] + within - PARTS[0],
        )
        carry = carry + part[:, 128:]
    copy = pltpu.make_async_copy(spot_ref, spot_sm, sems.at[2])
    copy.start()
    rows_copy.wait()
    wide_ref[...] = rows_ref[...].astype(jnp.float32)
    copy.wait()

    @pl.loop(0, LINES)
    def _(i):
        for lane in range(128):
            spot = spot_sm[i, lane]
            out_ref[pl.ds(spot, 1), :] = wide_ref[pl.ds(i * 128 + lane, 1), :]

    split = GROUPS * PARTS[0]
    first_ref[...] = out_ref[pl.ds(0, split), :].astype(jnp.bfloat16)
    second_ref[...] = out_ref[pl.ds(split, GROUPS * PARTS[1]), :].astype(jnp.bfloat16)


def place(ids, rows):
    return pl.pallas_call(
        place_kernel,
        out_shape=(
            jax.ShapeDtypeStruct((GROUPS * PARTS[0], WIDTH), jnp.bfloat16),
            jax.ShapeDtypeStruct((GROUPS * PARTS[1], WIDTH), jnp.bfloat16),
            jax.ShapeDtypeStruct((LINES, 128), jnp.int32),
        ),
        in_specs=[pl.BlockSpec(memory_space=pltpu.HBM)] * 2,
        out_specs=(VMEM, VMEM, VMEM),
        scratch_shapes=[
            pltpu.VMEM((LINES, 128), jnp.int32),
            pltpu.VMEM((ROWS, WIDTH), jnp.bfloat16),
            pltpu.VMEM((LINES * GROUPS, 128), jnp.bfloat16),
            pltpu.VMEM((ROWS, WIDTH), jnp.float32),
            pltpu.VMEM((GROUPS * CAP, WIDTH), jnp.float32),
            pltpu.VMEM((LINES, 128), jnp.int32),
            pltpu.SMEM((LINES, 128), jnp.int32),
            pltpu.SemaphoreType.DMA((3,)),
        ],
        compiler_params=pltpu.CompilerParams(vmem_limit_bytes=60 * 2**20),
        name="place",
    )(ids, rows)


def ranks_kernel(ids_ref, slot_ref, orders_ref, table_ref):
    group = lax.broadcasted_iota(jnp.int32, (GROUPS, 128), 0)
    spot = lax.broadcasted_iota(jnp.int32, (CAP, 128), 0)
    total = jnp.zeros((3 * GROUPS, CAP), jnp.float32)
    for i in range(LINES):
        ids = ids_ref[pl.ds(i, 1), :]
        within = slot_ref[pl.ds(i, 1), :] - ids * CAP
        value = orders_ref[pl.ds(i, 1), :] + 1
        hit = group == ids
        digits = [
            jnp.where(hit, digit.astype(jnp.float32), 0.0)
            for digit in (value & 255, (value >> 8) & 255, value >> 16)
        ]
        left = jnp.concatenate(digits, axis=0).astype(jnp.bfloat16)
        right = (spot == within).astype(jnp.float32).astype(jnp.bfloat16)
        total = total + dot_rows(left, right)
    value = total[:GROUPS] + 256.0 * total[GROUPS : 2 * GROUPS] + 65536.0 * total[2 * GROUPS :]
    table_ref[...] = value


def ranks(ids, slots, orders):
    return pl.pallas_call(
        ranks_kernel,
        out_shape=jax.ShapeDtypeStruct((GROUPS, CAP), jnp.float32),
        in_specs=[VMEM] * 3,
        out_specs=VMEM,
        compiler_params=PARAMS,
        name="ranks",
    )(ids, slots, orders)


def dot_rows(p, q):
    return lax.dot_general(p, q, (((1,), (1,)), ((), ())), preferred_element_type=jnp.float32)


def eye():
    r = lax.broadcasted_iota(jnp.int32, (128, 128), 0)
    return r == lax.broadcasted_iota(jnp.int32, (128, 128), 1)


def to_row(col):
    pieces = []
    for i in range(col.shape[0] // 128):
        piece = jnp.broadcast_to(col[i * 128 : (i + 1) * 128], (128, 128))
        pieces.append(jnp.max(jnp.where(eye(), piece, low), axis=0, keepdims=True))
    return jnp.concatenate(pieces, axis=1)


def to_col(row):
    pieces = []
    for i in range(row.shape[1] // 128):
        piece = jnp.broadcast_to(row[:, i * 128 : (i + 1) * 128], (128, 128))
        pieces.append(jnp.max(jnp.where(eye(), piece, low), axis=1, keepdims=True))
    return jnp.concatenate(pieces, axis=0)


def gather_kernel(size, in_ref, rank_ref, out_ref, meta_ref):
    part = size // Y
    cols = []
    for y in range(Y):
        total = jnp.zeros((part, WIDTH), jnp.float32)
        for z in range(Z):
            piece = in_ref[pl.ds((y * Z + z) * part, part), :]
            out_ref[pl.ds(y * part, part), pl.ds(z * WIDTH, WIDTH)] = piece
            wide = piece.astype(jnp.float32)
            total = total + wide * wide
        cols.append(lax.rsqrt(jnp.sum(total, axis=1, keepdims=True) + 1e-06))
    inverse = to_row(jnp.concatenate(cols, axis=0))
    high = inverse.astype(jnp.bfloat16).astype(jnp.float32)
    middle = (inverse - high).astype(jnp.bfloat16).astype(jnp.float32)
    rank = rank_ref[...].astype(jnp.int32)
    lines = (high, middle, inverse - high - middle, rank & 255, (rank >> 8) & 255, rank >> 16)
    meta_ref[...] = jnp.zeros_like(meta_ref)
    for i, line in enumerate(lines):
        meta_ref[pl.ds(i, 1), pl.ds(0, size)] = line.astype(jnp.float32)
    out_ref[pl.ds(size, META), :] = meta_ref[...].astype(jnp.bfloat16)


def gather(size, arrived, rank):
    return pl.pallas_call(
        functools.partial(gather_kernel, size),
        out_shape=jax.ShapeDtypeStruct((size + META, Z * WIDTH), jnp.bfloat16),
        in_specs=[VMEM] * 2,
        out_specs=VMEM,
        scratch_shapes=[pltpu.VMEM((META, Z * WIDTH), jnp.float32)],
        compiler_params=PARAMS,
        name="gather",
    )(arrived, rank)


def size_of(ref):
    return ref.shape[0] - META


def row_meta(ref):
    size = size_of(ref)
    meta = ref[pl.ds(size, META), pl.ds(0, size)].astype(jnp.float32)
    rank = meta[3:4] + 256.0 * meta[4:5] + 65536.0 * meta[5:6]
    return meta[0:1] + meta[1:2] + meta[2:3], jnp.where(rank > 0, rank, never_order)


def meet(best, p_name, p_ref, others):
    size = size_of(p_ref)
    inv_p, rank_p = (to_col(row) for row in row_meta(p_ref))
    p_best = jnp.full((size, 128), low, jnp.float32)
    for q_name, q_ref in others:
        inv_q, rank_q = row_meta(q_ref)
        q_best = []
        for j in range(0, size_of(q_ref), 256):
            s = dot_rows(p_ref[pl.ds(0, size), :], q_ref[pl.ds(j, 256), :])
            s = s * inv_p * inv_q[:, j : j + 256]
            earlier = rank_q[:, j : j + 256] < rank_p
            mine = jnp.where(earlier, s, low)
            p_best = jnp.maximum(p_best, jnp.maximum(mine[:, :128], mine[:, 128:]))
            if q_name != p_name:
                q_best.append(jnp.max(jnp.where(earlier, low, s), axis=0, keepdims=True))
        if q_best:
            record(best, q_name, jnp.concatenate(q_best, axis=1))
    record(best, p_name, to_row(jnp.max(p_best, axis=1, keepdims=True)))


def record(best, name, row):
    at = (pl.ds(name, 1), pl.ds(0, row.shape[1]))
    best[at] = jnp.maximum(best[at], row)


O1, O2, U1, U2, V1, V2, E1, E2, W1, W2 = range(10)


def own_kernel(spots, o1, e1, best):
    best[...] = jnp.full_like(best, -1.0)
    meet(best, O1, o1, [(O1, o1)])

    @pl.when(spots[0] == 0)
    def _():
        meet(best, O1, o1, [(E1, e1)])


def first_kernel(spots, o1, u1, v1, e1, w1, before, best):
    best[...] = before[...]
    meet(best, O1, o1, [(U1, u1)])

    @pl.when(spots[0] == 0)
    def _():
        meet(best, E1, e1, [(V1, v1)])

    @pl.when(spots[0] != 0)
    def _():
        meet(best, E1, e1, [(U1, u1)])

    @pl.when(spots[1] != 0)
    def _():
        meet(best, U1, u1, [(V1, v1)])

    @pl.when(spots[1] == 0)
    def _():
        meet(best, U1, u1, [(W1, w1)])


def second_kernel(spots, o1, o2, u1, v1, e1, e2, before, best):
    best[...] = before[...]
    meet(best, O2, o2, [(O1, o1), (O2, o2), (U1, u1), (V1, v1)])
    meet(best, E2, e2, [(O1, o1), (U1, u1), (V1, v1)])

    @pl.when(spots[0] != 0)
    def _():
        meet(best, O2, o2, [(E2, e2)])


def third_kernel(spots, o2, u2, v2, e2, before, best):
    best[...] = before[...]
    meet(best, O2, o2, [(U2, u2)])

    @pl.when(spots[0] == 0)
    def _():
        meet(best, E2, e2, [(V2, v2)])

    @pl.when(spots[0] != 0)
    def _():
        meet(best, E2, e2, [(U2, u2)])


def fourth_kernel(spots, u1, u2, v1, v2, w1, w2, before, *refs):
    *outs, best = refs
    best[...] = before[...]

    @pl.when(spots[1] != 0)
    def _():
        meet(best, V2, v2, [(U1, u1)])
        meet(best, U2, u2, [(V1, v1), (V2, v2)])

    @pl.when(spots[1] == 0)
    def _():
        meet(best, W2, w2, [(U1, u1)])
        meet(best, U2, u2, [(W1, w1), (W2, w2)])

    for i, out in enumerate(outs):
        for y in range(Y):
            at = pl.ds(y, 1)
            out[at, pl.ds(0, PARTS[0])] = best[pl.ds(2 * i, 1), pl.ds(y * PARTS[0], PARTS[0])]
            pair = best[pl.ds(2 * i + 1, 1), pl.ds(y // 2 * 128, 128)]
            pair = pltpu.roll(pair, 64, 1) if y % 2 else pair
            out[at, pl.ds(PARTS[0], PARTS[1])] = pair[:, : PARTS[1]]


def is_dims(item):
    return isinstance(item, tuple) and isinstance(item[0], int)


def scores_call(kernel, units, inputs, out, scratch, name):
    return pl.pallas_call(
        kernel,
        out_shape=jax.tree.map(lambda dims: jax.ShapeDtypeStruct(dims, jnp.float32), out, is_leaf=is_dims),
        in_specs=[SMEM] + [VMEM] * (len(inputs) - 1),
        out_specs=jax.tree.map(lambda _: VMEM, out, is_leaf=is_dims),
        scratch_shapes=scratch,
        compiler_params=PARAMS,
        cost_estimate=pl.CostEstimate(
            flops=int(units * 2 * 256 * 256 * 1024), bytes_accessed=4 * 2**20, transcendentals=0
        ),
        name=name,
    )(*inputs)


def answer_kernel(ids_ref, slot_ref, table_ref, out_ref):
    table = table_ref[...]
    high = table.astype(jnp.bfloat16)
    rest = table - high.astype(jnp.float32)
    middle = rest.astype(jnp.bfloat16)
    small = (rest - middle.astype(jnp.float32)).astype(jnp.bfloat16)
    pieces = jnp.concatenate([high, middle, small], axis=0)
    group = lax.broadcasted_iota(jnp.int32, (3 * GROUPS, 128), 0) & (GROUPS - 1)
    place_in = lax.broadcasted_iota(jnp.int32, (CAP, 128), 0)
    for i in range(LINES):
        ids = ids_ref[pl.ds(i, 1), :]
        within = slot_ref[pl.ds(i, 1), :] - ids * CAP
        member = (group == ids).astype(jnp.float32).astype(jnp.bfloat16)
        found = lax.dot_general(
            pieces, member, (((0,), (0,)), ((), ())), preferred_element_type=jnp.float32
        )
        out_ref[pl.ds(i, 1), :] = jnp.sum(
            jnp.where(place_in == within, found, 0.0), axis=0, keepdims=True
        )


def answer(ids, slots, table):
    return pl.pallas_call(
        answer_kernel,
        out_shape=jax.ShapeDtypeStruct((LINES, 128), jnp.float32),
        in_specs=[VMEM] * 3,
        out_specs=VMEM,
        compiler_params=PARAMS,
        name="answer",
    )(ids, slots, table)


def shards(embeds, cluster_ids, orders):
    y, x, core, z = (lax.axis_index(name) for name in ALL)
    ids = cluster_ids.reshape(LINES, 128)
    *placed, slots = place(ids, embeds)
    arrived = [
        lax.all_to_all(
            rows.reshape(GROUPS, part, WIDTH), ("y", "z"), split_axis=0, concat_axis=0, tiled=True
        ).reshape(GROUPS * part, WIDTH)
        for rows, part in zip(placed, PARTS)
    ]

    table = ranks(ids, slots, orders.reshape(LINES, 128)).reshape(Y, Z, CAP)
    table = lax.dynamic_index_in_dim(table, z, 1, keepdims=False)
    rank_parts = []
    for j in range(Y):
        row = lax.dynamic_slice_in_dim(table, (y + j) % Y, 1, 0)
        if j:
            row = lax.ppermute(row, ALL, routes(lambda y, x, c, z: (y + j, x, c, z)))
        rank_parts.append(row)
    member_ranks = jnp.concatenate(rank_parts)[(y - jnp.arange(Y)) % Y]
    rank1 = member_ranks[:, : PARTS[0]].reshape(1, SIZES[0])
    rank2 = member_ranks[:, PARTS[0] :].reshape(1, SIZES[1])

    spots = jnp.stack([core, ((x < X // 2) == (core == 0)).astype(jnp.int32)]).astype(jnp.int32)

    swap = routes(lambda y, x, c, z: (y, x, 1 - c, z))
    ahead = routes(lambda y, x, c, z: (y, x + 1 - 2 * c, c, z))
    behind = routes(lambda y, x, c, z: (y, x - 1 + 2 * c, c, z))

    def share(own, after):
        u = lax.ppermute(own, ALL, ahead)
        v = lax.ppermute(own, ALL, behind)
        e = lax.ppermute(own, ALL, swap)
        u, *after = lax.optimization_barrier((u, *after(e)))
        return (u, v, e, lax.ppermute(u, ALL, swap), *after)

    wide = (16, SIZES[0])
    o1 = gather(SIZES[0], arrived[0], rank1)
    u1, v1, e1, w1, best, later = share(
        o1,
        lambda e: (scores_call(own_kernel, 8, (spots, o1, e), wide, [], "own"), arrived[1]),
    )
    o2 = gather(SIZES[1], later, rank2)

    def before_arrival(e2):
        first = scores_call(
            first_kernel, 12, (spots, o1, u1, v1, e1, w1, best), wide, [], "first"
        )
        inputs = (spots, o1, o2, u1, v1, e1, e2, first)
        return (scores_call(second_kernel, 14, inputs, wide, [], "second"),)

    u2, v2, e2, w2, best = share(o2, before_arrival)
    best = scores_call(third_kernel, 2, (spots, o2, u2, v2, e2, best), wide, [], "third")
    own, *others = scores_call(
        fourth_kernel, 5, (spots, u1, u2, v1, v2, w1, w2, best), [(Y, CAP)] * 5,
        [pltpu.VMEM(wide, jnp.float32)], "fourth",
    )
    across = routes(lambda y, x, c, z: (y, x + 1 - 2 * c, 1 - c, z))
    for part, way in zip(others, (behind, ahead, swap, across)):
        own = jnp.maximum(own, lax.ppermute(part, ALL, way))
    table = lax.all_to_all(
        jnp.broadcast_to(own[:, None], (Y, Z, CAP)).reshape(GROUPS, CAP),
        ("y", "z"), split_axis=0, concat_axis=0, tiled=True,
    )
    return answer(ids, slots, table).reshape(ROWS)


def solution(mesh):
    fine = Mesh(mesh.devices.reshape(Y, X, C, Z), ALL)
    clus = ("y", "x", "core")
    return jax.shard_map(
        shards,
        mesh=fine,
        in_specs=(P(clus, "z"), P(clus), P(clus)),
        out_specs=P(clus),
        check_vma=False,
    )
```

```python
import functools

import jax
import jax.numpy as jnp
from jax import lax
from jax.experimental import pallas as pl
from jax.experimental.pallas import tpu as pltpu
from jax.sharding import Mesh, PartitionSpec as P

never_order = 2.0**30
low = -3e38
Y, X, C, Z = 4, 4, 2, 8
ROWS = 3072
GROUPS = 32
CAP = 192
WIDTH = 128
PARTS = (128, 64)
SIZES = (Y * 128, Y * 64)
LINES = ROWS // 128
ALL = ("y", "x", "core", "z")
PARAMS = pltpu.CompilerParams(vmem_limit_bytes=40 * 2**20)
VMEM = pl.BlockSpec(memory_space=pltpu.VMEM)
SMEM = pl.BlockSpec(memory_space=pltpu.SMEM)


def routes(move):
    pairs = []
    for y in range(Y):
        for x in range(X):
            for c in range(C):
                for z in range(Z):
                    y2, x2, c2, z2 = move(y, x, c, z)
                    to = (((y2 % Y) * X + x2 % X) * C + c2 % C) * Z + z2 % Z
                    pairs.append((((y * X + x) * C + c) * Z + z, to))
    return pairs


def scatter_rows(spot_sm, wide_ref, out_ref):
    @pl.loop(0, LINES)
    def _(i):
        for lane in range(128):
            spot = spot_sm[i, lane]
            out_ref[pl.ds(spot, 1), :] = wide_ref[pl.ds(i * 128 + lane, 1), :]


def place_kernel(
    ids_any, rows_any, placed_ref, slot_ref,
    ids_ref, rows_ref, member_ref, wide_ref, out_ref, spot_ref, spot_sm, sems,
):
    ids_copy = pltpu.make_async_copy(ids_any, ids_ref, sems.at[0])
    rows_copy = pltpu.make_async_copy(rows_any, rows_ref, sems.at[1])
    ids_copy.start()
    rows_copy.start()
    out_ref[...] = jnp.zeros_like(out_ref)
    r = lax.broadcasted_iota(jnp.int32, (128, 256), 0)
    c = lax.broadcasted_iota(jnp.int32, (128, 256), 1)
    weights = ((r < c) | (c >= 128)).astype(jnp.float32).astype(jnp.bfloat16)
    group = lax.broadcasted_iota(jnp.int32, (GROUPS, 128), 0)
    ids_copy.wait()
    for i in range(LINES):
        hit = group == ids_ref[pl.ds(i, 1), :]
        member_ref[pl.ds(i * GROUPS, GROUPS), :] = hit.astype(jnp.float32).astype(jnp.bfloat16)
    counts = jnp.dot(member_ref[...], weights, preferred_element_type=jnp.float32)
    carry = jnp.zeros((GROUPS, 128), jnp.float32)
    for i in range(LINES):
        part = counts[i * GROUPS : (i + 1) * GROUPS]
        line = ids_ref[pl.ds(i, 1), :]
        within = jnp.sum(jnp.where(group == line, part[:, :128] + carry, 0.0), axis=0, keepdims=True)
        within = within.astype(jnp.int32)
        slot_ref[pl.ds(i, 1), :] = line * CAP + within
        spot_ref[pl.ds(i, 1), :] = jnp.where(
            within < PARTS[0], line * PARTS[0] + within, GROUPS * PARTS[0]
        )
        carry = carry + part[:, 128:]
    copy = pltpu.make_async_copy(spot_ref, spot_sm, sems.at[2])
    copy.start()
    rows_copy.wait()
    wide_ref[...] = rows_ref[...].astype(jnp.float32)
    copy.wait()
    scatter_rows(spot_sm, wide_ref, out_ref)
    placed_ref[...] = out_ref[pl.ds(0, GROUPS * PARTS[0]), :].astype(jnp.bfloat16)


def place(ids, rows):
    return pl.pallas_call(
        place_kernel,
        out_shape=(
            jax.ShapeDtypeStruct((GROUPS * PARTS[0], WIDTH), jnp.bfloat16),
            jax.ShapeDtypeStruct((LINES, 128), jnp.int32),
        ),
        in_specs=[pl.BlockSpec(memory_space=pltpu.HBM)] * 2,
        out_specs=(VMEM, VMEM),
        scratch_shapes=[
            pltpu.VMEM((LINES, 128), jnp.int32),
            pltpu.VMEM((ROWS, WIDTH), jnp.bfloat16),
            pltpu.VMEM((LINES * GROUPS, 128), jnp.bfloat16),
            pltpu.VMEM((ROWS, WIDTH), jnp.float32),
            pltpu.VMEM((GROUPS * PARTS[0] + 8, WIDTH), jnp.float32),
            pltpu.VMEM((LINES, 128), jnp.int32),
            pltpu.SMEM((LINES, 128), jnp.int32),
            pltpu.SemaphoreType.DMA((3,)),
        ],
        compiler_params=pltpu.CompilerParams(vmem_limit_bytes=60 * 2**20),
        name="place",
    )(ids, rows)


def place_rest_kernel(
    ids_ref, slot_ref, rows_ref, placed_ref, wide_ref, out_ref, spot_ref, spot_sm, sem
):
    ids = ids_ref[...]
    within = slot_ref[...] - ids * CAP
    spot_ref[...] = jnp.where(
        within < PARTS[0], GROUPS * PARTS[1], ids * PARTS[1] + within - PARTS[0]
    )
    copy = pltpu.make_async_copy(spot_ref, spot_sm, sem)
    copy.start()
    out_ref[...] = jnp.zeros_like(out_ref)
    wide_ref[...] = rows_ref[...].astype(jnp.float32)
    copy.wait()
    scatter_rows(spot_sm, wide_ref, out_ref)
    placed_ref[...] = out_ref[pl.ds(0, GROUPS * PARTS[1]), :].astype(jnp.bfloat16)


def place_rest(ids, slots, rows):
    return pl.pallas_call(
        place_rest_kernel,
        out_shape=jax.ShapeDtypeStruct((GROUPS * PARTS[1], WIDTH), jnp.bfloat16),
        in_specs=[VMEM] * 3,
        out_specs=VMEM,
        scratch_shapes=[
            pltpu.VMEM((ROWS, WIDTH), jnp.float32),
            pltpu.VMEM((GROUPS * PARTS[1] + 8, WIDTH), jnp.float32),
            pltpu.VMEM((LINES, 128), jnp.int32),
            pltpu.SMEM((LINES, 128), jnp.int32),
            pltpu.SemaphoreType.DMA,
        ],
        compiler_params=PARAMS,
        name="place_rest",
    )(ids, slots, rows)


def ranks_kernel(ids_ref, slot_ref, orders_ref, table_ref):
    group = lax.broadcasted_iota(jnp.int32, (GROUPS, 128), 0)
    spot = lax.broadcasted_iota(jnp.int32, (CAP, 128), 0)
    total = jnp.zeros((3 * GROUPS, CAP), jnp.float32)
    for i in range(LINES):
        ids = ids_ref[pl.ds(i, 1), :]
        within = slot_ref[pl.ds(i, 1), :] - ids * CAP
        value = orders_ref[pl.ds(i, 1), :] + 1
        hit = group == ids
        digits = [
            jnp.where(hit, digit.astype(jnp.float32), 0.0)
            for digit in (value & 255, (value >> 8) & 255, value >> 16)
        ]
        left = jnp.concatenate(digits, axis=0).astype(jnp.bfloat16)
        right = (spot == within).astype(jnp.float32).astype(jnp.bfloat16)
        total = total + dot_rows(left, right)
    value = total[:GROUPS] + 256.0 * total[GROUPS : 2 * GROUPS] + 65536.0 * total[2 * GROUPS :]
    table_ref[...] = value


def ranks(ids, slots, orders):
    return pl.pallas_call(
        ranks_kernel,
        out_shape=jax.ShapeDtypeStruct((GROUPS, CAP), jnp.float32),
        in_specs=[VMEM] * 3,
        out_specs=VMEM,
        compiler_params=PARAMS,
        name="ranks",
    )(ids, slots, orders)


def dot_rows(p, q):
    return lax.dot_general(p, q, (((1,), (1,)), ((), ())), preferred_element_type=jnp.float32)


def eye():
    r = lax.broadcasted_iota(jnp.int32, (128, 128), 0)
    return r == lax.broadcasted_iota(jnp.int32, (128, 128), 1)


def to_row(col):
    pieces = []
    for i in range(col.shape[0] // 128):
        piece = jnp.broadcast_to(col[i * 128 : (i + 1) * 128], (128, 128))
        pieces.append(jnp.max(jnp.where(eye(), piece, low), axis=0, keepdims=True))
    return jnp.concatenate(pieces, axis=1)


def to_col(row):
    pieces = []
    for i in range(row.shape[1] // 128):
        piece = jnp.broadcast_to(row[:, i * 128 : (i + 1) * 128], (128, 128))
        pieces.append(jnp.max(jnp.where(eye(), piece, low), axis=1, keepdims=True))
    return jnp.concatenate(pieces, axis=0)


def part_of(ref):
    return ref.shape[0] // GROUPS


def size_of(ref):
    return Y * part_of(ref)


def rows_of(ref, start, count):
    part = part_of(ref)
    lines = []
    for y in range(start // part, (start + count) // part):
        pieces = [ref[pl.ds((y * Z + z) * part, part), :] for z in range(Z)]
        lines.append(jnp.concatenate(pieces, axis=1))
    return jnp.concatenate(lines, axis=0)


def note(inverses, name, ref):
    part = part_of(ref)
    cols = []
    for y in range(Y):
        total = jnp.zeros((part, WIDTH), jnp.float32)
        for z in range(Z):
            wide = ref[pl.ds((y * Z + z) * part, part), :].astype(jnp.float32)
            total = total + wide * wide
        cols.append(lax.rsqrt(jnp.sum(total, axis=1, keepdims=True) + 1e-06))
    inverses[pl.ds(name, 1), pl.ds(0, Y * part)] = to_row(jnp.concatenate(cols, axis=0))


def meet(best, inverses, ranks, p_name, p_ref, others):
    size = size_of(p_ref)
    at = (pl.ds(p_name, 1), pl.ds(0, size))
    inv_p, rank_p = to_col(inverses[at]), to_col(ranks[at])
    p_best = jnp.full((size, 128), low, jnp.float32)
    for q_name, q_ref in others:
        q_best = []
        for j in range(0, size_of(q_ref), 256):
            at = (pl.ds(q_name, 1), pl.ds(j, 256))
            s = dot_rows(rows_of(p_ref, 0, size), rows_of(q_ref, j, 256))
            s = s * inv_p * inverses[at]
            earlier = ranks[at] < rank_p
            mine = jnp.where(earlier, s, low)
            p_best = jnp.maximum(p_best, jnp.maximum(mine[:, :128], mine[:, 128:]))
            if q_name != p_name:
                q_best.append(jnp.max(jnp.where(earlier, low, s), axis=0, keepdims=True))
        if q_best:
            record(best, q_name, jnp.concatenate(q_best, axis=1))
    record(best, p_name, to_row(jnp.max(p_best, axis=1, keepdims=True)))


def record(best, name, row):
    at = (pl.ds(name, 1), pl.ds(0, row.shape[1]))
    best[at] = jnp.maximum(best[at], row)


O1, O2, U1, U2, V1, V2, E1, E2, W1, W2 = range(10)


def own_kernel(spots, ranks, o1, e1, best, inverses):
    best[...] = jnp.full_like(best, -1.0)
    inverses[...] = jnp.zeros_like(inverses)
    note(inverses, O1, o1)
    note(inverses, E1, e1)
    meet(best, inverses, ranks, O1, o1, [(O1, o1)])

    @pl.when(spots[0] == 0)
    def _():
        meet(best, inverses, ranks, O1, o1, [(E1, e1)])


def first_kernel(spots, ranks, o1, u1, v1, e1, w1, before, known, best, inverses):
    best[...] = before[...]
    inverses[...] = known[...]
    note(inverses, U1, u1)
    note(inverses, V1, v1)
    note(inverses, W1, w1)
    meet(best, inverses, ranks, O1, o1, [(U1, u1)])

    @pl.when(spots[0] == 0)
    def _():
        meet(best, inverses, ranks, E1, e1, [(V1, v1)])

    @pl.when(spots[0] != 0)
    def _():
        meet(best, inverses, ranks, E1, e1, [(U1, u1)])

    @pl.when(spots[1] != 0)
    def _():
        meet(best, inverses, ranks, U1, u1, [(V1, v1)])

    @pl.when(spots[1] == 0)
    def _():
        meet(best, inverses, ranks, U1, u1, [(W1, w1)])


def second_kernel(spots, ranks, o1, o2, u1, v1, e1, e2, before, known, best, inverses):
    best[...] = before[...]
    inverses[...] = known[...]
    note(inverses, O2, o2)
    note(inverses, E2, e2)
    meet(best, inverses, ranks, O2, o2, [(O1, o1), (O2, o2), (U1, u1), (V1, v1)])
    meet(best, inverses, ranks, E2, e2, [(O1, o1), (U1, u1), (V1, v1)])

    @pl.when(spots[0] != 0)
    def _():
        meet(best, inverses, ranks, O2, o2, [(E2, e2)])


def third_kernel(spots, ranks, o2, u2, v2, e2, before, known, best, inverses):
    best[...] = before[...]
    inverses[...] = known[...]
    note(inverses, U2, u2)
    note(inverses, V2, v2)
    meet(best, inverses, ranks, O2, o2, [(U2, u2)])

    @pl.when(spots[0] == 0)
    def _():
        meet(best, inverses, ranks, E2, e2, [(V2, v2)])

    @pl.when(spots[0] != 0)
    def _():
        meet(best, inverses, ranks, E2, e2, [(U2, u2)])


def fourth_kernel(spots, ranks, before, known, u1, u2, v1, v2, w1, w2, *refs):
    *outs, best, inverses, near1, near2, far1, far2, sems = refs
    best[...] = before[...]
    inverses[...] = known[...]

    def opposite(name1, other1, name2, other2):
        pairs = ((u2, near2), (other2, far2), (u1, near1), (other1, far1))
        copies = [pltpu.make_async_copy(*pair, sems.at[i]) for i, pair in enumerate(pairs)]
        for copy in copies:
            copy.start()
        copies[0].wait()
        copies[1].wait()
        if name2 == W2:
            note(inverses, W2, far2)
        meet(best, inverses, ranks, U2, near2, [(name2, far2)])
        copies[2].wait()
        meet(best, inverses, ranks, name2, far2, [(U1, near1)])
        copies[3].wait()
        meet(best, inverses, ranks, U2, near2, [(name1, far1)])

    @pl.when(spots[1] != 0)
    def _():
        opposite(V1, v1, V2, v2)

    @pl.when(spots[1] == 0)
    def _():
        opposite(W1, w1, W2, w2)

    for i, out in enumerate(outs):
        for y in range(Y):
            at = pl.ds(y, 1)
            out[at, pl.ds(0, PARTS[0])] = best[pl.ds(2 * i, 1), pl.ds(y * PARTS[0], PARTS[0])]
            pair = best[pl.ds(2 * i + 1, 1), pl.ds(y // 2 * 128, 128)]
            pair = pltpu.roll(pair, 64, 1) if y % 2 else pair
            out[at, pl.ds(PARTS[0], PARTS[1])] = pair[:, : PARTS[1]]


def is_dims(item):
    return isinstance(item, tuple) and isinstance(item[0], int)


def scores_call(kernel, units, inputs, out, scratch, name, loose=0):
    return pl.pallas_call(
        kernel,
        out_shape=jax.tree.map(lambda dims: jax.ShapeDtypeStruct(dims, jnp.float32), out, is_leaf=is_dims),
        in_specs=[SMEM]
        + [VMEM] * (len(inputs) - 1 - loose)
        + [pl.BlockSpec(memory_space=pl.ANY)] * loose,
        out_specs=jax.tree.map(lambda _: VMEM, out, is_leaf=is_dims),
        scratch_shapes=scratch,
        compiler_params=PARAMS,
        cost_estimate=pl.CostEstimate(
            flops=int(units * 2 * 256 * 256 * 1024), bytes_accessed=4 * 2**20, transcendentals=0
        ),
        name=name,
    )(*inputs)


def answer_kernel(ids_ref, slot_ref, table_ref, out_ref):
    table = table_ref[...]
    high = table.astype(jnp.bfloat16)
    rest = table - high.astype(jnp.float32)
    middle = rest.astype(jnp.bfloat16)
    small = (rest - middle.astype(jnp.float32)).astype(jnp.bfloat16)
    pieces = jnp.concatenate([high, middle, small], axis=0)
    group = lax.broadcasted_iota(jnp.int32, (3 * GROUPS, 128), 0) & (GROUPS - 1)
    place_in = lax.broadcasted_iota(jnp.int32, (CAP, 128), 0)
    for i in range(LINES):
        ids = ids_ref[pl.ds(i, 1), :]
        within = slot_ref[pl.ds(i, 1), :] - ids * CAP
        member = (group == ids).astype(jnp.float32).astype(jnp.bfloat16)
        found = lax.dot_general(
            pieces, member, (((0,), (0,)), ((), ())), preferred_element_type=jnp.float32
        )
        out_ref[pl.ds(i, 1), :] = jnp.sum(
            jnp.where(place_in == within, found, 0.0), axis=0, keepdims=True
        )


def answer(ids, slots, table):
    return pl.pallas_call(
        answer_kernel,
        out_shape=jax.ShapeDtypeStruct((LINES, 128), jnp.float32),
        in_specs=[VMEM] * 3,
        out_specs=VMEM,
        compiler_params=PARAMS,
        name="answer",
    )(ids, slots, table)


def shards(embeds, cluster_ids, orders):
    y, x, core, z = (lax.axis_index(name) for name in ALL)
    swap = routes(lambda y, x, c, z: (y, x, 1 - c, z))
    ahead = routes(lambda y, x, c, z: (y, x + 1 - 2 * c, c, z))
    behind = routes(lambda y, x, c, z: (y, x - 1 + 2 * c, c, z))

    def bring(rows):
        part = rows.shape[0] // GROUPS
        return lax.all_to_all(
            rows.reshape(GROUPS, part, WIDTH), ("y", "z"), split_axis=0, concat_axis=0, tiled=True
        ).reshape(GROUPS * part, WIDTH)

    ids = cluster_ids.reshape(LINES, 128)
    placed1, slots = place(ids, embeds)
    o1 = bring(placed1)
    placed2 = place_rest(ids, slots, embeds)

    table = ranks(ids, slots, orders.reshape(LINES, 128)).reshape(Y, Z, CAP)
    table = lax.dynamic_index_in_dim(table, z, 1, keepdims=False)
    rank_parts = []
    for j in range(Y):
        row = lax.dynamic_slice_in_dim(table, (y + j) % Y, 1, 0)
        if j:
            row = lax.ppermute(row, ALL, routes(lambda y, x, c, z: (y + j, x, c, z)))
        rank_parts.append(row)
    own_ranks = jnp.concatenate(rank_parts)[(y - jnp.arange(Y)) % Y]
    own_ranks = jnp.where(own_ranks > 0, own_ranks, never_order)
    own_ranks = jnp.stack(
        [
            own_ranks[:, : PARTS[0]].reshape(SIZES[0]),
            jnp.pad(own_ranks[:, PARTS[0] :].reshape(SIZES[1]), (0, SIZES[0] - SIZES[1])),
        ]
    )
    near_ranks = lax.ppermute(own_ranks, ALL, ahead)
    member_ranks = jnp.concatenate(
        [
            own_ranks,
            near_ranks,
            lax.ppermute(own_ranks, ALL, behind),
            lax.ppermute(own_ranks, ALL, swap),
            lax.ppermute(near_ranks, ALL, swap),
            jnp.zeros((6, SIZES[0]), jnp.float32),
        ]
    )
    spots = jnp.stack([core, ((x < X // 2) == (core == 0)).astype(jnp.int32)]).astype(jnp.int32)
    o1, placed2, member_ranks, spots = lax.optimization_barrier((o1, placed2, member_ranks, spots))
    o2 = bring(placed2)

    def share(own, after):
        u = lax.ppermute(own, ALL, ahead)
        v = lax.ppermute(own, ALL, behind)
        e = lax.ppermute(own, ALL, swap)
        u, *after = lax.optimization_barrier((u, *after(e)))
        return (u, v, e, lax.ppermute(u, ALL, swap), *after)

    wide = (16, SIZES[0])

    def score(kernel, units, blocks, state, name):
        return scores_call(
            kernel, units, (spots, member_ranks, *blocks, *state), [wide, wide], [], name
        )

    u1, v1, e1, w1, *state, o2 = share(
        o1, lambda e: (*score(own_kernel, 8, (o1, e), (), "own"), o2)
    )

    def before_arrival(e2):
        first = score(first_kernel, 12, (o1, u1, v1, e1, w1), state, "first")
        return score(second_kernel, 14, (o1, o2, u1, v1, e1, e2), first, "second")

    u2, v2, e2, w2, *known = share(o2, before_arrival)
    best, inverses = score(third_kernel, 2, (o2, u2, v2, e2), known, "third")
    own, *others = scores_call(
        fourth_kernel, 5, (spots, member_ranks, best, inverses, u1, u2, v1, v2, w1, w2),
        [(Y, CAP)] * 5,
        [
            pltpu.VMEM(wide, jnp.float32),
            pltpu.VMEM(wide, jnp.float32),
            pltpu.VMEM((GROUPS * PARTS[0], WIDTH), jnp.bfloat16),
            pltpu.VMEM((GROUPS * PARTS[1], WIDTH), jnp.bfloat16),
            pltpu.VMEM((GROUPS * PARTS[0], WIDTH), jnp.bfloat16),
            pltpu.VMEM((GROUPS * PARTS[1], WIDTH), jnp.bfloat16),
            pltpu.SemaphoreType.DMA((4,)),
        ],
        "fourth", 6,
    )
    across = routes(lambda y, x, c, z: (y, x + 1 - 2 * c, 1 - c, z))
    for part, way in zip(others, (behind, ahead, swap, across)):
        own = jnp.maximum(own, lax.ppermute(part, ALL, way))
    table = lax.all_to_all(
        jnp.broadcast_to(own[:, None], (Y, Z, CAP)).reshape(GROUPS, CAP),
        ("y", "z"), split_axis=0, concat_axis=0, tiled=True,
    )
    return answer(ids, slots, table).reshape(ROWS)


def solution(mesh):
    fine = Mesh(mesh.devices.reshape(Y, X, C, Z), ALL)
    clus = ("y", "x", "core")
    return jax.shard_map(
        shards,
        mesh=fine,
        in_specs=(P(clus, "z"), P(clus), P(clus)),
        out_specs=P(clus),
        check_vma=False,
    )
```

```python
import functools

import jax
import jax.numpy as jnp
from jax import lax
from jax.experimental import pallas as pl
from jax.experimental.pallas import tpu as pltpu
from jax.sharding import Mesh, PartitionSpec as P

never_order = 2.0**30
low = -3e38
Y, X, C, Z = 4, 4, 2, 8
ROWS = 3072
GROUPS = 32
CAP = 192
WIDTH = 128
PARTS = (128, 64)
SIZES = (Y * 128, Y * 64)
LINES = ROWS // 128
ALL = ("y", "x", "core", "z")
PARAMS = pltpu.CompilerParams(vmem_limit_bytes=40 * 2**20)
VMEM = pl.BlockSpec(memory_space=pltpu.VMEM)
SMEM = pl.BlockSpec(memory_space=pltpu.SMEM)


def routes(move):
    pairs = []
    for y in range(Y):
        for x in range(X):
            for c in range(C):
                for z in range(Z):
                    y2, x2, c2, z2 = move(y, x, c, z)
                    to = (((y2 % Y) * X + x2 % X) * C + c2 % C) * Z + z2 % Z
                    pairs.append((((y * X + x) * C + c) * Z + z, to))
    return pairs


def scatter_rows(spot_sm, wide_ref, out_ref):
    @pl.loop(0, LINES)
    def _(i):
        for lane in range(128):
            spot = spot_sm[i, lane]
            out_ref[pl.ds(spot, 1), :] = wide_ref[pl.ds(i * 128 + lane, 1), :]


def place_kernel(
    ids_any, rows_any, placed_ref, slot_ref,
    ids_ref, rows_ref, member_ref, wide_ref, out_ref, spot_ref, spot_sm, sems,
):
    ids_copy = pltpu.make_async_copy(ids_any, ids_ref, sems.at[0])
    rows_copy = pltpu.make_async_copy(rows_any, rows_ref, sems.at[1])
    ids_copy.start()
    rows_copy.start()
    out_ref[...] = jnp.zeros_like(out_ref)
    r = lax.broadcasted_iota(jnp.int32, (128, 256), 0)
    c = lax.broadcasted_iota(jnp.int32, (128, 256), 1)
    weights = ((r < c) | (c >= 128)).astype(jnp.float32).astype(jnp.bfloat16)
    group = lax.broadcasted_iota(jnp.int32, (GROUPS, 128), 0)
    ids_copy.wait()
    for i in range(LINES):
        hit = group == ids_ref[pl.ds(i, 1), :]
        member_ref[pl.ds(i * GROUPS, GROUPS), :] = hit.astype(jnp.float32).astype(jnp.bfloat16)
    counts = jnp.dot(member_ref[...], weights, preferred_element_type=jnp.float32)
    carry = jnp.zeros((GROUPS, 128), jnp.float32)
    for i in range(LINES):
        part = counts[i * GROUPS : (i + 1) * GROUPS]
        line = ids_ref[pl.ds(i, 1), :]
        within = jnp.sum(jnp.where(group == line, part[:, :128] + carry, 0.0), axis=0, keepdims=True)
        within = within.astype(jnp.int32)
        slot_ref[pl.ds(i, 1), :] = line * CAP + within
        spot_ref[pl.ds(i, 1), :] = jnp.where(
            within < PARTS[0], line * PARTS[0] + within, GROUPS * PARTS[0]
        )
        carry = carry + part[:, 128:]
    copy = pltpu.make_async_copy(spot_ref, spot_sm, sems.at[2])
    copy.start()
    rows_copy.wait()
    wide_ref[...] = rows_ref[...].astype(jnp.float32)
    copy.wait()
    scatter_rows(spot_sm, wide_ref, out_ref)
    placed_ref[...] = out_ref[pl.ds(0, GROUPS * PARTS[0]), :].astype(jnp.bfloat16)


def place(ids, rows):
    return pl.pallas_call(
        place_kernel,
        out_shape=(
            jax.ShapeDtypeStruct((GROUPS * PARTS[0], WIDTH), jnp.bfloat16),
            jax.ShapeDtypeStruct((LINES, 128), jnp.int32),
        ),
        in_specs=[pl.BlockSpec(memory_space=pltpu.HBM)] * 2,
        out_specs=(VMEM, VMEM),
        scratch_shapes=[
            pltpu.VMEM((LINES, 128), jnp.int32),
            pltpu.VMEM((ROWS, WIDTH), jnp.bfloat16),
            pltpu.VMEM((LINES * GROUPS, 128), jnp.bfloat16),
            pltpu.VMEM((ROWS, WIDTH), jnp.float32),
            pltpu.VMEM((GROUPS * PARTS[0] + 8, WIDTH), jnp.float32),
            pltpu.VMEM((LINES, 128), jnp.int32),
            pltpu.SMEM((LINES, 128), jnp.int32),
            pltpu.SemaphoreType.DMA((3,)),
        ],
        compiler_params=pltpu.CompilerParams(vmem_limit_bytes=60 * 2**20),
        name="place",
    )(ids, rows)


def place_rest_kernel(
    ids_ref, slot_ref, rows_ref, placed_ref, wide_ref, out_ref, spot_ref, spot_sm, sem
):
    ids = ids_ref[...]
    within = slot_ref[...] - ids * CAP
    spot_ref[...] = jnp.where(
        within < PARTS[0], GROUPS * PARTS[1], ids * PARTS[1] + within - PARTS[0]
    )
    copy = pltpu.make_async_copy(spot_ref, spot_sm, sem)
    copy.start()
    out_ref[...] = jnp.zeros_like(out_ref)
    wide_ref[...] = rows_ref[...].astype(jnp.float32)
    copy.wait()
    scatter_rows(spot_sm, wide_ref, out_ref)
    placed_ref[...] = out_ref[pl.ds(0, GROUPS * PARTS[1]), :].astype(jnp.bfloat16)


def place_rest(ids, slots, rows):
    return pl.pallas_call(
        place_rest_kernel,
        out_shape=jax.ShapeDtypeStruct((GROUPS * PARTS[1], WIDTH), jnp.bfloat16),
        in_specs=[VMEM] * 3,
        out_specs=VMEM,
        scratch_shapes=[
            pltpu.VMEM((ROWS, WIDTH), jnp.float32),
            pltpu.VMEM((GROUPS * PARTS[1] + 8, WIDTH), jnp.float32),
            pltpu.VMEM((LINES, 128), jnp.int32),
            pltpu.SMEM((LINES, 128), jnp.int32),
            pltpu.SemaphoreType.DMA,
        ],
        compiler_params=PARAMS,
        name="place_rest",
    )(ids, slots, rows)


def ranks_kernel(ids_ref, slot_ref, orders_ref, table_ref):
    group = lax.broadcasted_iota(jnp.int32, (GROUPS, 128), 0)
    spot = lax.broadcasted_iota(jnp.int32, (CAP, 128), 0)
    total = jnp.zeros((3 * GROUPS, CAP), jnp.float32)
    for i in range(LINES):
        ids = ids_ref[pl.ds(i, 1), :]
        within = slot_ref[pl.ds(i, 1), :] - ids * CAP
        value = orders_ref[pl.ds(i, 1), :] + 1
        hit = group == ids
        digits = [
            jnp.where(hit, digit.astype(jnp.float32), 0.0)
            for digit in (value & 255, (value >> 8) & 255, value >> 16)
        ]
        left = jnp.concatenate(digits, axis=0).astype(jnp.bfloat16)
        right = (spot == within).astype(jnp.float32).astype(jnp.bfloat16)
        total = total + dot_rows(left, right)
    value = total[:GROUPS] + 256.0 * total[GROUPS : 2 * GROUPS] + 65536.0 * total[2 * GROUPS :]
    table_ref[...] = value


def ranks(ids, slots, orders):
    return pl.pallas_call(
        ranks_kernel,
        out_shape=jax.ShapeDtypeStruct((GROUPS, CAP), jnp.float32),
        in_specs=[VMEM] * 3,
        out_specs=VMEM,
        compiler_params=PARAMS,
        name="ranks",
    )(ids, slots, orders)


def dot_rows(p, q):
    return lax.dot_general(p, q, (((1,), (1,)), ((), ())), preferred_element_type=jnp.float32)


def eye():
    r = lax.broadcasted_iota(jnp.int32, (128, 128), 0)
    return r == lax.broadcasted_iota(jnp.int32, (128, 128), 1)


def to_row(col):
    pieces = []
    for i in range(col.shape[0] // 128):
        piece = jnp.broadcast_to(col[i * 128 : (i + 1) * 128], (128, 128))
        pieces.append(jnp.max(jnp.where(eye(), piece, low), axis=0, keepdims=True))
    return jnp.concatenate(pieces, axis=1)


def to_col(row):
    pieces = []
    for i in range(row.shape[1] // 128):
        piece = jnp.broadcast_to(row[:, i * 128 : (i + 1) * 128], (128, 128))
        pieces.append(jnp.max(jnp.where(eye(), piece, low), axis=1, keepdims=True))
    return jnp.concatenate(pieces, axis=0)


def part_of(ref):
    return ref.shape[0] // GROUPS


def size_of(ref):
    return Y * part_of(ref)


def rows_of(ref, start, count):
    part = part_of(ref)
    lines = []
    for y in range(start // part, (start + count) // part):
        pieces = [ref[pl.ds((y * Z + z) * part, part), :] for z in range(Z)]
        lines.append(jnp.concatenate(pieces, axis=1))
    return jnp.concatenate(lines, axis=0)


def note(inverses, name, ref):
    part = part_of(ref)
    cols = []
    for y in range(Y):
        total = jnp.zeros((part, WIDTH), jnp.float32)
        for z in range(Z):
            wide = ref[pl.ds((y * Z + z) * part, part), :].astype(jnp.float32)
            total = total + wide * wide
        cols.append(lax.rsqrt(jnp.sum(total, axis=1, keepdims=True) + 1e-06))
    inverses[pl.ds(name, 1), pl.ds(0, Y * part)] = to_row(jnp.concatenate(cols, axis=0))


def meet(best, inverses, ranks, p_name, p_ref, others):
    size = size_of(p_ref)
    at = (pl.ds(p_name, 1), pl.ds(0, size))
    inv_p, rank_p = to_col(inverses[at]), to_col(ranks[at])
    p_best = jnp.full((size, 128), low, jnp.float32)
    for q_name, q_ref in others:
        q_best = []
        for j in range(0, size_of(q_ref), 256):
            at = (pl.ds(q_name, 1), pl.ds(j, 256))
            s = dot_rows(rows_of(p_ref, 0, size), rows_of(q_ref, j, 256))
            s = s * inv_p * inverses[at]
            earlier = ranks[at] < rank_p
            mine = jnp.where(earlier, s, low)
            p_best = jnp.maximum(p_best, jnp.maximum(mine[:, :128], mine[:, 128:]))
            if q_name != p_name:
                q_best.append(jnp.max(jnp.where(earlier, low, s), axis=0, keepdims=True))
        if q_best:
            record(best, q_name, jnp.concatenate(q_best, axis=1))
    record(best, p_name, to_row(jnp.max(p_best, axis=1, keepdims=True)))


def record(best, name, row):
    at = (pl.ds(name, 1), pl.ds(0, row.shape[1]))
    best[at] = jnp.maximum(best[at], row)


O1, O2, U1, U2, V1, V2, E1, E2, W1, W2 = range(10)


def own_kernel(spots, ranks, o1, e1, best, inverses):
    best[...] = jnp.full_like(best, -1.0)
    inverses[...] = jnp.zeros_like(inverses)
    note(inverses, O1, o1)
    note(inverses, E1, e1)
    meet(best, inverses, ranks, O1, o1, [(O1, o1)])

    @pl.when(spots[0] == 0)
    def _():
        meet(best, inverses, ranks, O1, o1, [(E1, e1)])


def first_kernel(spots, ranks, o1, u1, v1, e1, w1, before, known, best, inverses):
    best[...] = before[...]
    inverses[...] = known[...]
    note(inverses, U1, u1)
    note(inverses, V1, v1)
    note(inverses, W1, w1)
    meet(best, inverses, ranks, O1, o1, [(U1, u1)])

    @pl.when(spots[0] == 0)
    def _():
        meet(best, inverses, ranks, E1, e1, [(V1, v1)])

    @pl.when(spots[0] != 0)
    def _():
        meet(best, inverses, ranks, E1, e1, [(U1, u1)])

    @pl.when(spots[1] != 0)
    def _():
        meet(best, inverses, ranks, U1, u1, [(V1, v1)])

    @pl.when(spots[1] == 0)
    def _():
        meet(best, inverses, ranks, U1, u1, [(W1, w1)])


def second_kernel(spots, ranks, o1, o2, u1, v1, e1, e2, before, known, best, inverses):
    best[...] = before[...]
    inverses[...] = known[...]
    note(inverses, O2, o2)
    note(inverses, E2, e2)
    meet(best, inverses, ranks, O2, o2, [(O1, o1), (O2, o2), (U1, u1), (V1, v1)])
    meet(best, inverses, ranks, E2, e2, [(O1, o1), (U1, u1), (V1, v1)])

    @pl.when(spots[0] != 0)
    def _():
        meet(best, inverses, ranks, O2, o2, [(E2, e2)])


def give(best, name, out):
    for y in range(Y):
        at = pl.ds(y, 1)
        out[at, pl.ds(0, PARTS[0])] = best[pl.ds(name, 1), pl.ds(y * PARTS[0], PARTS[0])]
        pair = best[pl.ds(name + 1, 1), pl.ds(y // 2 * 128, 128)]
        pair = pltpu.roll(pair, 64, 1) if y % 2 else pair
        out[at, pl.ds(PARTS[0], PARTS[1])] = pair[:, : PARTS[1]]


def third_kernel(spots, ranks, o2, u2, v2, e2, before, known, best, inverses, e_best):
    best[...] = before[...]
    inverses[...] = known[...]
    note(inverses, U2, u2)
    note(inverses, V2, v2)
    meet(best, inverses, ranks, O2, o2, [(U2, u2)])

    @pl.when(spots[0] == 0)
    def _():
        meet(best, inverses, ranks, E2, e2, [(V2, v2)])

    @pl.when(spots[0] != 0)
    def _():
        meet(best, inverses, ranks, E2, e2, [(U2, u2)])

    give(best, E1, e_best)


def fourth_kernel(
    spots, ranks, u1, u2, v1, v2, w1, w2, before, known, o_best, u_best, v_best, w_best,
    best, inverses,
):
    best[...] = before[...]
    inverses[...] = known[...]

    @pl.when(spots[1] != 0)
    def _():
        meet(best, inverses, ranks, V2, v2, [(U1, u1)])
        meet(best, inverses, ranks, U2, u2, [(V1, v1), (V2, v2)])

    @pl.when(spots[1] == 0)
    def _():
        note(inverses, W2, w2)
        meet(best, inverses, ranks, W2, w2, [(U1, u1)])
        meet(best, inverses, ranks, U2, u2, [(W1, w1), (W2, w2)])

    give(best, O1, o_best)
    give(best, U1, u_best)
    give(best, V1, v_best)
    give(best, W1, w_best)


def is_dims(item):
    return isinstance(item, tuple) and isinstance(item[0], int)


def scores_call(kernel, units, inputs, out, scratch, name):
    return pl.pallas_call(
        kernel,
        out_shape=jax.tree.map(lambda dims: jax.ShapeDtypeStruct(dims, jnp.float32), out, is_leaf=is_dims),
        in_specs=[SMEM] + [VMEM] * (len(inputs) - 1),
        out_specs=jax.tree.map(lambda _: VMEM, out, is_leaf=is_dims),
        scratch_shapes=scratch,
        compiler_params=PARAMS,
        cost_estimate=pl.CostEstimate(
            flops=int(units * 2 * 256 * 256 * 1024), bytes_accessed=4 * 2**20, transcendentals=0
        ),
        name=name,
    )(*inputs)


def answer_kernel(ids_ref, slot_ref, table_ref, out_ref):
    table = table_ref[...]
    high = table.astype(jnp.bfloat16)
    rest = table - high.astype(jnp.float32)
    middle = rest.astype(jnp.bfloat16)
    small = (rest - middle.astype(jnp.float32)).astype(jnp.bfloat16)
    pieces = jnp.concatenate([high, middle, small], axis=0)
    group = lax.broadcasted_iota(jnp.int32, (3 * GROUPS, 128), 0) & (GROUPS - 1)
    place_in = lax.broadcasted_iota(jnp.int32, (CAP, 128), 0)
    for i in range(LINES):
        ids = ids_ref[pl.ds(i, 1), :]
        within = slot_ref[pl.ds(i, 1), :] - ids * CAP
        member = (group == ids).astype(jnp.float32).astype(jnp.bfloat16)
        found = lax.dot_general(
            pieces, member, (((0,), (0,)), ((), ())), preferred_element_type=jnp.float32
        )
        out_ref[pl.ds(i, 1), :] = jnp.sum(
            jnp.where(place_in == within, found, 0.0), axis=0, keepdims=True
        )


def answer(ids, slots, table):
    return pl.pallas_call(
        answer_kernel,
        out_shape=jax.ShapeDtypeStruct((LINES, 128), jnp.float32),
        in_specs=[VMEM] * 3,
        out_specs=VMEM,
        compiler_params=PARAMS,
        name="answer",
    )(ids, slots, table)


def shards(embeds, cluster_ids, orders):
    y, x, core, z = (lax.axis_index(name) for name in ALL)
    swap = routes(lambda y, x, c, z: (y, x, 1 - c, z))
    ahead = routes(lambda y, x, c, z: (y, x + 1 - 2 * c, c, z))
    behind = routes(lambda y, x, c, z: (y, x - 1 + 2 * c, c, z))

    def bring(rows):
        part = rows.shape[0] // GROUPS
        return lax.all_to_all(
            rows.reshape(GROUPS, part, WIDTH), ("y", "z"), split_axis=0, concat_axis=0, tiled=True
        ).reshape(GROUPS * part, WIDTH)

    ids = cluster_ids.reshape(LINES, 128)
    placed1, slots = place(ids, embeds)
    o1 = bring(placed1)
    placed2 = place_rest(ids, slots, embeds)

    table = ranks(ids, slots, orders.reshape(LINES, 128)).reshape(Y, Z, CAP)
    table = lax.dynamic_index_in_dim(table, z, 1, keepdims=False)
    rank_parts = []
    for j in range(Y):
        row = lax.dynamic_slice_in_dim(table, (y + j) % Y, 1, 0)
        if j:
            row = lax.ppermute(row, ALL, routes(lambda y, x, c, z: (y + j, x, c, z)))
        rank_parts.append(row)
    own_ranks = jnp.concatenate(rank_parts)[(y - jnp.arange(Y)) % Y]
    own_ranks = jnp.where(own_ranks > 0, own_ranks, never_order)
    own_ranks = jnp.stack(
        [
            own_ranks[:, : PARTS[0]].reshape(SIZES[0]),
            jnp.pad(own_ranks[:, PARTS[0] :].reshape(SIZES[1]), (0, SIZES[0] - SIZES[1])),
        ]
    )
    near_ranks = lax.ppermute(own_ranks, ALL, ahead)
    member_ranks = jnp.concatenate(
        [
            own_ranks,
            near_ranks,
            lax.ppermute(own_ranks, ALL, behind),
            lax.ppermute(own_ranks, ALL, swap),
            lax.ppermute(near_ranks, ALL, swap),
            jnp.zeros((6, SIZES[0]), jnp.float32),
        ]
    )
    spots = jnp.stack([core, ((x < X // 2) == (core == 0)).astype(jnp.int32)]).astype(jnp.int32)
    o1, placed2, member_ranks, spots = lax.optimization_barrier((o1, placed2, member_ranks, spots))
    o2 = bring(placed2)

    def share(own, after):
        u = lax.ppermute(own, ALL, ahead)
        v = lax.ppermute(own, ALL, behind)
        e = lax.ppermute(own, ALL, swap)
        u, *after = lax.optimization_barrier((u, *after(e)))
        return (u, v, e, lax.ppermute(u, ALL, swap), *after)

    wide = (16, SIZES[0])

    def score(kernel, units, blocks, state, name, out=(wide, wide), scratch=()):
        inputs = (spots, member_ranks, *blocks, *state)
        return scores_call(kernel, units, inputs, list(out), list(scratch), name)

    u1, v1, e1, w1, *state, o2 = share(
        o1, lambda e: (*score(own_kernel, 8, (o1, e), (), "own"), o2)
    )

    def before_arrival(e2):
        first = score(first_kernel, 12, (o1, u1, v1, e1, w1), state, "first")
        return score(second_kernel, 14, (o1, o2, u1, v1, e1, e2), first, "second")

    u2, v2, e2, w2, *known = share(o2, before_arrival)
    across = routes(lambda y, x, c, z: (y, x + 1 - 2 * c, 1 - c, z))
    *known, e_best = score(
        third_kernel, 2, (o2, u2, v2, e2), known, "third", (wide, wide, (Y, CAP))
    )
    from_core = lax.ppermute(e_best, ALL, swap)
    own, *others = score(
        fourth_kernel, 5, (u1, u2, v1, v2, w1, w2), known, "fourth", [(Y, CAP)] * 4,
        [pltpu.VMEM(wide, jnp.float32)] * 2,
    )
    for part, way in zip(others, (behind, ahead, across)):
        own = jnp.maximum(own, lax.ppermute(part, ALL, way))
    own = jnp.maximum(own, from_core)
    table = lax.all_to_all(
        jnp.broadcast_to(own[:, None], (Y, Z, CAP)).reshape(GROUPS, CAP),
        ("y", "z"), split_axis=0, concat_axis=0, tiled=True,
    )
    return answer(ids, slots, table).reshape(ROWS)


def solution(mesh):
    fine = Mesh(mesh.devices.reshape(Y, X, C, Z), ALL)
    clus = ("y", "x", "core")
    return jax.shard_map(
        shards,
        mesh=fine,
        in_specs=(P(clus, "z"), P(clus), P(clus)),
        out_specs=P(clus),
        check_vma=False,
    )
```

```python
import functools

import jax
import jax.numpy as jnp
from jax import lax
from jax.experimental import pallas as pl
from jax.experimental.pallas import tpu as pltpu
from jax.sharding import Mesh, PartitionSpec as P

never_order = 2.0**30
low = -3e38
Y, X, C, Z = 4, 4, 2, 8
ROWS = 3072
GROUPS = 32
CAP = 192
WIDTH = 128
PARTS = (128, 64)
SIZES = (Y * 128, Y * 64)
LINES = ROWS // 128
ALL = ("y", "x", "core", "z")
PARAMS = pltpu.CompilerParams(vmem_limit_bytes=40 * 2**20)
VMEM = pl.BlockSpec(memory_space=pltpu.VMEM)
SMEM = pl.BlockSpec(memory_space=pltpu.SMEM)


def routes(move):
    pairs = []
    for y in range(Y):
        for x in range(X):
            for c in range(C):
                for z in range(Z):
                    y2, x2, c2, z2 = move(y, x, c, z)
                    to = (((y2 % Y) * X + x2 % X) * C + c2 % C) * Z + z2 % Z
                    pairs.append((((y * X + x) * C + c) * Z + z, to))
    return pairs


def scatter_rows(spot_sm, wide_ref, out_ref):
    @pl.loop(0, LINES)
    def _(i):
        for lane in range(128):
            spot = spot_sm[i, lane]
            out_ref[pl.ds(spot, 1), :] = wide_ref[pl.ds(i * 128 + lane, 1), :]


def place_kernel(
    ids_any, rows_any, placed_ref, slot_ref,
    ids_ref, rows_ref, member_ref, wide_ref, out_ref, spot_ref, spot_sm, sems,
):
    ids_copy = pltpu.make_async_copy(ids_any, ids_ref, sems.at[0])
    rows_copy = pltpu.make_async_copy(rows_any, rows_ref, sems.at[1])
    ids_copy.start()
    rows_copy.start()
    out_ref[...] = jnp.zeros_like(out_ref)
    r = lax.broadcasted_iota(jnp.int32, (128, 256), 0)
    c = lax.broadcasted_iota(jnp.int32, (128, 256), 1)
    weights = ((r < c) | (c >= 128)).astype(jnp.float32).astype(jnp.bfloat16)
    group = lax.broadcasted_iota(jnp.int32, (GROUPS, 128), 0)
    ids_copy.wait()
    for i in range(LINES):
        hit = group == ids_ref[pl.ds(i, 1), :]
        member_ref[pl.ds(i * GROUPS, GROUPS), :] = hit.astype(jnp.float32).astype(jnp.bfloat16)
    counts = jnp.dot(member_ref[...], weights, preferred_element_type=jnp.float32)
    carry = jnp.zeros((GROUPS, 128), jnp.float32)
    for i in range(LINES):
        part = counts[i * GROUPS : (i + 1) * GROUPS]
        line = ids_ref[pl.ds(i, 1), :]
        within = jnp.sum(jnp.where(group == line, part[:, :128] + carry, 0.0), axis=0, keepdims=True)
        within = within.astype(jnp.int32)
        slot_ref[pl.ds(i, 1), :] = line * CAP + within
        spot_ref[pl.ds(i, 1), :] = jnp.where(
            within < PARTS[0], line * PARTS[0] + within, GROUPS * PARTS[0]
        )
        carry = carry + part[:, 128:]
    copy = pltpu.make_async_copy(spot_ref, spot_sm, sems.at[2])
    copy.start()
    rows_copy.wait()
    wide_ref[...] = rows_ref[...].astype(jnp.float32)
    copy.wait()
    scatter_rows(spot_sm, wide_ref, out_ref)
    placed_ref[...] = out_ref[pl.ds(0, GROUPS * PARTS[0]), :].astype(jnp.bfloat16)


def place(ids, rows):
    return pl.pallas_call(
        place_kernel,
        out_shape=(
            jax.ShapeDtypeStruct((GROUPS * PARTS[0], WIDTH), jnp.bfloat16),
            jax.ShapeDtypeStruct((LINES, 128), jnp.int32),
        ),
        in_specs=[pl.BlockSpec(memory_space=pltpu.HBM)] * 2,
        out_specs=(VMEM, VMEM),
        scratch_shapes=[
            pltpu.VMEM((LINES, 128), jnp.int32),
            pltpu.VMEM((ROWS, WIDTH), jnp.bfloat16),
            pltpu.VMEM((LINES * GROUPS, 128), jnp.bfloat16),
            pltpu.VMEM((ROWS, WIDTH), jnp.float32),
            pltpu.VMEM((GROUPS * PARTS[0] + 8, WIDTH), jnp.float32),
            pltpu.VMEM((LINES, 128), jnp.int32),
            pltpu.SMEM((LINES, 128), jnp.int32),
            pltpu.SemaphoreType.DMA((3,)),
        ],
        compiler_params=pltpu.CompilerParams(vmem_limit_bytes=60 * 2**20),
        name="place",
    )(ids, rows)


def place_rest_kernel(
    ids_ref, slot_ref, rows_ref, placed_ref, wide_ref, out_ref, spot_ref, spot_sm, sem
):
    ids = ids_ref[...]
    within = slot_ref[...] - ids * CAP
    spot_ref[...] = jnp.where(
        within < PARTS[0], GROUPS * PARTS[1], ids * PARTS[1] + within - PARTS[0]
    )
    copy = pltpu.make_async_copy(spot_ref, spot_sm, sem)
    copy.start()
    out_ref[...] = jnp.zeros_like(out_ref)
    wide_ref[...] = rows_ref[...].astype(jnp.float32)
    copy.wait()
    scatter_rows(spot_sm, wide_ref, out_ref)
    placed_ref[...] = out_ref[pl.ds(0, GROUPS * PARTS[1]), :].astype(jnp.bfloat16)


def place_rest(ids, slots, rows):
    return pl.pallas_call(
        place_rest_kernel,
        out_shape=jax.ShapeDtypeStruct((GROUPS * PARTS[1], WIDTH), jnp.bfloat16),
        in_specs=[VMEM] * 3,
        out_specs=VMEM,
        scratch_shapes=[
            pltpu.VMEM((ROWS, WIDTH), jnp.float32),
            pltpu.VMEM((GROUPS * PARTS[1] + 8, WIDTH), jnp.float32),
            pltpu.VMEM((LINES, 128), jnp.int32),
            pltpu.SMEM((LINES, 128), jnp.int32),
            pltpu.SemaphoreType.DMA,
        ],
        compiler_params=PARAMS,
        name="place_rest",
    )(ids, slots, rows)


def ranks_kernel(ids_ref, slot_ref, orders_ref, table_ref):
    group = lax.broadcasted_iota(jnp.int32, (GROUPS, 128), 0)
    spot = lax.broadcasted_iota(jnp.int32, (CAP, 128), 0)
    total = jnp.zeros((3 * GROUPS, CAP), jnp.float32)
    for i in range(LINES):
        ids = ids_ref[pl.ds(i, 1), :]
        within = slot_ref[pl.ds(i, 1), :] - ids * CAP
        value = orders_ref[pl.ds(i, 1), :] + 1
        hit = group == ids
        digits = [
            jnp.where(hit, digit.astype(jnp.float32), 0.0)
            for digit in (value & 255, (value >> 8) & 255, value >> 16)
        ]
        left = jnp.concatenate(digits, axis=0).astype(jnp.bfloat16)
        right = (spot == within).astype(jnp.float32).astype(jnp.bfloat16)
        total = total + dot_rows(left, right)
    value = total[:GROUPS] + 256.0 * total[GROUPS : 2 * GROUPS] + 65536.0 * total[2 * GROUPS :]
    table_ref[...] = value


def ranks(ids, slots, orders):
    return pl.pallas_call(
        ranks_kernel,
        out_shape=jax.ShapeDtypeStruct((GROUPS, CAP), jnp.float32),
        in_specs=[VMEM] * 3,
        out_specs=VMEM,
        compiler_params=PARAMS,
        name="ranks",
    )(ids, slots, orders)


def dot_rows(p, q):
    return lax.dot_general(p, q, (((1,), (1,)), ((), ())), preferred_element_type=jnp.float32)


def eye():
    r = lax.broadcasted_iota(jnp.int32, (128, 128), 0)
    return r == lax.broadcasted_iota(jnp.int32, (128, 128), 1)


def to_row(col):
    pieces = []
    for i in range(col.shape[0] // 128):
        piece = jnp.broadcast_to(col[i * 128 : (i + 1) * 128], (128, 128))
        pieces.append(jnp.max(jnp.where(eye(), piece, low), axis=0, keepdims=True))
    return jnp.concatenate(pieces, axis=1)


def to_col(row):
    pieces = []
    for i in range(row.shape[1] // 128):
        piece = jnp.broadcast_to(row[:, i * 128 : (i + 1) * 128], (128, 128))
        pieces.append(jnp.max(jnp.where(eye(), piece, low), axis=1, keepdims=True))
    return jnp.concatenate(pieces, axis=0)


def part_of(ref):
    return ref.shape[0] // GROUPS


def size_of(ref):
    return Y * part_of(ref)


def rows_of(ref, start, count):
    part = part_of(ref)
    lines = []
    for y in range(start // part, (start + count) // part):
        pieces = [ref[pl.ds((y * Z + z) * part, part), :] for z in range(Z)]
        lines.append(jnp.concatenate(pieces, axis=1))
    return jnp.concatenate(lines, axis=0)


def note(inverses, name, ref):
    part = part_of(ref)
    cols = []
    for y in range(Y):
        total = jnp.zeros((part, WIDTH), jnp.float32)
        for z in range(Z):
            wide = ref[pl.ds((y * Z + z) * part, part), :].astype(jnp.float32)
            total = total + wide * wide
        cols.append(lax.rsqrt(jnp.sum(total, axis=1, keepdims=True) + 1e-06))
    inverses[pl.ds(name, 1), pl.ds(0, Y * part)] = to_row(jnp.concatenate(cols, axis=0))


def meet(best, inverses, ranks, p_name, p_ref, others):
    size = size_of(p_ref)
    at = (pl.ds(p_name, 1), pl.ds(0, size))
    inv_p, rank_p = to_col(inverses[at]), to_col(ranks[at])
    p_best = jnp.full((size, 128), low, jnp.float32)
    for q_name, q_ref in others:
        q_best = []
        for j in range(0, size_of(q_ref), 256):
            at = (pl.ds(q_name, 1), pl.ds(j, 256))
            s = dot_rows(rows_of(p_ref, 0, size), rows_of(q_ref, j, 256))
            s = s * inv_p * inverses[at]
            earlier = ranks[at] < rank_p
            mine = jnp.where(earlier, s, low)
            p_best = jnp.maximum(p_best, jnp.maximum(mine[:, :128], mine[:, 128:]))
            if q_name != p_name:
                q_best.append(jnp.max(jnp.where(earlier, low, s), axis=0, keepdims=True))
        if q_best:
            record(best, q_name, jnp.concatenate(q_best, axis=1))
    record(best, p_name, to_row(jnp.max(p_best, axis=1, keepdims=True)))


def record(best, name, row):
    at = (pl.ds(name, 1), pl.ds(0, row.shape[1]))
    best[at] = jnp.maximum(best[at], row)


O1, O2, U1, U2, V1, V2, E1, E2, W1, W2 = range(10)


def own_kernel(spots, ranks, o1, e1, best, inverses):
    best[...] = jnp.full_like(best, -1.0)
    inverses[...] = jnp.zeros_like(inverses)
    note(inverses, O1, o1)
    note(inverses, E1, e1)
    meet(best, inverses, ranks, O1, o1, [(O1, o1)])

    @pl.when(spots[0] == 0)
    def _():
        meet(best, inverses, ranks, O1, o1, [(E1, e1)])


def first_kernel(spots, ranks, o1, u1, v1, e1, w1, before, known, best, inverses):
    best[...] = before[...]
    inverses[...] = known[...]
    note(inverses, U1, u1)
    note(inverses, V1, v1)
    note(inverses, W1, w1)
    meet(best, inverses, ranks, O1, o1, [(U1, u1)])

    @pl.when(spots[0] == 0)
    def _():
        meet(best, inverses, ranks, E1, e1, [(V1, v1)])

    @pl.when(spots[0] != 0)
    def _():
        meet(best, inverses, ranks, E1, e1, [(U1, u1)])

    @pl.when(spots[1] != 0)
    def _():
        meet(best, inverses, ranks, U1, u1, [(V1, v1)])

    @pl.when(spots[1] == 0)
    def _():
        meet(best, inverses, ranks, U1, u1, [(W1, w1)])


def second_kernel(spots, ranks, o1, o2, u1, v1, e1, e2, before, known, best, inverses):
    best[...] = before[...]
    inverses[...] = known[...]
    note(inverses, O2, o2)
    note(inverses, E2, e2)
    meet(best, inverses, ranks, O2, o2, [(O1, o1), (O2, o2), (U1, u1), (V1, v1)])
    meet(best, inverses, ranks, E2, e2, [(O1, o1), (U1, u1), (V1, v1)])

    @pl.when(spots[0] != 0)
    def _():
        meet(best, inverses, ranks, O2, o2, [(E2, e2)])


def give(best, name, out):
    for y in range(Y):
        at = pl.ds(y, 1)
        out[at, pl.ds(0, PARTS[0])] = best[pl.ds(name, 1), pl.ds(y * PARTS[0], PARTS[0])]
        pair = best[pl.ds(name + 1, 1), pl.ds(y // 2 * 128, 128)]
        pair = pltpu.roll(pair, 64, 1) if y % 2 else pair
        out[at, pl.ds(PARTS[0], PARTS[1])] = pair[:, : PARTS[1]]


def third_kernel(spots, ranks, o2, u2, e2, v1, w1, before, known, best, inverses):
    best[...] = before[...]
    inverses[...] = known[...]
    note(inverses, U2, u2)
    meet(best, inverses, ranks, U2, u2, [(O2, o2)])

    @pl.when(spots[0] != 0)
    def _():
        meet(best, inverses, ranks, U2, u2, [(E2, e2)])

    @pl.when(spots[1] != 0)
    def _():
        meet(best, inverses, ranks, U2, u2, [(V1, v1)])

    @pl.when(spots[1] == 0)
    def _():
        meet(best, inverses, ranks, U2, u2, [(W1, w1)])


def fourth_kernel(
    spots, ranks, u1, u2, v2, e2, w2, before, known, o_best, u_best, v_best, e_best, w_best,
    best, inverses,
):
    best[...] = before[...]
    inverses[...] = known[...]
    note(inverses, V2, v2)

    @pl.when(spots[0] == 0)
    def _():
        meet(best, inverses, ranks, V2, v2, [(E2, e2)])

    @pl.when(spots[1] != 0)
    def _():
        meet(best, inverses, ranks, V2, v2, [(U1, u1), (U2, u2)])

    @pl.when(spots[1] == 0)
    def _():
        note(inverses, W2, w2)
        meet(best, inverses, ranks, W2, w2, [(U1, u1), (U2, u2)])

    give(best, O1, o_best)
    give(best, U1, u_best)
    give(best, V1, v_best)
    give(best, E1, e_best)
    give(best, W1, w_best)


def is_dims(item):
    return isinstance(item, tuple) and isinstance(item[0], int)


def scores_call(kernel, units, inputs, out, scratch, name):
    return pl.pallas_call(
        kernel,
        out_shape=jax.tree.map(lambda dims: jax.ShapeDtypeStruct(dims, jnp.float32), out, is_leaf=is_dims),
        in_specs=[SMEM] + [VMEM] * (len(inputs) - 1),
        out_specs=jax.tree.map(lambda _: VMEM, out, is_leaf=is_dims),
        scratch_shapes=scratch,
        compiler_params=PARAMS,
        cost_estimate=pl.CostEstimate(
            flops=int(units * 2 * 256 * 256 * 1024), bytes_accessed=4 * 2**20, transcendentals=0
        ),
        name=name,
    )(*inputs)


def answer_kernel(ids_ref, slot_ref, table_ref, out_ref):
    table = table_ref[...]
    high = table.astype(jnp.bfloat16)
    rest = table - high.astype(jnp.float32)
    middle = rest.astype(jnp.bfloat16)
    small = (rest - middle.astype(jnp.float32)).astype(jnp.bfloat16)
    pieces = jnp.concatenate([high, middle, small], axis=0)
    group = lax.broadcasted_iota(jnp.int32, (3 * GROUPS, 128), 0) & (GROUPS - 1)
    place_in = lax.broadcasted_iota(jnp.int32, (CAP, 128), 0)
    for i in range(LINES):
        ids = ids_ref[pl.ds(i, 1), :]
        within = slot_ref[pl.ds(i, 1), :] - ids * CAP
        member = (group == ids).astype(jnp.float32).astype(jnp.bfloat16)
        found = lax.dot_general(
            pieces, member, (((0,), (0,)), ((), ())), preferred_element_type=jnp.float32
        )
        out_ref[pl.ds(i, 1), :] = jnp.sum(
            jnp.where(place_in == within, found, 0.0), axis=0, keepdims=True
        )


def answer(ids, slots, table):
    return pl.pallas_call(
        answer_kernel,
        out_shape=jax.ShapeDtypeStruct((LINES, 128), jnp.float32),
        in_specs=[VMEM] * 3,
        out_specs=VMEM,
        compiler_params=PARAMS,
        name="answer",
    )(ids, slots, table)


def shards(embeds, cluster_ids, orders):
    y, x, core, z = (lax.axis_index(name) for name in ALL)
    swap = routes(lambda y, x, c, z: (y, x, 1 - c, z))
    ahead = routes(lambda y, x, c, z: (y, x + 1 - 2 * c, c, z))
    behind = routes(lambda y, x, c, z: (y, x - 1 + 2 * c, c, z))

    def bring(rows):
        part = rows.shape[0] // GROUPS
        return lax.all_to_all(
            rows.reshape(GROUPS, part, WIDTH), ("y", "z"), split_axis=0, concat_axis=0, tiled=True
        ).reshape(GROUPS * part, WIDTH)

    ids = cluster_ids.reshape(LINES, 128)
    placed1, slots = place(ids, embeds)
    o1 = bring(placed1)
    placed2 = place_rest(ids, slots, embeds)

    table = ranks(ids, slots, orders.reshape(LINES, 128)).reshape(Y, Z, CAP)
    table = lax.dynamic_index_in_dim(table, z, 1, keepdims=False)
    rank_parts = []
    for j in range(Y):
        row = lax.dynamic_slice_in_dim(table, (y + j) % Y, 1, 0)
        if j:
            row = lax.ppermute(row, ALL, routes(lambda y, x, c, z: (y + j, x, c, z)))
        rank_parts.append(row)
    own_ranks = jnp.concatenate(rank_parts)[(y - jnp.arange(Y)) % Y]
    own_ranks = jnp.where(own_ranks > 0, own_ranks, never_order)
    own_ranks = jnp.stack(
        [
            own_ranks[:, : PARTS[0]].reshape(SIZES[0]),
            jnp.pad(own_ranks[:, PARTS[0] :].reshape(SIZES[1]), (0, SIZES[0] - SIZES[1])),
        ]
    )
    near_ranks = lax.ppermute(own_ranks, ALL, ahead)
    member_ranks = jnp.concatenate(
        [
            own_ranks,
            near_ranks,
            lax.ppermute(own_ranks, ALL, behind),
            lax.ppermute(own_ranks, ALL, swap),
            lax.ppermute(near_ranks, ALL, swap),
            jnp.zeros((6, SIZES[0]), jnp.float32),
        ]
    )
    spots = jnp.stack([core, ((x < X // 2) == (core == 0)).astype(jnp.int32)]).astype(jnp.int32)
    o1, placed2, member_ranks, spots = lax.optimization_barrier((o1, placed2, member_ranks, spots))
    o2 = bring(placed2)

    wide = (16, SIZES[0])

    def score(kernel, units, blocks, state, name, out=(wide, wide), scratch=()):
        inputs = (spots, member_ranks, *blocks, *state)
        return scores_call(kernel, units, inputs, list(out), list(scratch), name)

    u1 = lax.ppermute(o1, ALL, ahead)
    v1 = lax.ppermute(o1, ALL, behind)
    e1 = lax.ppermute(o1, ALL, swap)
    state = score(own_kernel, 8, (o1, e1), (), "own")
    u1, o2, *state = lax.optimization_barrier((u1, o2, *state))
    w1 = lax.ppermute(u1, ALL, swap)

    u2 = lax.ppermute(o2, ALL, ahead)
    e2 = lax.ppermute(o2, ALL, swap)
    state = score(first_kernel, 12, (o1, u1, v1, e1, w1), state, "first")
    o2, *state = lax.optimization_barrier((o2, *state))
    v2 = lax.ppermute(o2, ALL, behind)
    state = score(second_kernel, 14, (o1, o2, u1, v1, e1, e2), state, "second")
    u2, *state = lax.optimization_barrier((u2, *state))
    w2 = lax.ppermute(u2, ALL, swap)
    state = score(third_kernel, 4, (o2, u2, e2, v1, w1), state, "third")
    v2, *state = lax.optimization_barrier((v2, *state))
    own, *others = score(
        fourth_kernel, 4, (u1, u2, v2, e2, w2), state, "fourth", [(Y, CAP)] * 5,
        [pltpu.VMEM(wide, jnp.float32)] * 2,
    )

    across = routes(lambda y, x, c, z: (y, x + 1 - 2 * c, 1 - c, z))
    for part, way in zip(others, (behind, ahead, swap, across)):
        own = jnp.maximum(own, lax.ppermute(part, ALL, way))
    table = lax.all_to_all(
        jnp.broadcast_to(own[:, None], (Y, Z, CAP)).reshape(GROUPS, CAP),
        ("y", "z"), split_axis=0, concat_axis=0, tiled=True,
    )
    return answer(ids, slots, table).reshape(ROWS)


def solution(mesh):
    fine = Mesh(mesh.devices.reshape(Y, X, C, Z), ALL)
    clus = ("y", "x", "core")
    return jax.shard_map(
        shards,
        mesh=fine,
        in_specs=(P(clus, "z"), P(clus), P(clus)),
        out_specs=P(clus),
        check_vma=False,
    )
```

```python
import functools

import jax
import jax.numpy as jnp
from jax import lax
from jax.experimental import pallas as pl
from jax.experimental.pallas import tpu as pltpu
from jax.sharding import Mesh, PartitionSpec as P

never_order = 2.0**30
low = -3e38
Y, X, C, Z = 4, 4, 2, 8
ROWS = 3072
GROUPS = 32
CAP = 192
WIDTH = 128
PARTS = (128, 64)
SIZES = (Y * 128, Y * 64)
LINES = ROWS // 128
ALL = ("y", "x", "core", "z")
PARAMS = pltpu.CompilerParams(vmem_limit_bytes=40 * 2**20)
VMEM = pl.BlockSpec(memory_space=pltpu.VMEM)
SMEM = pl.BlockSpec(memory_space=pltpu.SMEM)


def routes(move):
    pairs = []
    for y in range(Y):
        for x in range(X):
            for c in range(C):
                for z in range(Z):
                    y2, x2, c2, z2 = move(y, x, c, z)
                    to = (((y2 % Y) * X + x2 % X) * C + c2 % C) * Z + z2 % Z
                    pairs.append((((y * X + x) * C + c) * Z + z, to))
    return pairs


def scatter_rows(spot_sm, wide_ref, out_ref):
    @pl.loop(0, LINES)
    def _(i):
        for lane in range(128):
            spot = spot_sm[i, lane]
            out_ref[pl.ds(spot, 1), :] = wide_ref[pl.ds(i * 128 + lane, 1), :]


def place_kernel(
    ids_any, rows_any, placed_ref, slot_ref,
    ids_ref, rows_ref, member_ref, wide_ref, out_ref, spot_ref, spot_sm, sems,
):
    ids_copy = pltpu.make_async_copy(ids_any, ids_ref, sems.at[0])
    rows_copy = pltpu.make_async_copy(rows_any, rows_ref, sems.at[1])
    ids_copy.start()
    rows_copy.start()
    out_ref[...] = jnp.zeros_like(out_ref)
    r = lax.broadcasted_iota(jnp.int32, (128, 256), 0)
    c = lax.broadcasted_iota(jnp.int32, (128, 256), 1)
    weights = ((r < c) | (c >= 128)).astype(jnp.float32).astype(jnp.bfloat16)
    group = lax.broadcasted_iota(jnp.int32, (GROUPS, 128), 0)
    ids_copy.wait()
    for i in range(LINES):
        hit = group == ids_ref[pl.ds(i, 1), :]
        member_ref[pl.ds(i * GROUPS, GROUPS), :] = hit.astype(jnp.float32).astype(jnp.bfloat16)
    counts = jnp.dot(member_ref[...], weights, preferred_element_type=jnp.float32)
    carry = jnp.zeros((GROUPS, 128), jnp.float32)
    for i in range(LINES):
        part = counts[i * GROUPS : (i + 1) * GROUPS]
        line = ids_ref[pl.ds(i, 1), :]
        within = jnp.sum(jnp.where(group == line, part[:, :128] + carry, 0.0), axis=0, keepdims=True)
        within = within.astype(jnp.int32)
        slot_ref[pl.ds(i, 1), :] = line * CAP + within
        spot_ref[pl.ds(i, 1), :] = jnp.where(
            within < PARTS[0], line * PARTS[0] + within, GROUPS * PARTS[0]
        )
        carry = carry + part[:, 128:]
    copy = pltpu.make_async_copy(spot_ref, spot_sm, sems.at[2])
    copy.start()
    rows_copy.wait()
    wide_ref[...] = rows_ref[...].astype(jnp.float32)
    copy.wait()
    scatter_rows(spot_sm, wide_ref, out_ref)
    placed_ref[...] = out_ref[pl.ds(0, GROUPS * PARTS[0]), :].astype(jnp.bfloat16)


def place(ids, rows):
    return pl.pallas_call(
        place_kernel,
        out_shape=(
            jax.ShapeDtypeStruct((GROUPS * PARTS[0], WIDTH), jnp.bfloat16),
            jax.ShapeDtypeStruct((LINES, 128), jnp.int32),
        ),
        in_specs=[pl.BlockSpec(memory_space=pltpu.HBM)] * 2,
        out_specs=(VMEM, VMEM),
        scratch_shapes=[
            pltpu.VMEM((LINES, 128), jnp.int32),
            pltpu.VMEM((ROWS, WIDTH), jnp.bfloat16),
            pltpu.VMEM((LINES * GROUPS, 128), jnp.bfloat16),
            pltpu.VMEM((ROWS, WIDTH), jnp.float32),
            pltpu.VMEM((GROUPS * PARTS[0] + 8, WIDTH), jnp.float32),
            pltpu.VMEM((LINES, 128), jnp.int32),
            pltpu.SMEM((LINES, 128), jnp.int32),
            pltpu.SemaphoreType.DMA((3,)),
        ],
        compiler_params=pltpu.CompilerParams(vmem_limit_bytes=60 * 2**20),
        name="place",
    )(ids, rows)


def place_rest_kernel(
    ids_ref, slot_ref, rows_ref, placed_ref, wide_ref, out_ref, spot_ref, spot_sm, sem
):
    ids = ids_ref[...]
    within = slot_ref[...] - ids * CAP
    spot_ref[...] = jnp.where(
        within < PARTS[0], GROUPS * PARTS[1], ids * PARTS[1] + within - PARTS[0]
    )
    copy = pltpu.make_async_copy(spot_ref, spot_sm, sem)
    copy.start()
    out_ref[...] = jnp.zeros_like(out_ref)
    wide_ref[...] = rows_ref[...].astype(jnp.float32)
    copy.wait()
    scatter_rows(spot_sm, wide_ref, out_ref)
    placed_ref[...] = out_ref[pl.ds(0, GROUPS * PARTS[1]), :].astype(jnp.bfloat16)


def place_rest(ids, slots, rows):
    return pl.pallas_call(
        place_rest_kernel,
        out_shape=jax.ShapeDtypeStruct((GROUPS * PARTS[1], WIDTH), jnp.bfloat16),
        in_specs=[VMEM] * 3,
        out_specs=VMEM,
        scratch_shapes=[
            pltpu.VMEM((ROWS, WIDTH), jnp.float32),
            pltpu.VMEM((GROUPS * PARTS[1] + 8, WIDTH), jnp.float32),
            pltpu.VMEM((LINES, 128), jnp.int32),
            pltpu.SMEM((LINES, 128), jnp.int32),
            pltpu.SemaphoreType.DMA,
        ],
        compiler_params=PARAMS,
        name="place_rest",
    )(ids, slots, rows)


def ranks_kernel(ids_ref, slot_ref, orders_ref, table_ref):
    group = lax.broadcasted_iota(jnp.int32, (GROUPS, 128), 0)
    spot = lax.broadcasted_iota(jnp.int32, (CAP, 128), 0)
    total = jnp.zeros((3 * GROUPS, CAP), jnp.float32)
    for i in range(LINES):
        ids = ids_ref[pl.ds(i, 1), :]
        within = slot_ref[pl.ds(i, 1), :] - ids * CAP
        value = orders_ref[pl.ds(i, 1), :] + 1
        hit = group == ids
        digits = [
            jnp.where(hit, digit.astype(jnp.float32), 0.0)
            for digit in (value & 255, (value >> 8) & 255, value >> 16)
        ]
        left = jnp.concatenate(digits, axis=0).astype(jnp.bfloat16)
        right = (spot == within).astype(jnp.float32).astype(jnp.bfloat16)
        total = total + dot_rows(left, right)
    value = total[:GROUPS] + 256.0 * total[GROUPS : 2 * GROUPS] + 65536.0 * total[2 * GROUPS :]
    table_ref[...] = value


def ranks(ids, slots, orders):
    return pl.pallas_call(
        ranks_kernel,
        out_shape=jax.ShapeDtypeStruct((GROUPS, CAP), jnp.float32),
        in_specs=[VMEM] * 3,
        out_specs=VMEM,
        compiler_params=PARAMS,
        name="ranks",
    )(ids, slots, orders)


def dot_rows(p, q):
    return lax.dot_general(p, q, (((1,), (1,)), ((), ())), preferred_element_type=jnp.float32)


def eye():
    r = lax.broadcasted_iota(jnp.int32, (128, 128), 0)
    return r == lax.broadcasted_iota(jnp.int32, (128, 128), 1)


def to_row(col):
    pieces = []
    for i in range(col.shape[0] // 128):
        piece = jnp.broadcast_to(col[i * 128 : (i + 1) * 128], (128, 128))
        pieces.append(jnp.max(jnp.where(eye(), piece, low), axis=0, keepdims=True))
    return jnp.concatenate(pieces, axis=1)


def to_col(row):
    pieces = []
    for i in range(row.shape[1] // 128):
        piece = jnp.broadcast_to(row[:, i * 128 : (i + 1) * 128], (128, 128))
        pieces.append(jnp.max(jnp.where(eye(), piece, low), axis=1, keepdims=True))
    return jnp.concatenate(pieces, axis=0)


def part_of(ref):
    return ref.shape[0] // GROUPS


def size_of(ref):
    return Y * part_of(ref)


def rows_of(ref, start, count):
    part = part_of(ref)
    lines = []
    for y in range(start // part, (start + count) // part):
        pieces = [ref[pl.ds((y * Z + z) * part, part), :] for z in range(Z)]
        lines.append(jnp.concatenate(pieces, axis=1))
    return jnp.concatenate(lines, axis=0)


def note(inverses, name, ref):
    part = part_of(ref)
    cols = []
    for y in range(Y):
        total = jnp.zeros((part, WIDTH), jnp.float32)
        for z in range(Z):
            wide = ref[pl.ds((y * Z + z) * part, part), :].astype(jnp.float32)
            total = total + wide * wide
        cols.append(lax.rsqrt(jnp.sum(total, axis=1, keepdims=True) + 1e-06))
    inverses[pl.ds(name, 1), pl.ds(0, Y * part)] = to_row(jnp.concatenate(cols, axis=0))


def meet(best, inverses, ranks, p_name, p_ref, others):
    size = size_of(p_ref)
    at = (pl.ds(p_name, 1), pl.ds(0, size))
    inv_p, rank_p = to_col(inverses[at]), to_col(ranks[at])
    p_best = jnp.full((size, 128), low, jnp.float32)
    for q_name, q_ref in others:
        q_best = []
        for j in range(0, size_of(q_ref), 256):
            at = (pl.ds(q_name, 1), pl.ds(j, 256))
            s = dot_rows(rows_of(p_ref, 0, size), rows_of(q_ref, j, 256))
            s = s * inv_p * inverses[at]
            earlier = ranks[at] < rank_p
            mine = jnp.where(earlier, s, low)
            p_best = jnp.maximum(p_best, jnp.maximum(mine[:, :128], mine[:, 128:]))
            if q_name != p_name:
                q_best.append(jnp.max(jnp.where(earlier, low, s), axis=0, keepdims=True))
        if q_best:
            record(best, q_name, jnp.concatenate(q_best, axis=1))
    record(best, p_name, to_row(jnp.max(p_best, axis=1, keepdims=True)))


def record(best, name, row):
    at = (pl.ds(name, 1), pl.ds(0, row.shape[1]))
    best[at] = jnp.maximum(best[at], row)


O1, O2, U1, U2, V1, V2, E1, E2, W1, W2 = range(10)


def own_kernel(spots, ranks, o1, e1, best, inverses):
    best[...] = jnp.full_like(best, -1.0)
    inverses[...] = jnp.zeros_like(inverses)
    note(inverses, O1, o1)
    note(inverses, E1, e1)
    meet(best, inverses, ranks, O1, o1, [(O1, o1)])

    @pl.when(spots[0] == 0)
    def _():
        meet(best, inverses, ranks, O1, o1, [(E1, e1)])


def near_kernel(spots, ranks, o1, u1, e1, before, known, best, inverses):
    best[...] = before[...]
    inverses[...] = known[...]
    note(inverses, U1, u1)
    meet(best, inverses, ranks, U1, u1, [(O1, o1)])

    @pl.when(spots[0] != 0)
    def _():
        meet(best, inverses, ranks, U1, u1, [(E1, e1)])


def first_kernel(spots, ranks, u1, v1, e1, w1, before, known, best, inverses):
    best[...] = before[...]
    inverses[...] = known[...]
    note(inverses, V1, v1)
    note(inverses, W1, w1)

    @pl.when(spots[0] == 0)
    def _():
        meet(best, inverses, ranks, V1, v1, [(E1, e1)])

    @pl.when(spots[1] != 0)
    def _():
        meet(best, inverses, ranks, V1, v1, [(U1, u1)])

    @pl.when(spots[1] == 0)
    def _():
        meet(best, inverses, ranks, W1, w1, [(U1, u1)])


def second_kernel(spots, ranks, o1, o2, u1, v1, e1, e2, before, known, best, inverses):
    best[...] = before[...]
    inverses[...] = known[...]
    note(inverses, O2, o2)
    note(inverses, E2, e2)
    meet(best, inverses, ranks, O2, o2, [(O1, o1), (O2, o2), (U1, u1), (V1, v1)])
    meet(best, inverses, ranks, E2, e2, [(O1, o1), (U1, u1), (V1, v1)])

    @pl.when(spots[0] != 0)
    def _():
        meet(best, inverses, ranks, O2, o2, [(E2, e2)])


def give(best, name, out):
    for y in range(Y):
        at = pl.ds(y, 1)
        out[at, pl.ds(0, PARTS[0])] = best[pl.ds(name, 1), pl.ds(y * PARTS[0], PARTS[0])]
        pair = best[pl.ds(name + 1, 1), pl.ds(y // 2 * 128, 128)]
        pair = pltpu.roll(pair, 64, 1) if y % 2 else pair
        out[at, pl.ds(PARTS[0], PARTS[1])] = pair[:, : PARTS[1]]


def third_kernel(spots, ranks, o2, u2, e2, v1, w1, before, known, best, inverses):
    best[...] = before[...]
    inverses[...] = known[...]
    note(inverses, U2, u2)
    meet(best, inverses, ranks, U2, u2, [(O2, o2)])

    @pl.when(spots[0] != 0)
    def _():
        meet(best, inverses, ranks, U2, u2, [(E2, e2)])

    @pl.when(spots[1] != 0)
    def _():
        meet(best, inverses, ranks, U2, u2, [(V1, v1)])

    @pl.when(spots[1] == 0)
    def _():
        meet(best, inverses, ranks, U2, u2, [(W1, w1)])


def fourth_kernel(
    spots, ranks, u1, u2, v2, e2, w2, before, known, o_best, u_best, v_best, e_best, w_best,
    best, inverses,
):
    best[...] = before[...]
    inverses[...] = known[...]
    note(inverses, V2, v2)

    @pl.when(spots[0] == 0)
    def _():
        meet(best, inverses, ranks, V2, v2, [(E2, e2)])

    @pl.when(spots[1] != 0)
    def _():
        meet(best, inverses, ranks, V2, v2, [(U1, u1), (U2, u2)])

    @pl.when(spots[1] == 0)
    def _():
        note(inverses, W2, w2)
        meet(best, inverses, ranks, W2, w2, [(U1, u1), (U2, u2)])

    give(best, O1, o_best)
    give(best, U1, u_best)
    give(best, V1, v_best)
    give(best, E1, e_best)
    give(best, W1, w_best)


def is_dims(item):
    return isinstance(item, tuple) and isinstance(item[0], int)


def scores_call(kernel, units, inputs, out, scratch, name):
    return pl.pallas_call(
        kernel,
        out_shape=jax.tree.map(lambda dims: jax.ShapeDtypeStruct(dims, jnp.float32), out, is_leaf=is_dims),
        in_specs=[SMEM] + [VMEM] * (len(inputs) - 1),
        out_specs=jax.tree.map(lambda _: VMEM, out, is_leaf=is_dims),
        scratch_shapes=scratch,
        compiler_params=PARAMS,
        cost_estimate=pl.CostEstimate(
            flops=int(units * 2 * 256 * 256 * 1024), bytes_accessed=4 * 2**20, transcendentals=0
        ),
        name=name,
    )(*inputs)


def answer_kernel(ids_ref, slot_ref, table_ref, out_ref):
    table = table_ref[...]
    high = table.astype(jnp.bfloat16)
    rest = table - high.astype(jnp.float32)
    middle = rest.astype(jnp.bfloat16)
    small = (rest - middle.astype(jnp.float32)).astype(jnp.bfloat16)
    pieces = jnp.concatenate([high, middle, small], axis=0)
    group = lax.broadcasted_iota(jnp.int32, (3 * GROUPS, 128), 0) & (GROUPS - 1)
    place_in = lax.broadcasted_iota(jnp.int32, (CAP, 128), 0)
    for i in range(LINES):
        ids = ids_ref[pl.ds(i, 1), :]
        within = slot_ref[pl.ds(i, 1), :] - ids * CAP
        member = (group == ids).astype(jnp.float32).astype(jnp.bfloat16)
        found = lax.dot_general(
            pieces, member, (((0,), (0,)), ((), ())), preferred_element_type=jnp.float32
        )
        out_ref[pl.ds(i, 1), :] = jnp.sum(
            jnp.where(place_in == within, found, 0.0), axis=0, keepdims=True
        )


def answer(ids, slots, table):
    return pl.pallas_call(
        answer_kernel,
        out_shape=jax.ShapeDtypeStruct((LINES, 128), jnp.float32),
        in_specs=[VMEM] * 3,
        out_specs=VMEM,
        compiler_params=PARAMS,
        name="answer",
    )(ids, slots, table)


def shards(embeds, cluster_ids, orders):
    y, x, core, z = (lax.axis_index(name) for name in ALL)
    swap = routes(lambda y, x, c, z: (y, x, 1 - c, z))
    ahead = routes(lambda y, x, c, z: (y, x + 1 - 2 * c, c, z))
    behind = routes(lambda y, x, c, z: (y, x - 1 + 2 * c, c, z))

    def bring(rows):
        part = rows.shape[0] // GROUPS
        return lax.all_to_all(
            rows.reshape(GROUPS, part, WIDTH), ("y", "z"), split_axis=0, concat_axis=0, tiled=True
        ).reshape(GROUPS * part, WIDTH)

    ids = cluster_ids.reshape(LINES, 128)
    placed1, slots = place(ids, embeds)
    o1 = bring(placed1)
    placed2 = place_rest(ids, slots, embeds)

    table = ranks(ids, slots, orders.reshape(LINES, 128)).reshape(Y, Z, CAP)
    table = lax.dynamic_index_in_dim(table, z, 1, keepdims=False)
    rank_parts = []
    for j in range(Y):
        row = lax.dynamic_slice_in_dim(table, (y + j) % Y, 1, 0)
        if j:
            row = lax.ppermute(row, ALL, routes(lambda y, x, c, z: (y + j, x, c, z)))
        rank_parts.append(row)
    own_ranks = jnp.concatenate(rank_parts)[(y - jnp.arange(Y)) % Y]
    own_ranks = jnp.where(own_ranks > 0, own_ranks, never_order)
    own_ranks = jnp.stack(
        [
            own_ranks[:, : PARTS[0]].reshape(SIZES[0]),
            jnp.pad(own_ranks[:, PARTS[0] :].reshape(SIZES[1]), (0, SIZES[0] - SIZES[1])),
        ]
    )
    near_ranks = lax.ppermute(own_ranks, ALL, ahead)
    member_ranks = jnp.concatenate(
        [
            own_ranks,
            near_ranks,
            lax.ppermute(own_ranks, ALL, behind),
            lax.ppermute(own_ranks, ALL, swap),
            lax.ppermute(near_ranks, ALL, swap),
            jnp.zeros((6, SIZES[0]), jnp.float32),
        ]
    )
    spots = jnp.stack([core, ((x < X // 2) == (core == 0)).astype(jnp.int32)]).astype(jnp.int32)
    o1, placed2, member_ranks, spots = lax.optimization_barrier((o1, placed2, member_ranks, spots))
    o2 = bring(placed2)

    wide = (16, SIZES[0])

    def score(kernel, units, blocks, state, name, out=(wide, wide), scratch=()):
        inputs = (spots, member_ranks, *blocks, *state)
        return scores_call(kernel, units, inputs, list(out), list(scratch), name)

    u1 = lax.ppermute(o1, ALL, ahead)
    e1 = lax.ppermute(o1, ALL, swap)
    state = score(own_kernel, 8, (o1, e1), (), "own")
    o1, *state = lax.optimization_barrier((o1, *state))
    v1 = lax.ppermute(o1, ALL, behind)
    w1 = lax.ppermute(u1, ALL, swap)
    state = score(near_kernel, 6, (o1, u1, e1), state, "near")
    o2, *state = lax.optimization_barrier((o2, *state))

    u2 = lax.ppermute(o2, ALL, ahead)
    e2 = lax.ppermute(o2, ALL, swap)
    state = score(first_kernel, 6, (u1, v1, e1, w1), state, "first")
    o2, *state = lax.optimization_barrier((o2, *state))
    v2 = lax.ppermute(o2, ALL, behind)
    state = score(second_kernel, 14, (o1, o2, u1, v1, e1, e2), state, "second")
    u2, *state = lax.optimization_barrier((u2, *state))
    w2 = lax.ppermute(u2, ALL, swap)
    state = score(third_kernel, 4, (o2, u2, e2, v1, w1), state, "third")
    v2, *state = lax.optimization_barrier((v2, *state))
    own, *others = score(
        fourth_kernel, 4, (u1, u2, v2, e2, w2), state, "fourth", [(Y, CAP)] * 5,
        [pltpu.VMEM(wide, jnp.float32)] * 2,
    )

    across = routes(lambda y, x, c, z: (y, x + 1 - 2 * c, 1 - c, z))
    for part, way in zip(others, (behind, ahead, swap, across)):
        own = jnp.maximum(own, lax.ppermute(part, ALL, way))
    table = lax.all_to_all(
        jnp.broadcast_to(own[:, None], (Y, Z, CAP)).reshape(GROUPS, CAP),
        ("y", "z"), split_axis=0, concat_axis=0, tiled=True,
    )
    return answer(ids, slots, table).reshape(ROWS)


def solution(mesh):
    fine = Mesh(mesh.devices.reshape(Y, X, C, Z), ALL)
    clus = ("y", "x", "core")
    return jax.shard_map(
        shards,
        mesh=fine,
        in_specs=(P(clus, "z"), P(clus), P(clus)),
        out_specs=P(clus),
        check_vma=False,
    )
```

```python
import functools

import jax
import jax.numpy as jnp
from jax import lax
from jax.experimental import pallas as pl
from jax.experimental.pallas import tpu as pltpu
from jax.sharding import Mesh, PartitionSpec as P

never_order = 2.0**30
low = -3e38
Y, X, C, Z = 4, 4, 2, 8
ROWS = 3072
GROUPS = 32
CAP = 192
WIDTH = 128
PARTS = (128, 64)
SIZES = (Y * 128, Y * 64)
LINES = ROWS // 128
ALL = ("y", "x", "core", "z")
PARAMS = pltpu.CompilerParams(vmem_limit_bytes=40 * 2**20)
VMEM = pl.BlockSpec(memory_space=pltpu.VMEM)
SMEM = pl.BlockSpec(memory_space=pltpu.SMEM)


def routes(move):
    pairs = []
    for y in range(Y):
        for x in range(X):
            for c in range(C):
                for z in range(Z):
                    y2, x2, c2, z2 = move(y, x, c, z)
                    to = (((y2 % Y) * X + x2 % X) * C + c2 % C) * Z + z2 % Z
                    pairs.append((((y * X + x) * C + c) * Z + z, to))
    return pairs


def scatter_rows(spot_sm, wide_ref, out_ref):
    @pl.loop(0, LINES)
    def _(i):
        for lane in range(128):
            spot = spot_sm[i, lane]
            out_ref[pl.ds(spot, 1), :] = wide_ref[pl.ds(i * 128 + lane, 1), :]


def place_kernel(
    ids_any, rows_any, placed_ref, slot_ref,
    ids_ref, rows_ref, member_ref, wide_ref, out_ref, spot_ref, spot_sm, sems,
):
    ids_copy = pltpu.make_async_copy(ids_any, ids_ref, sems.at[0])
    rows_copy = pltpu.make_async_copy(rows_any, rows_ref, sems.at[1])
    ids_copy.start()
    rows_copy.start()
    out_ref[...] = jnp.zeros_like(out_ref)
    r = lax.broadcasted_iota(jnp.int32, (128, 256), 0)
    c = lax.broadcasted_iota(jnp.int32, (128, 256), 1)
    weights = ((r < c) | (c >= 128)).astype(jnp.float32).astype(jnp.bfloat16)
    group = lax.broadcasted_iota(jnp.int32, (GROUPS, 128), 0)
    ids_copy.wait()
    for i in range(LINES):
        hit = group == ids_ref[pl.ds(i, 1), :]
        member_ref[pl.ds(i * GROUPS, GROUPS), :] = hit.astype(jnp.float32).astype(jnp.bfloat16)
    counts = jnp.dot(member_ref[...], weights, preferred_element_type=jnp.float32)
    carry = jnp.zeros((GROUPS, 128), jnp.float32)
    for i in range(LINES):
        part = counts[i * GROUPS : (i + 1) * GROUPS]
        line = ids_ref[pl.ds(i, 1), :]
        within = jnp.sum(jnp.where(group == line, part[:, :128] + carry, 0.0), axis=0, keepdims=True)
        within = within.astype(jnp.int32)
        slot_ref[pl.ds(i, 1), :] = line * CAP + within
        spot_ref[pl.ds(i, 1), :] = jnp.where(
            within < PARTS[0], line * PARTS[0] + within, GROUPS * PARTS[0]
        )
        carry = carry + part[:, 128:]
    copy = pltpu.make_async_copy(spot_ref, spot_sm, sems.at[2])
    copy.start()
    rows_copy.wait()
    wide_ref[...] = rows_ref[...].astype(jnp.float32)
    copy.wait()
    scatter_rows(spot_sm, wide_ref, out_ref)
    placed_ref[...] = out_ref[pl.ds(0, GROUPS * PARTS[0]), :].astype(jnp.bfloat16)


def place(ids, rows):
    return pl.pallas_call(
        place_kernel,
        out_shape=(
            jax.ShapeDtypeStruct((GROUPS * PARTS[0], WIDTH), jnp.bfloat16),
            jax.ShapeDtypeStruct((LINES, 128), jnp.int32),
        ),
        in_specs=[pl.BlockSpec(memory_space=pltpu.HBM)] * 2,
        out_specs=(VMEM, VMEM),
        scratch_shapes=[
            pltpu.VMEM((LINES, 128), jnp.int32),
            pltpu.VMEM((ROWS, WIDTH), jnp.bfloat16),
            pltpu.VMEM((LINES * GROUPS, 128), jnp.bfloat16),
            pltpu.VMEM((ROWS, WIDTH), jnp.float32),
            pltpu.VMEM((GROUPS * PARTS[0] + 8, WIDTH), jnp.float32),
            pltpu.VMEM((LINES, 128), jnp.int32),
            pltpu.SMEM((LINES, 128), jnp.int32),
            pltpu.SemaphoreType.DMA((3,)),
        ],
        compiler_params=pltpu.CompilerParams(vmem_limit_bytes=60 * 2**20),
        name="place",
    )(ids, rows)


def place_rest_kernel(
    ids_ref, slot_ref, rows_ref, placed_ref, wide_ref, out_ref, spot_ref, spot_sm, sem
):
    ids = ids_ref[...]
    within = slot_ref[...] - ids * CAP
    spot_ref[...] = jnp.where(
        within < PARTS[0], GROUPS * PARTS[1], ids * PARTS[1] + within - PARTS[0]
    )
    copy = pltpu.make_async_copy(spot_ref, spot_sm, sem)
    copy.start()
    out_ref[...] = jnp.zeros_like(out_ref)
    wide_ref[...] = rows_ref[...].astype(jnp.float32)
    copy.wait()
    scatter_rows(spot_sm, wide_ref, out_ref)
    placed_ref[...] = out_ref[pl.ds(0, GROUPS * PARTS[1]), :].astype(jnp.bfloat16)


def place_rest(ids, slots, rows):
    return pl.pallas_call(
        place_rest_kernel,
        out_shape=jax.ShapeDtypeStruct((GROUPS * PARTS[1], WIDTH), jnp.bfloat16),
        in_specs=[VMEM] * 3,
        out_specs=VMEM,
        scratch_shapes=[
            pltpu.VMEM((ROWS, WIDTH), jnp.float32),
            pltpu.VMEM((GROUPS * PARTS[1] + 8, WIDTH), jnp.float32),
            pltpu.VMEM((LINES, 128), jnp.int32),
            pltpu.SMEM((LINES, 128), jnp.int32),
            pltpu.SemaphoreType.DMA,
        ],
        compiler_params=PARAMS,
        name="place_rest",
    )(ids, slots, rows)


def ranks_kernel(ids_ref, slot_ref, orders_ref, table_ref):
    group = lax.broadcasted_iota(jnp.int32, (GROUPS, 128), 0)
    spot = lax.broadcasted_iota(jnp.int32, (CAP, 128), 0)
    total = jnp.zeros((3 * GROUPS, CAP), jnp.float32)
    for i in range(LINES):
        ids = ids_ref[pl.ds(i, 1), :]
        within = slot_ref[pl.ds(i, 1), :] - ids * CAP
        value = orders_ref[pl.ds(i, 1), :] + 1
        hit = group == ids
        digits = [
            jnp.where(hit, digit.astype(jnp.float32), 0.0)
            for digit in (value & 255, (value >> 8) & 255, value >> 16)
        ]
        left = jnp.concatenate(digits, axis=0).astype(jnp.bfloat16)
        right = (spot == within).astype(jnp.float32).astype(jnp.bfloat16)
        total = total + dot_rows(left, right)
    value = total[:GROUPS] + 256.0 * total[GROUPS : 2 * GROUPS] + 65536.0 * total[2 * GROUPS :]
    table_ref[...] = value


def ranks(ids, slots, orders):
    return pl.pallas_call(
        ranks_kernel,
        out_shape=jax.ShapeDtypeStruct((GROUPS, CAP), jnp.float32),
        in_specs=[VMEM] * 3,
        out_specs=VMEM,
        compiler_params=PARAMS,
        name="ranks",
    )(ids, slots, orders)


def dot_rows(p, q):
    return lax.dot_general(p, q, (((1,), (1,)), ((), ())), preferred_element_type=jnp.float32)


def eye():
    r = lax.broadcasted_iota(jnp.int32, (128, 128), 0)
    return r == lax.broadcasted_iota(jnp.int32, (128, 128), 1)


def to_row(col):
    pieces = []
    for i in range(col.shape[0] // 128):
        piece = jnp.broadcast_to(col[i * 128 : (i + 1) * 128], (128, 128))
        pieces.append(jnp.max(jnp.where(eye(), piece, low), axis=0, keepdims=True))
    return jnp.concatenate(pieces, axis=1)


def to_col(row):
    pieces = []
    for i in range(row.shape[1] // 128):
        piece = jnp.broadcast_to(row[:, i * 128 : (i + 1) * 128], (128, 128))
        pieces.append(jnp.max(jnp.where(eye(), piece, low), axis=1, keepdims=True))
    return jnp.concatenate(pieces, axis=0)


def part_of(ref):
    return ref.shape[0] // GROUPS


def size_of(ref):
    return Y * part_of(ref)


def rows_of(ref, start, count):
    part = part_of(ref)
    lines = []
    for y in range(start // part, (start + count) // part):
        pieces = [ref[pl.ds((y * Z + z) * part, part), :] for z in range(Z)]
        lines.append(jnp.concatenate(pieces, axis=1))
    return jnp.concatenate(lines, axis=0)


def note(inverses, name, ref):
    part = part_of(ref)
    cols = []
    for y in range(Y):
        total = jnp.zeros((part, WIDTH), jnp.float32)
        for z in range(Z):
            wide = ref[pl.ds((y * Z + z) * part, part), :].astype(jnp.float32)
            total = total + wide * wide
        cols.append(lax.rsqrt(jnp.sum(total, axis=1, keepdims=True) + 1e-06))
    inverses[pl.ds(name, 1), pl.ds(0, Y * part)] = to_row(jnp.concatenate(cols, axis=0))


def meet(best, inverses, ranks, ps, others):
    sizes = [size_of(ref) for _, ref in ps]
    inv_p, rank_p = (
        jnp.concatenate(
            [to_col(rows[pl.ds(name, 1), pl.ds(0, size)]) for (name, _), size in zip(ps, sizes)]
        )
        for rows in (inverses, ranks)
    )
    p_best = jnp.full((sum(sizes), 128), low, jnp.float32)
    for q_name, q_ref in others:
        q_best = []
        for j in range(0, size_of(q_ref), 256):
            at = (pl.ds(q_name, 1), pl.ds(j, 256))
            p = jnp.concatenate([rows_of(ref, 0, size) for (_, ref), size in zip(ps, sizes)])
            s = dot_rows(p, rows_of(q_ref, j, 256))
            s = s * inv_p * inverses[at]
            earlier = ranks[at] < rank_p
            mine = jnp.where(earlier, s, low)
            p_best = jnp.maximum(p_best, jnp.maximum(mine[:, :128], mine[:, 128:]))
            if q_name != ps[0][0]:
                q_best.append(jnp.max(jnp.where(earlier, low, s), axis=0, keepdims=True))
        if q_best:
            record(best, q_name, jnp.concatenate(q_best, axis=1))
    start = 0
    for (name, _), size in zip(ps, sizes):
        record(best, name, to_row(jnp.max(p_best[start : start + size], axis=1, keepdims=True)))
        start += size


def by_place(spots, run):
    for core in range(2):
        for side in range(2):

            @pl.when((spots[0] == core) & (spots[1] == side))
            def _():
                run(core, side)


def record(best, name, row):
    at = (pl.ds(name, 1), pl.ds(0, row.shape[1]))
    best[at] = jnp.maximum(best[at], row)


O1, O2, U1, U2, V1, V2, E1, E2, W1, W2 = range(10)


def own_kernel(spots, ranks, o1, e1, best, inverses):
    best[...] = jnp.full_like(best, -1.0)
    inverses[...] = jnp.zeros_like(inverses)
    note(inverses, O1, o1)
    note(inverses, E1, e1)

    @pl.when(spots[0] == 0)
    def _():
        meet(best, inverses, ranks, [(O1, o1)], [(O1, o1), (E1, e1)])

    @pl.when(spots[0] != 0)
    def _():
        meet(best, inverses, ranks, [(O1, o1)], [(O1, o1)])


def near_kernel(spots, ranks, o1, u1, e1, before, known, best, inverses):
    best[...] = before[...]
    inverses[...] = known[...]
    note(inverses, U1, u1)

    @pl.when(spots[0] == 0)
    def _():
        meet(best, inverses, ranks, [(U1, u1)], [(O1, o1)])

    @pl.when(spots[0] != 0)
    def _():
        meet(best, inverses, ranks, [(U1, u1)], [(O1, o1), (E1, e1)])


def second_kernel(spots, ranks, o1, o2, u1, v1, e1, e2, w1, before, known, best, inverses):
    best[...] = before[...]
    inverses[...] = known[...]
    note(inverses, V1, v1)
    note(inverses, W1, w1)
    note(inverses, O2, o2)
    note(inverses, E2, e2)
    meet(best, inverses, ranks, [(O2, o2), (E2, e2)], [(O1, o1), (U1, u1), (V1, v1)])

    def run(core, side):
        meet(best, inverses, ranks, [(O2, o2)], [(O2, o2)] + [(E2, e2)] * core)
        if side:
            meet(best, inverses, ranks, [(V1, v1)], [(E1, e1)] * (1 - core) + [(U1, u1)])
        else:
            if core == 0:
                meet(best, inverses, ranks, [(V1, v1)], [(E1, e1)])
            meet(best, inverses, ranks, [(W1, w1)], [(U1, u1)])

    by_place(spots, run)


def third_kernel(spots, ranks, o2, u2, e2, v1, w1, before, known, best, inverses):
    best[...] = before[...]
    inverses[...] = known[...]
    note(inverses, U2, u2)

    def run(core, side):
        others = [(O2, o2), (V1, v1) if side else (W1, w1)] + [(E2, e2)] * core
        meet(best, inverses, ranks, [(U2, u2)], others)

    by_place(spots, run)


def give(best, name, out):
    for y in range(Y):
        at = pl.ds(y, 1)
        out[at, pl.ds(0, PARTS[0])] = best[pl.ds(name, 1), pl.ds(y * PARTS[0], PARTS[0])]
        pair = best[pl.ds(name + 1, 1), pl.ds(y // 2 * 128, 128)]
        pair = pltpu.roll(pair, 64, 1) if y % 2 else pair
        out[at, pl.ds(PARTS[0], PARTS[1])] = pair[:, : PARTS[1]]


def fourth_kernel(
    spots, ranks, u1, u2, v2, e2, w2, before, known, o_best, u_best, v_best, e_best, w_best,
    best, inverses,
):
    best[...] = before[...]
    inverses[...] = known[...]
    note(inverses, V2, v2)

    def run(core, side):
        if side:
            others = [(E2, e2)] * (1 - core) + [(U1, u1), (U2, u2)]
            meet(best, inverses, ranks, [(V2, v2)], others)
        else:
            note(inverses, W2, w2)
            if core == 0:
                meet(best, inverses, ranks, [(V2, v2)], [(E2, e2)])
            meet(best, inverses, ranks, [(W2, w2)], [(U1, u1), (U2, u2)])

    by_place(spots, run)

    give(best, O1, o_best)
    give(best, U1, u_best)
    give(best, V1, v_best)
    give(best, E1, e_best)
    give(best, W1, w_best)


def is_dims(item):
    return isinstance(item, tuple) and isinstance(item[0], int)


def scores_call(kernel, units, inputs, out, scratch, name):
    return pl.pallas_call(
        kernel,
        out_shape=jax.tree.map(lambda dims: jax.ShapeDtypeStruct(dims, jnp.float32), out, is_leaf=is_dims),
        in_specs=[SMEM] + [VMEM] * (len(inputs) - 1),
        out_specs=jax.tree.map(lambda _: VMEM, out, is_leaf=is_dims),
        scratch_shapes=scratch,
        compiler_params=PARAMS,
        cost_estimate=pl.CostEstimate(
            flops=int(units * 2 * 256 * 256 * 1024), bytes_accessed=4 * 2**20, transcendentals=0
        ),
        name=name,
    )(*inputs)


def answer_kernel(ids_ref, slot_ref, table_ref, out_ref):
    table = table_ref[...]
    high = table.astype(jnp.bfloat16)
    rest = table - high.astype(jnp.float32)
    middle = rest.astype(jnp.bfloat16)
    small = (rest - middle.astype(jnp.float32)).astype(jnp.bfloat16)
    pieces = jnp.concatenate([high, middle, small], axis=0)
    group = lax.broadcasted_iota(jnp.int32, (3 * GROUPS, 128), 0) & (GROUPS - 1)
    place_in = lax.broadcasted_iota(jnp.int32, (CAP, 128), 0)
    for i in range(LINES):
        ids = ids_ref[pl.ds(i, 1), :]
        within = slot_ref[pl.ds(i, 1), :] - ids * CAP
        member = (group == ids).astype(jnp.float32).astype(jnp.bfloat16)
        found = lax.dot_general(
            pieces, member, (((0,), (0,)), ((), ())), preferred_element_type=jnp.float32
        )
        out_ref[pl.ds(i, 1), :] = jnp.sum(
            jnp.where(place_in == within, found, 0.0), axis=0, keepdims=True
        )


def answer(ids, slots, table):
    return pl.pallas_call(
        answer_kernel,
        out_shape=jax.ShapeDtypeStruct((LINES, 128), jnp.float32),
        in_specs=[VMEM] * 3,
        out_specs=VMEM,
        compiler_params=PARAMS,
        name="answer",
    )(ids, slots, table)


def shards(embeds, cluster_ids, orders):
    y, x, core, z = (lax.axis_index(name) for name in ALL)
    swap = routes(lambda y, x, c, z: (y, x, 1 - c, z))
    ahead = routes(lambda y, x, c, z: (y, x + 1 - 2 * c, c, z))
    behind = routes(lambda y, x, c, z: (y, x - 1 + 2 * c, c, z))

    def bring(rows):
        part = rows.shape[0] // GROUPS
        return lax.all_to_all(
            rows.reshape(GROUPS, part, WIDTH), ("y", "z"), split_axis=0, concat_axis=0, tiled=True
        ).reshape(GROUPS * part, WIDTH)

    ids = cluster_ids.reshape(LINES, 128)
    placed1, slots = place(ids, embeds)
    o1 = bring(placed1)
    placed2 = place_rest(ids, slots, embeds)

    table = ranks(ids, slots, orders.reshape(LINES, 128)).reshape(Y, Z, CAP)
    table = lax.dynamic_index_in_dim(table, z, 1, keepdims=False)
    rank_parts = []
    for j in range(Y):
        row = lax.dynamic_slice_in_dim(table, (y + j) % Y, 1, 0)
        if j:
            row = lax.ppermute(row, ALL, routes(lambda y, x, c, z: (y + j, x, c, z)))
        rank_parts.append(row)
    own_ranks = jnp.concatenate(rank_parts)[(y - jnp.arange(Y)) % Y]
    own_ranks = jnp.where(own_ranks > 0, own_ranks, never_order)
    own_ranks = jnp.stack(
        [
            own_ranks[:, : PARTS[0]].reshape(SIZES[0]),
            jnp.pad(own_ranks[:, PARTS[0] :].reshape(SIZES[1]), (0, SIZES[0] - SIZES[1])),
        ]
    )
    near_ranks = lax.ppermute(own_ranks, ALL, ahead)
    member_ranks = jnp.concatenate(
        [
            own_ranks,
            near_ranks,
            lax.ppermute(own_ranks, ALL, behind),
            lax.ppermute(own_ranks, ALL, swap),
            lax.ppermute(near_ranks, ALL, swap),
            jnp.zeros((6, SIZES[0]), jnp.float32),
        ]
    )
    spots = jnp.stack([core, ((x < X // 2) == (core == 0)).astype(jnp.int32)]).astype(jnp.int32)
    o1, placed2, member_ranks, spots = lax.optimization_barrier((o1, placed2, member_ranks, spots))
    o2 = bring(placed2)

    wide = (16, SIZES[0])

    def score(kernel, units, blocks, state, name, out=(wide, wide), scratch=()):
        inputs = (spots, member_ranks, *blocks, *state)
        return scores_call(kernel, units, inputs, list(out), list(scratch), name)

    u1 = lax.ppermute(o1, ALL, ahead)
    v1 = lax.ppermute(o1, ALL, behind)
    e1 = lax.ppermute(o1, ALL, swap)
    state = score(own_kernel, 8, (o1, e1), (), "own")
    u1, *state = lax.optimization_barrier((u1, *state))
    w1 = lax.ppermute(u1, ALL, swap)
    o2, *state = lax.optimization_barrier((o2, *state))

    u2 = lax.ppermute(o2, ALL, ahead)
    e2 = lax.ppermute(o2, ALL, swap)
    state = score(near_kernel, 6, (o1, u1, e1), state, "near")
    o2, *state = lax.optimization_barrier((o2, *state))
    v2 = lax.ppermute(o2, ALL, behind)
    state = score(second_kernel, 20, (o1, o2, u1, v1, e1, e2, w1), state, "second")
    u2, *state = lax.optimization_barrier((u2, *state))
    w2 = lax.ppermute(u2, ALL, swap)
    state = score(third_kernel, 4, (o2, u2, e2, v1, w1), state, "third")
    v2, *state = lax.optimization_barrier((v2, *state))
    own, *others = score(
        fourth_kernel, 4, (u1, u2, v2, e2, w2), state, "fourth", [(Y, CAP)] * 5,
        [pltpu.VMEM(wide, jnp.float32)] * 2,
    )

    across = routes(lambda y, x, c, z: (y, x + 1 - 2 * c, 1 - c, z))
    for part, way in zip(others, (behind, ahead, swap, across)):
        own = jnp.maximum(own, lax.ppermute(part, ALL, way))
    table = lax.all_to_all(
        jnp.broadcast_to(own[:, None], (Y, Z, CAP)).reshape(GROUPS, CAP),
        ("y", "z"), split_axis=0, concat_axis=0, tiled=True,
    )
    return answer(ids, slots, table).reshape(ROWS)


def solution(mesh):
    fine = Mesh(mesh.devices.reshape(Y, X, C, Z), ALL)
    clus = ("y", "x", "core")
    return jax.shard_map(
        shards,
        mesh=fine,
        in_specs=(P(clus, "z"), P(clus), P(clus)),
        out_specs=P(clus),
        check_vma=False,
    )
```

```python
import functools

import jax
import jax.numpy as jnp
from jax import lax
from jax.experimental import pallas as pl
from jax.experimental.pallas import tpu as pltpu
from jax.sharding import Mesh, PartitionSpec as P

never_order = 2.0**30
low = -3e38
Y, X, C, Z = 4, 4, 2, 8
ROWS = 3072
GROUPS = 32
CAP = 192
WIDTH = 128
PARTS = (128, 64)
SIZES = (Y * 128, Y * 64)
LINES = ROWS // 128
ALL = ("y", "x", "core", "z")
PARAMS = pltpu.CompilerParams(vmem_limit_bytes=40 * 2**20)
VMEM = pl.BlockSpec(memory_space=pltpu.VMEM)
SMEM = pl.BlockSpec(memory_space=pltpu.SMEM)


def routes(move):
    pairs = []
    for y in range(Y):
        for x in range(X):
            for c in range(C):
                for z in range(Z):
                    y2, x2, c2, z2 = move(y, x, c, z)
                    to = (((y2 % Y) * X + x2 % X) * C + c2 % C) * Z + z2 % Z
                    pairs.append((((y * X + x) * C + c) * Z + z, to))
    return pairs


def scatter_rows(spot_sm, wide_ref, out_ref):
    @pl.loop(0, LINES)
    def _(i):
        for lane in range(128):
            spot = spot_sm[i, lane]
            out_ref[pl.ds(spot, 1), :] = wide_ref[pl.ds(i * 128 + lane, 1), :]


def place_kernel(
    ids_any, rows_any, placed_ref, slot_ref,
    ids_ref, rows_ref, member_ref, wide_ref, out_ref, spot_ref, spot_sm, sems,
):
    ids_copy = pltpu.make_async_copy(ids_any, ids_ref, sems.at[0])
    rows_copy = pltpu.make_async_copy(rows_any, rows_ref, sems.at[1])
    ids_copy.start()
    rows_copy.start()
    out_ref[...] = jnp.zeros_like(out_ref)
    r = lax.broadcasted_iota(jnp.int32, (128, 256), 0)
    c = lax.broadcasted_iota(jnp.int32, (128, 256), 1)
    weights = ((r < c) | (c >= 128)).astype(jnp.float32).astype(jnp.bfloat16)
    group = lax.broadcasted_iota(jnp.int32, (GROUPS, 128), 0)
    ids_copy.wait()
    for i in range(LINES):
        hit = group == ids_ref[pl.ds(i, 1), :]
        member_ref[pl.ds(i * GROUPS, GROUPS), :] = hit.astype(jnp.float32).astype(jnp.bfloat16)
    counts = jnp.dot(member_ref[...], weights, preferred_element_type=jnp.float32)
    carry = jnp.zeros((GROUPS, 128), jnp.float32)
    for i in range(LINES):
        part = counts[i * GROUPS : (i + 1) * GROUPS]
        line = ids_ref[pl.ds(i, 1), :]
        within = jnp.sum(jnp.where(group == line, part[:, :128] + carry, 0.0), axis=0, keepdims=True)
        within = within.astype(jnp.int32)
        slot_ref[pl.ds(i, 1), :] = line * CAP + within
        spot_ref[pl.ds(i, 1), :] = jnp.where(
            within < PARTS[0], line * PARTS[0] + within, GROUPS * PARTS[0]
        )
        carry = carry + part[:, 128:]
    copy = pltpu.make_async_copy(spot_ref, spot_sm, sems.at[2])
    copy.start()
    rows_copy.wait()
    wide_ref[...] = rows_ref[...].astype(jnp.float32)
    copy.wait()
    scatter_rows(spot_sm, wide_ref, out_ref)
    placed_ref[...] = out_ref[pl.ds(0, GROUPS * PARTS[0]), :].astype(jnp.bfloat16)


def place(ids, rows):
    return pl.pallas_call(
        place_kernel,
        out_shape=(
            jax.ShapeDtypeStruct((GROUPS * PARTS[0], WIDTH), jnp.bfloat16),
            jax.ShapeDtypeStruct((LINES, 128), jnp.int32),
        ),
        in_specs=[pl.BlockSpec(memory_space=pltpu.HBM)] * 2,
        out_specs=(VMEM, VMEM),
        scratch_shapes=[
            pltpu.VMEM((LINES, 128), jnp.int32),
            pltpu.VMEM((ROWS, WIDTH), jnp.bfloat16),
            pltpu.VMEM((LINES * GROUPS, 128), jnp.bfloat16),
            pltpu.VMEM((ROWS, WIDTH), jnp.float32),
            pltpu.VMEM((GROUPS * PARTS[0] + 8, WIDTH), jnp.float32),
            pltpu.VMEM((LINES, 128), jnp.int32),
            pltpu.SMEM((LINES, 128), jnp.int32),
            pltpu.SemaphoreType.DMA((3,)),
        ],
        compiler_params=pltpu.CompilerParams(vmem_limit_bytes=60 * 2**20),
        name="place",
    )(ids, rows)


def place_rest_kernel(
    ids_ref, slot_ref, rows_ref, placed_ref, wide_ref, out_ref, spot_ref, spot_sm, sem
):
    ids = ids_ref[...]
    within = slot_ref[...] - ids * CAP
    spot_ref[...] = jnp.where(
        within < PARTS[0], GROUPS * PARTS[1], ids * PARTS[1] + within - PARTS[0]
    )
    copy = pltpu.make_async_copy(spot_ref, spot_sm, sem)
    copy.start()
    out_ref[...] = jnp.zeros_like(out_ref)
    wide_ref[...] = rows_ref[...].astype(jnp.float32)
    copy.wait()
    scatter_rows(spot_sm, wide_ref, out_ref)
    placed_ref[...] = out_ref[pl.ds(0, GROUPS * PARTS[1]), :].astype(jnp.bfloat16)


def place_rest(ids, slots, rows):
    return pl.pallas_call(
        place_rest_kernel,
        out_shape=jax.ShapeDtypeStruct((GROUPS * PARTS[1], WIDTH), jnp.bfloat16),
        in_specs=[VMEM] * 3,
        out_specs=VMEM,
        scratch_shapes=[
            pltpu.VMEM((ROWS, WIDTH), jnp.float32),
            pltpu.VMEM((GROUPS * PARTS[1] + 8, WIDTH), jnp.float32),
            pltpu.VMEM((LINES, 128), jnp.int32),
            pltpu.SMEM((LINES, 128), jnp.int32),
            pltpu.SemaphoreType.DMA,
        ],
        compiler_params=PARAMS,
        name="place_rest",
    )(ids, slots, rows)


def ranks_kernel(ids_ref, slot_ref, orders_ref, table_ref):
    group = lax.broadcasted_iota(jnp.int32, (GROUPS, 128), 0)
    spot = lax.broadcasted_iota(jnp.int32, (CAP, 128), 0)
    total = jnp.zeros((3 * GROUPS, CAP), jnp.float32)
    for i in range(LINES):
        ids = ids_ref[pl.ds(i, 1), :]
        within = slot_ref[pl.ds(i, 1), :] - ids * CAP
        value = orders_ref[pl.ds(i, 1), :] + 1
        hit = group == ids
        digits = [
            jnp.where(hit, digit.astype(jnp.float32), 0.0)
            for digit in (value & 255, (value >> 8) & 255, value >> 16)
        ]
        left = jnp.concatenate(digits, axis=0).astype(jnp.bfloat16)
        right = (spot == within).astype(jnp.float32).astype(jnp.bfloat16)
        total = total + dot_rows(left, right)
    value = total[:GROUPS] + 256.0 * total[GROUPS : 2 * GROUPS] + 65536.0 * total[2 * GROUPS :]
    table_ref[...] = value


def ranks(ids, slots, orders):
    return pl.pallas_call(
        ranks_kernel,
        out_shape=jax.ShapeDtypeStruct((GROUPS, CAP), jnp.float32),
        in_specs=[VMEM] * 3,
        out_specs=VMEM,
        compiler_params=PARAMS,
        name="ranks",
    )(ids, slots, orders)


def dot_rows(p, q):
    return lax.dot_general(p, q, (((1,), (1,)), ((), ())), preferred_element_type=jnp.float32)


def eye():
    r = lax.broadcasted_iota(jnp.int32, (128, 128), 0)
    return r == lax.broadcasted_iota(jnp.int32, (128, 128), 1)


def to_row(col):
    pieces = []
    for i in range(col.shape[0] // 128):
        piece = jnp.broadcast_to(col[i * 128 : (i + 1) * 128], (128, 128))
        pieces.append(jnp.max(jnp.where(eye(), piece, low), axis=0, keepdims=True))
    return jnp.concatenate(pieces, axis=1)


def to_col(row):
    pieces = []
    for i in range(row.shape[1] // 128):
        piece = jnp.broadcast_to(row[:, i * 128 : (i + 1) * 128], (128, 128))
        pieces.append(jnp.max(jnp.where(eye(), piece, low), axis=1, keepdims=True))
    return jnp.concatenate(pieces, axis=0)


def part_of(ref):
    return ref.shape[0] // GROUPS


def size_of(ref):
    return Y * part_of(ref)


def rows_of(ref, start, count):
    part = part_of(ref)
    lines = []
    for y in range(start // part, (start + count) // part):
        pieces = [ref[pl.ds((y * Z + z) * part, part), :] for z in range(Z)]
        lines.append(jnp.concatenate(pieces, axis=1))
    return jnp.concatenate(lines, axis=0)


def note(inverses, name, ref):
    part = part_of(ref)
    cols = []
    for y in range(Y):
        total = jnp.zeros((part, WIDTH), jnp.float32)
        for z in range(Z):
            wide = ref[pl.ds((y * Z + z) * part, part), :].astype(jnp.float32)
            total = total + wide * wide
        cols.append(lax.rsqrt(jnp.sum(total, axis=1, keepdims=True) + 1e-06))
    inverses[pl.ds(name, 1), pl.ds(0, Y * part)] = to_row(jnp.concatenate(cols, axis=0))


def meet(best, inverses, ranks, ps, others):
    sizes = [size_of(ref) for _, ref in ps]
    inv_p, rank_p = (
        jnp.concatenate(
            [to_col(rows[pl.ds(name, 1), pl.ds(0, size)]) for (name, _), size in zip(ps, sizes)]
        )
        for rows in (inverses, ranks)
    )
    p_best = jnp.full((sum(sizes), 128), low, jnp.float32)
    for q_name, q_ref in others:
        q_best = []
        for j in range(0, size_of(q_ref), 256):
            at = (pl.ds(q_name, 1), pl.ds(j, 256))
            p = jnp.concatenate([rows_of(ref, 0, size) for (_, ref), size in zip(ps, sizes)])
            s = dot_rows(p, rows_of(q_ref, j, 256))
            s = s * inv_p * inverses[at]
            earlier = ranks[at] < rank_p
            mine = jnp.where(earlier, s, low)
            p_best = jnp.maximum(p_best, jnp.maximum(mine[:, :128], mine[:, 128:]))
            if q_name != ps[0][0]:
                q_best.append(jnp.max(jnp.where(earlier, low, s), axis=0, keepdims=True))
        if q_best:
            record(best, q_name, jnp.concatenate(q_best, axis=1))
    start = 0
    for (name, _), size in zip(ps, sizes):
        record(best, name, to_row(jnp.max(p_best[start : start + size], axis=1, keepdims=True)))
        start += size


def by_place(spots, run):
    for core in range(2):
        for side in range(2):

            @pl.when((spots[0] == core) & (spots[1] == side))
            def _():
                run(core, side)


def record(best, name, row):
    at = (pl.ds(name, 1), pl.ds(0, row.shape[1]))
    best[at] = jnp.maximum(best[at], row)


O1, O2, U1, U2, V1, V2, E1, E2, W1, W2 = range(10)


def own_kernel(spots, ranks, o1, e1, best, inverses):
    best[...] = jnp.full_like(best, -1.0)
    inverses[...] = jnp.zeros_like(inverses)
    note(inverses, O1, o1)
    note(inverses, E1, e1)

    @pl.when(spots[0] == 0)
    def _():
        meet(best, inverses, ranks, [(O1, o1)], [(O1, o1), (E1, e1)])

    @pl.when(spots[0] != 0)
    def _():
        meet(best, inverses, ranks, [(O1, o1)], [(O1, o1)])


def near_kernel(spots, ranks, o1, u1, e1, before, known, best, inverses):
    best[...] = before[...]
    inverses[...] = known[...]
    note(inverses, U1, u1)

    @pl.when(spots[0] == 0)
    def _():
        meet(best, inverses, ranks, [(U1, u1)], [(O1, o1)])

    @pl.when(spots[0] != 0)
    def _():
        meet(best, inverses, ranks, [(U1, u1)], [(O1, o1), (E1, e1)])


def second_kernel(spots, ranks, o1, o2, u1, v1, e1, e2, w1, before, known, best, inverses):
    best[...] = before[...]
    inverses[...] = known[...]
    note(inverses, V1, v1)
    note(inverses, W1, w1)
    note(inverses, O2, o2)
    note(inverses, E2, e2)
    meet(best, inverses, ranks, [(O2, o2), (E2, e2)], [(O1, o1), (U1, u1), (V1, v1)])

    def run(core, side):
        meet(best, inverses, ranks, [(O2, o2)], [(O2, o2)] + [(E2, e2)] * core)
        if side:
            meet(best, inverses, ranks, [(V1, v1)], [(E1, e1)] * (1 - core) + [(U1, u1)])
        else:
            if core == 0:
                meet(best, inverses, ranks, [(V1, v1)], [(E1, e1)])
            meet(best, inverses, ranks, [(W1, w1)], [(U1, u1)])

    by_place(spots, run)


def third_kernel(spots, ranks, o2, u2, e2, v1, w1, before, known, best, inverses):
    best[...] = before[...]
    inverses[...] = known[...]
    note(inverses, U2, u2)

    def run(core, side):
        others = [(O2, o2), (V1, v1) if side else (W1, w1)] + [(E2, e2)] * core
        meet(best, inverses, ranks, [(U2, u2)], others)

    by_place(spots, run)


def give(best, name, out, start):
    for y in range(Y):
        at = pl.ds(start + y, 1)
        out[at, pl.ds(0, PARTS[0])] = best[pl.ds(name, 1), pl.ds(y * PARTS[0], PARTS[0])]
        pair = best[pl.ds(name + 1, 1), pl.ds(y // 2 * 128, 128)]
        pair = pltpu.roll(pair, 64, 1) if y % 2 else pair
        out[at, pl.ds(PARTS[0], PARTS[1])] = pair[:, : PARTS[1]]


def fourth_kernel(
    spots, ranks, u1, u2, v2, e2, w2, before, known, mine, others, v_best, best, inverses
):
    best[...] = before[...]
    inverses[...] = known[...]
    note(inverses, V2, v2)

    def run(core, side):
        if side:
            others = [(E2, e2)] * (1 - core) + [(U1, u1), (U2, u2)]
            meet(best, inverses, ranks, [(V2, v2)], others)
        else:
            note(inverses, W2, w2)
            if core == 0:
                meet(best, inverses, ranks, [(V2, v2)], [(E2, e2)])
            meet(best, inverses, ranks, [(W2, w2)], [(U1, u1), (U2, u2)])

    by_place(spots, run)

    give(best, O1, mine, 0)
    give(best, U1, mine, Y)
    give(best, E1, others, 0)
    give(best, W1, others, Y)
    give(best, V1, v_best, 0)


def is_dims(item):
    return isinstance(item, tuple) and isinstance(item[0], int)


def scores_call(kernel, units, inputs, out, scratch, name):
    return pl.pallas_call(
        kernel,
        out_shape=jax.tree.map(lambda dims: jax.ShapeDtypeStruct(dims, jnp.float32), out, is_leaf=is_dims),
        in_specs=[SMEM] + [VMEM] * (len(inputs) - 1),
        out_specs=jax.tree.map(lambda _: VMEM, out, is_leaf=is_dims),
        scratch_shapes=scratch,
        compiler_params=PARAMS,
        cost_estimate=pl.CostEstimate(
            flops=int(units * 2 * 256 * 256 * 1024), bytes_accessed=4 * 2**20, transcendentals=0
        ),
        name=name,
    )(*inputs)


def answer_kernel(ids_ref, slot_ref, table_ref, out_ref):
    table = table_ref[...]
    high = table.astype(jnp.bfloat16)
    rest = table - high.astype(jnp.float32)
    middle = rest.astype(jnp.bfloat16)
    small = (rest - middle.astype(jnp.float32)).astype(jnp.bfloat16)
    pieces = jnp.concatenate([high, middle, small], axis=0)
    group = lax.broadcasted_iota(jnp.int32, (3 * GROUPS, 128), 0) & (GROUPS - 1)
    place_in = lax.broadcasted_iota(jnp.int32, (CAP, 128), 0)
    for i in range(LINES):
        ids = ids_ref[pl.ds(i, 1), :]
        within = slot_ref[pl.ds(i, 1), :] - ids * CAP
        member = (group == ids).astype(jnp.float32).astype(jnp.bfloat16)
        found = lax.dot_general(
            pieces, member, (((0,), (0,)), ((), ())), preferred_element_type=jnp.float32
        )
        out_ref[pl.ds(i, 1), :] = jnp.sum(
            jnp.where(place_in == within, found, 0.0), axis=0, keepdims=True
        )


def answer(ids, slots, table):
    return pl.pallas_call(
        answer_kernel,
        out_shape=jax.ShapeDtypeStruct((LINES, 128), jnp.float32),
        in_specs=[VMEM] * 3,
        out_specs=VMEM,
        compiler_params=PARAMS,
        name="answer",
    )(ids, slots, table)


def shards(embeds, cluster_ids, orders):
    y, x, core, z = (lax.axis_index(name) for name in ALL)
    swap = routes(lambda y, x, c, z: (y, x, 1 - c, z))
    ahead = routes(lambda y, x, c, z: (y, x + 1 - 2 * c, c, z))
    behind = routes(lambda y, x, c, z: (y, x - 1 + 2 * c, c, z))

    def bring(rows):
        part = rows.shape[0] // GROUPS
        return lax.all_to_all(
            rows.reshape(GROUPS, part, WIDTH), ("y", "z"), split_axis=0, concat_axis=0, tiled=True
        ).reshape(GROUPS * part, WIDTH)

    ids = cluster_ids.reshape(LINES, 128)
    placed1, slots = place(ids, embeds)
    o1 = bring(placed1)
    placed2 = place_rest(ids, slots, embeds)

    table = ranks(ids, slots, orders.reshape(LINES, 128)).reshape(Y, Z, CAP)
    table = lax.dynamic_index_in_dim(table, z, 1, keepdims=False)
    rank_parts = []
    for j in range(Y):
        row = lax.dynamic_slice_in_dim(table, (y + j) % Y, 1, 0)
        if j:
            row = lax.ppermute(row, ALL, routes(lambda y, x, c, z: (y + j, x, c, z)))
        rank_parts.append(row)
    own_ranks = jnp.concatenate(rank_parts)[(y - jnp.arange(Y)) % Y]
    own_ranks = jnp.where(own_ranks > 0, own_ranks, never_order)
    own_ranks = jnp.stack(
        [
            own_ranks[:, : PARTS[0]].reshape(SIZES[0]),
            jnp.pad(own_ranks[:, PARTS[0] :].reshape(SIZES[1]), (0, SIZES[0] - SIZES[1])),
        ]
    )
    near_ranks = lax.ppermute(own_ranks, ALL, ahead)
    member_ranks = jnp.concatenate(
        [
            own_ranks,
            near_ranks,
            lax.ppermute(own_ranks, ALL, behind),
            lax.ppermute(own_ranks, ALL, swap),
            lax.ppermute(near_ranks, ALL, swap),
            jnp.zeros((6, SIZES[0]), jnp.float32),
        ]
    )
    spots = jnp.stack([core, ((x < X // 2) == (core == 0)).astype(jnp.int32)]).astype(jnp.int32)
    o1, placed2, member_ranks, spots = lax.optimization_barrier((o1, placed2, member_ranks, spots))
    o2 = bring(placed2)

    wide = (16, SIZES[0])

    def score(kernel, units, blocks, state, name, out=(wide, wide), scratch=()):
        inputs = (spots, member_ranks, *blocks, *state)
        return scores_call(kernel, units, inputs, list(out), list(scratch), name)

    u1 = lax.ppermute(o1, ALL, ahead)
    v1 = lax.ppermute(o1, ALL, behind)
    e1 = lax.ppermute(o1, ALL, swap)
    state = score(own_kernel, 8, (o1, e1), (), "own")
    u1, *state = lax.optimization_barrier((u1, *state))
    w1 = lax.ppermute(u1, ALL, swap)
    o2, *state = lax.optimization_barrier((o2, *state))

    u2 = lax.ppermute(o2, ALL, ahead)
    e2 = lax.ppermute(o2, ALL, swap)
    state = score(near_kernel, 6, (o1, u1, e1), state, "near")
    o2, *state = lax.optimization_barrier((o2, *state))
    v2 = lax.ppermute(o2, ALL, behind)
    state = score(second_kernel, 20, (o1, o2, u1, v1, e1, e2, w1), state, "second")
    u2, *state = lax.optimization_barrier((u2, *state))
    w2 = lax.ppermute(u2, ALL, swap)
    state = score(third_kernel, 4, (o2, u2, e2, v1, w1), state, "third")
    v2, *state = lax.optimization_barrier((v2, *state))
    mine, others, v_best = score(
        fourth_kernel, 4, (u1, u2, v2, e2, w2), state, "fourth",
        [(2 * Y, CAP), (2 * Y, CAP), (Y, CAP)], [pltpu.VMEM(wide, jnp.float32)] * 2,
    )
    v_best = lax.ppermute(v_best, ALL, ahead)
    mine = jnp.maximum(mine, lax.ppermute(others, ALL, swap))
    own = jnp.maximum(mine[:Y], v_best)
    own = jnp.maximum(own, lax.ppermute(mine[Y:], ALL, behind))
    table = lax.all_to_all(
        jnp.broadcast_to(own[:, None], (Y, Z, CAP)).reshape(GROUPS, CAP),
        ("y", "z"), split_axis=0, concat_axis=0, tiled=True,
    )
    return answer(ids, slots, table).reshape(ROWS)


def solution(mesh):
    fine = Mesh(mesh.devices.reshape(Y, X, C, Z), ALL)
    clus = ("y", "x", "core")
    return jax.shard_map(
        shards,
        mesh=fine,
        in_specs=(P(clus, "z"), P(clus), P(clus)),
        out_specs=P(clus),
        check_vma=False,
    )
```

```python
import functools

import jax
import jax.numpy as jnp
from jax import lax
from jax.experimental import pallas as pl
from jax.experimental.pallas import tpu as pltpu
from jax.sharding import Mesh, PartitionSpec as P

never_order = 2.0**30
low = -3e38
Y, X, C, Z = 4, 4, 2, 8
ROWS = 3072
GROUPS = 32
CAP = 192
WIDTH = 128
PARTS = (128, 64)
SIZES = (Y * 128, Y * 64)
LINES = ROWS // 128
ALL = ("y", "x", "core", "z")
PARAMS = pltpu.CompilerParams(vmem_limit_bytes=40 * 2**20)
VMEM = pl.BlockSpec(memory_space=pltpu.VMEM)
SMEM = pl.BlockSpec(memory_space=pltpu.SMEM)


def routes(move):
    pairs = []
    for y in range(Y):
        for x in range(X):
            for c in range(C):
                for z in range(Z):
                    y2, x2, c2, z2 = move(y, x, c, z)
                    to = (((y2 % Y) * X + x2 % X) * C + c2 % C) * Z + z2 % Z
                    pairs.append((((y * X + x) * C + c) * Z + z, to))
    return pairs


def scatter_rows(spot_sm, wide_ref, out_ref, first, last):
    @pl.loop(first, last)
    def _(i):
        for lane in range(128):
            spot = spot_sm[i, lane]
            out_ref[pl.ds(spot, 1), :] = wide_ref[pl.ds(i * 128 + lane, 1), :]


def place_kernel(
    ids_any, rows_any, placed_ref, slot_ref,
    ids_ref, rows_ref, member_ref, wide_ref, out_ref, spot_ref, spot_sm, sems,
):
    ids_copy = pltpu.make_async_copy(ids_any, ids_ref, sems.at[0])
    rows_copy = pltpu.make_async_copy(rows_any, rows_ref, sems.at[1])
    ids_copy.start()
    rows_copy.start()
    out_ref[...] = jnp.zeros_like(out_ref)
    r = lax.broadcasted_iota(jnp.int32, (128, 256), 0)
    c = lax.broadcasted_iota(jnp.int32, (128, 256), 1)
    weights = ((r < c) | (c >= 128)).astype(jnp.float32).astype(jnp.bfloat16)
    group = lax.broadcasted_iota(jnp.int32, (GROUPS, 128), 0)
    ids_copy.wait()
    carry = jnp.zeros((GROUPS, 128), jnp.float32)
    copies = []
    for piece in range(LINES // 8):
        lines = range(piece * 8, piece * 8 + 8)
        for i in lines:
            hit = group == ids_ref[pl.ds(i, 1), :]
            member_ref[pl.ds(i * GROUPS, GROUPS), :] = hit.astype(jnp.float32).astype(jnp.bfloat16)
        members = member_ref[pl.ds(piece * 8 * GROUPS, 8 * GROUPS), :]
        counts = jnp.dot(members, weights, preferred_element_type=jnp.float32)
        for at, i in enumerate(lines):
            part = counts[at * GROUPS : (at + 1) * GROUPS]
            line = ids_ref[pl.ds(i, 1), :]
            within = jnp.sum(
                jnp.where(group == line, part[:, :128] + carry, 0.0), axis=0, keepdims=True
            ).astype(jnp.int32)
            slot_ref[pl.ds(i, 1), :] = line * CAP + within
            spot_ref[pl.ds(i, 1), :] = jnp.where(
                within < PARTS[0], line * PARTS[0] + within, GROUPS * PARTS[0]
            )
            carry = carry + part[:, 128:]
        rows = pl.ds(piece * 8, 8)
        copies.append(pltpu.make_async_copy(spot_ref.at[rows], spot_sm.at[rows], sems.at[2 + piece]))
        copies[piece].start()
    rows_copy.wait()
    wide_ref[...] = rows_ref[...].astype(jnp.float32)
    for piece, copy in enumerate(copies):
        copy.wait()
        scatter_rows(spot_sm, wide_ref, out_ref, piece * 8, piece * 8 + 8)
    placed_ref[...] = out_ref[pl.ds(0, GROUPS * PARTS[0]), :].astype(jnp.bfloat16)


def place(ids, rows):
    return pl.pallas_call(
        place_kernel,
        out_shape=(
            jax.ShapeDtypeStruct((GROUPS * PARTS[0], WIDTH), jnp.bfloat16),
            jax.ShapeDtypeStruct((LINES, 128), jnp.int32),
        ),
        in_specs=[pl.BlockSpec(memory_space=pltpu.HBM)] * 2,
        out_specs=(VMEM, VMEM),
        scratch_shapes=[
            pltpu.VMEM((LINES, 128), jnp.int32),
            pltpu.VMEM((ROWS, WIDTH), jnp.bfloat16),
            pltpu.VMEM((LINES * GROUPS, 128), jnp.bfloat16),
            pltpu.VMEM((ROWS, WIDTH), jnp.float32),
            pltpu.VMEM((GROUPS * PARTS[0] + 8, WIDTH), jnp.float32),
            pltpu.VMEM((LINES, 128), jnp.int32),
            pltpu.SMEM((LINES, 128), jnp.int32),
            pltpu.SemaphoreType.DMA((2 + LINES // 8,)),
        ],
        compiler_params=pltpu.CompilerParams(vmem_limit_bytes=60 * 2**20),
        name="place",
    )(ids, rows)


def place_rest_kernel(
    ids_ref, slot_ref, rows_ref, placed_ref, wide_ref, out_ref, spot_ref, spot_sm, sem
):
    ids = ids_ref[...]
    within = slot_ref[...] - ids * CAP
    spot_ref[...] = jnp.where(
        within < PARTS[0], GROUPS * PARTS[1], ids * PARTS[1] + within - PARTS[0]
    )
    copy = pltpu.make_async_copy(spot_ref, spot_sm, sem)
    copy.start()
    out_ref[...] = jnp.zeros_like(out_ref)
    wide_ref[...] = rows_ref[...].astype(jnp.float32)
    copy.wait()
    scatter_rows(spot_sm, wide_ref, out_ref, 0, LINES)
    placed_ref[...] = out_ref[pl.ds(0, GROUPS * PARTS[1]), :].astype(jnp.bfloat16)


def place_rest(ids, slots, rows):
    return pl.pallas_call(
        place_rest_kernel,
        out_shape=jax.ShapeDtypeStruct((GROUPS * PARTS[1], WIDTH), jnp.bfloat16),
        in_specs=[VMEM] * 3,
        out_specs=VMEM,
        scratch_shapes=[
            pltpu.VMEM((ROWS, WIDTH), jnp.float32),
            pltpu.VMEM((GROUPS * PARTS[1] + 8, WIDTH), jnp.float32),
            pltpu.VMEM((LINES, 128), jnp.int32),
            pltpu.SMEM((LINES, 128), jnp.int32),
            pltpu.SemaphoreType.DMA,
        ],
        compiler_params=PARAMS,
        name="place_rest",
    )(ids, slots, rows)


def ranks_kernel(ids_ref, slot_ref, orders_ref, table_ref):
    group = lax.broadcasted_iota(jnp.int32, (GROUPS, 128), 0)
    spot = lax.broadcasted_iota(jnp.int32, (CAP, 128), 0)
    total = jnp.zeros((3 * GROUPS, CAP), jnp.float32)
    for i in range(LINES):
        ids = ids_ref[pl.ds(i, 1), :]
        within = slot_ref[pl.ds(i, 1), :] - ids * CAP
        value = orders_ref[pl.ds(i, 1), :] + 1
        hit = group == ids
        digits = [
            jnp.where(hit, digit.astype(jnp.float32), 0.0)
            for digit in (value & 255, (value >> 8) & 255, value >> 16)
        ]
        left = jnp.concatenate(digits, axis=0).astype(jnp.bfloat16)
        right = (spot == within).astype(jnp.float32).astype(jnp.bfloat16)
        total = total + dot_rows(left, right)
    value = total[:GROUPS] + 256.0 * total[GROUPS : 2 * GROUPS] + 65536.0 * total[2 * GROUPS :]
    table_ref[...] = value


def ranks(ids, slots, orders):
    return pl.pallas_call(
        ranks_kernel,
        out_shape=jax.ShapeDtypeStruct((GROUPS, CAP), jnp.float32),
        in_specs=[VMEM] * 3,
        out_specs=VMEM,
        compiler_params=PARAMS,
        name="ranks",
    )(ids, slots, orders)


def dot_rows(p, q):
    return lax.dot_general(p, q, (((1,), (1,)), ((), ())), preferred_element_type=jnp.float32)


def eye():
    r = lax.broadcasted_iota(jnp.int32, (128, 128), 0)
    return r == lax.broadcasted_iota(jnp.int32, (128, 128), 1)


def to_row(col):
    pieces = []
    for i in range(col.shape[0] // 128):
        piece = jnp.broadcast_to(col[i * 128 : (i + 1) * 128], (128, 128))
        pieces.append(jnp.max(jnp.where(eye(), piece, low), axis=0, keepdims=True))
    return jnp.concatenate(pieces, axis=1)


def to_col(row):
    pieces = []
    for i in range(row.shape[1] // 128):
        piece = jnp.broadcast_to(row[:, i * 128 : (i + 1) * 128], (128, 128))
        pieces.append(jnp.max(jnp.where(eye(), piece, low), axis=1, keepdims=True))
    return jnp.concatenate(pieces, axis=0)


def part_of(ref):
    return ref.shape[0] // GROUPS


def size_of(ref):
    return Y * part_of(ref)


def rows_of(ref, start, count):
    part = part_of(ref)
    lines = []
    for y in range(start // part, (start + count) // part):
        pieces = [ref[pl.ds((y * Z + z) * part, part), :] for z in range(Z)]
        lines.append(jnp.concatenate(pieces, axis=1))
    return jnp.concatenate(lines, axis=0)


def note(inverses, name, ref):
    part = part_of(ref)
    cols = []
    for y in range(Y):
        total = jnp.zeros((part, WIDTH), jnp.float32)
        for z in range(Z):
            wide = ref[pl.ds((y * Z + z) * part, part), :].astype(jnp.float32)
            total = total + wide * wide
        cols.append(lax.rsqrt(jnp.sum(total, axis=1, keepdims=True) + 1e-06))
    inverses[pl.ds(name, 1), pl.ds(0, Y * part)] = to_row(jnp.concatenate(cols, axis=0))


def meet(best, inverses, ranks, ps, others):
    sizes = [size_of(ref) for _, ref in ps]
    inv_p, rank_p = (
        jnp.concatenate(
            [to_col(rows[pl.ds(name, 1), pl.ds(0, size)]) for (name, _), size in zip(ps, sizes)]
        )
        for rows in (inverses, ranks)
    )
    p_best = jnp.full((sum(sizes), 128), low, jnp.float32)
    for q_name, q_ref in others:
        q_best = []
        for j in range(0, size_of(q_ref), 256):
            at = (pl.ds(q_name, 1), pl.ds(j, 256))
            p = jnp.concatenate([rows_of(ref, 0, size) for (_, ref), size in zip(ps, sizes)])
            s = dot_rows(p, rows_of(q_ref, j, 256))
            s = s * inv_p * inverses[at]
            earlier = ranks[at] < rank_p
            mine = jnp.where(earlier, s, low)
            p_best = jnp.maximum(p_best, jnp.maximum(mine[:, :128], mine[:, 128:]))
            if q_name != ps[0][0]:
                q_best.append(jnp.max(jnp.where(earlier, low, s), axis=0, keepdims=True))
        if q_best:
            record(best, q_name, jnp.concatenate(q_best, axis=1))
    start = 0
    for (name, _), size in zip(ps, sizes):
        record(best, name, to_row(jnp.max(p_best[start : start + size], axis=1, keepdims=True)))
        start += size


def by_place(spots, run):
    for core in range(2):
        for side in range(2):

            @pl.when((spots[0] == core) & (spots[1] == side))
            def _():
                run(core, side)


def record(best, name, row):
    at = (pl.ds(name, 1), pl.ds(0, row.shape[1]))
    best[at] = jnp.maximum(best[at], row)


O1, O2, U1, U2, V1, V2, E1, E2, W1, W2 = range(10)


def own_kernel(spots, ranks, o1, e1, best, inverses):
    best[...] = jnp.full_like(best, -1.0)
    inverses[...] = jnp.zeros_like(inverses)
    note(inverses, O1, o1)
    note(inverses, E1, e1)

    @pl.when(spots[0] == 0)
    def _():
        meet(best, inverses, ranks, [(O1, o1)], [(O1, o1), (E1, e1)])

    @pl.when(spots[0] != 0)
    def _():
        meet(best, inverses, ranks, [(O1, o1)], [(O1, o1)])


def near_kernel(spots, ranks, o1, u1, e1, before, known, best, inverses):
    best[...] = before[...]
    inverses[...] = known[...]
    note(inverses, U1, u1)

    @pl.when(spots[0] == 0)
    def _():
        meet(best, inverses, ranks, [(U1, u1)], [(O1, o1)])

    @pl.when(spots[0] != 0)
    def _():
        meet(best, inverses, ranks, [(U1, u1)], [(O1, o1), (E1, e1)])


def second_kernel(spots, ranks, o1, o2, u1, v1, e1, e2, w1, before, known, best, inverses):
    best[...] = before[...]
    inverses[...] = known[...]
    note(inverses, V1, v1)
    note(inverses, W1, w1)
    note(inverses, O2, o2)
    note(inverses, E2, e2)
    meet(best, inverses, ranks, [(O2, o2), (E2, e2)], [(O1, o1), (U1, u1), (V1, v1)])

    def run(core, side):
        meet(best, inverses, ranks, [(O2, o2)], [(O2, o2)] + [(E2, e2)] * core)
        if side:
            meet(best, inverses, ranks, [(V1, v1)], [(E1, e1)] * (1 - core) + [(U1, u1)])
        else:
            if core == 0:
                meet(best, inverses, ranks, [(V1, v1)], [(E1, e1)])
            meet(best, inverses, ranks, [(W1, w1)], [(U1, u1)])

    by_place(spots, run)


def third_kernel(spots, ranks, o2, u2, e2, v1, w1, before, known, best, inverses):
    best[...] = before[...]
    inverses[...] = known[...]
    note(inverses, U2, u2)

    def run(core, side):
        others = [(O2, o2), (V1, v1) if side else (W1, w1)] + [(E2, e2)] * core
        meet(best, inverses, ranks, [(U2, u2)], others)

    by_place(spots, run)


def give(best, name, out, start):
    for y in range(Y):
        at = pl.ds(start + y, 1)
        out[at, pl.ds(0, PARTS[0])] = best[pl.ds(name, 1), pl.ds(y * PARTS[0], PARTS[0])]
        pair = best[pl.ds(name + 1, 1), pl.ds(y // 2 * 128, 128)]
        pair = pltpu.roll(pair, 64, 1) if y % 2 else pair
        out[at, pl.ds(PARTS[0], PARTS[1])] = pair[:, : PARTS[1]]


def fourth_kernel(
    spots, ranks, u1, u2, v2, e2, w2, before, known, mine, others, v_best, best, inverses
):
    best[...] = before[...]
    inverses[...] = known[...]
    note(inverses, V2, v2)

    def run(core, side):
        if side:
            others = [(E2, e2)] * (1 - core) + [(U1, u1), (U2, u2)]
            meet(best, inverses, ranks, [(V2, v2)], others)
        else:
            note(inverses, W2, w2)
            if core == 0:
                meet(best, inverses, ranks, [(V2, v2)], [(E2, e2)])
            meet(best, inverses, ranks, [(W2, w2)], [(U1, u1), (U2, u2)])

    by_place(spots, run)

    give(best, O1, mine, 0)
    give(best, U1, mine, Y)
    give(best, E1, others, 0)
    give(best, W1, others, Y)
    give(best, V1, v_best, 0)


def is_dims(item):
    return isinstance(item, tuple) and isinstance(item[0], int)


def scores_call(kernel, units, inputs, out, scratch, name):
    return pl.pallas_call(
        kernel,
        out_shape=jax.tree.map(lambda dims: jax.ShapeDtypeStruct(dims, jnp.float32), out, is_leaf=is_dims),
        in_specs=[SMEM] + [VMEM] * (len(inputs) - 1),
        out_specs=jax.tree.map(lambda _: VMEM, out, is_leaf=is_dims),
        scratch_shapes=scratch,
        compiler_params=PARAMS,
        cost_estimate=pl.CostEstimate(
            flops=int(units * 2 * 256 * 256 * 1024), bytes_accessed=4 * 2**20, transcendentals=0
        ),
        name=name,
    )(*inputs)


def answer_kernel(ids_ref, slot_ref, table_ref, out_ref):
    table = table_ref[...]
    high = table.astype(jnp.bfloat16)
    rest = table - high.astype(jnp.float32)
    middle = rest.astype(jnp.bfloat16)
    small = (rest - middle.astype(jnp.float32)).astype(jnp.bfloat16)
    pieces = jnp.concatenate([high, middle, small], axis=0)
    group = lax.broadcasted_iota(jnp.int32, (3 * GROUPS, 128), 0) & (GROUPS - 1)
    place_in = lax.broadcasted_iota(jnp.int32, (CAP, 128), 0)
    for first in range(0, LINES, 4):
        lines = range(first, first + 4)
        member = jnp.concatenate(
            [(group == ids_ref[pl.ds(i, 1), :]).astype(jnp.float32) for i in lines], axis=1
        ).astype(jnp.bfloat16)
        found = lax.dot_general(
            pieces, member, (((0,), (0,)), ((), ())), preferred_element_type=jnp.float32
        )
        for at, i in enumerate(lines):
            within = slot_ref[pl.ds(i, 1), :] - ids_ref[pl.ds(i, 1), :] * CAP
            out_ref[pl.ds(i, 1), :] = jnp.sum(
                jnp.where(place_in == within, found[:, at * 128 : (at + 1) * 128], 0.0),
                axis=0,
                keepdims=True,
            )


def answer(ids, slots, table):
    return pl.pallas_call(
        answer_kernel,
        out_shape=jax.ShapeDtypeStruct((LINES, 128), jnp.float32),
        in_specs=[VMEM] * 3,
        out_specs=VMEM,
        compiler_params=PARAMS,
        name="answer",
    )(ids, slots, table)


def shards(embeds, cluster_ids, orders):
    y, x, core, z = (lax.axis_index(name) for name in ALL)
    swap = routes(lambda y, x, c, z: (y, x, 1 - c, z))
    ahead = routes(lambda y, x, c, z: (y, x + 1 - 2 * c, c, z))
    behind = routes(lambda y, x, c, z: (y, x - 1 + 2 * c, c, z))

    def bring(rows):
        part = rows.shape[0] // GROUPS
        return lax.all_to_all(
            rows.reshape(GROUPS, part, WIDTH), ("y", "z"), split_axis=0, concat_axis=0, tiled=True
        ).reshape(GROUPS * part, WIDTH)

    ids = cluster_ids.reshape(LINES, 128)
    placed1, slots = place(ids, embeds)
    o1 = bring(placed1)
    placed2 = place_rest(ids, slots, embeds)

    table = ranks(ids, slots, orders.reshape(LINES, 128)).reshape(Y, Z, CAP)
    table = lax.dynamic_index_in_dim(table, z, 1, keepdims=False)
    rank_parts = []
    for j in range(Y):
        row = lax.dynamic_slice_in_dim(table, (y + j) % Y, 1, 0)
        if j:
            row = lax.ppermute(row, ALL, routes(lambda y, x, c, z: (y + j, x, c, z)))
        rank_parts.append(row)
    own_ranks = jnp.concatenate(rank_parts)[(y - jnp.arange(Y)) % Y]
    own_ranks = jnp.where(own_ranks > 0, own_ranks, never_order)
    own_ranks = jnp.stack(
        [
            own_ranks[:, : PARTS[0]].reshape(SIZES[0]),
            jnp.pad(own_ranks[:, PARTS[0] :].reshape(SIZES[1]), (0, SIZES[0] - SIZES[1])),
        ]
    )
    near_ranks = lax.ppermute(own_ranks, ALL, ahead)
    member_ranks = jnp.concatenate(
        [
            own_ranks,
            near_ranks,
            lax.ppermute(own_ranks, ALL, behind),
            lax.ppermute(own_ranks, ALL, swap),
            lax.ppermute(near_ranks, ALL, swap),
            jnp.zeros((6, SIZES[0]), jnp.float32),
        ]
    )
    spots = jnp.stack([core, ((x < X // 2) == (core == 0)).astype(jnp.int32)]).astype(jnp.int32)
    o1, placed2, member_ranks, spots = lax.optimization_barrier((o1, placed2, member_ranks, spots))
    o2 = bring(placed2)

    wide = (16, SIZES[0])

    def score(kernel, units, blocks, state, name, out=(wide, wide), scratch=()):
        inputs = (spots, member_ranks, *blocks, *state)
        return scores_call(kernel, units, inputs, list(out), list(scratch), name)

    u1 = lax.ppermute(o1, ALL, ahead)
    v1 = lax.ppermute(o1, ALL, behind)
    e1 = lax.ppermute(o1, ALL, swap)
    state = score(own_kernel, 8, (o1, e1), (), "own")
    u1, *state = lax.optimization_barrier((u1, *state))
    w1 = lax.ppermute(u1, ALL, swap)
    o2, *state = lax.optimization_barrier((o2, *state))

    u2 = lax.ppermute(o2, ALL, ahead)
    e2 = lax.ppermute(o2, ALL, swap)
    state = score(near_kernel, 6, (o1, u1, e1), state, "near")
    o2, *state = lax.optimization_barrier((o2, *state))
    v2 = lax.ppermute(o2, ALL, behind)
    state = score(second_kernel, 20, (o1, o2, u1, v1, e1, e2, w1), state, "second")
    u2, *state = lax.optimization_barrier((u2, *state))
    w2 = lax.ppermute(u2, ALL, swap)
    state = score(third_kernel, 4, (o2, u2, e2, v1, w1), state, "third")
    v2, *state = lax.optimization_barrier((v2, *state))
    mine, others, v_best = score(
        fourth_kernel, 4, (u1, u2, v2, e2, w2), state, "fourth",
        [(2 * Y, CAP), (2 * Y, CAP), (Y, CAP)], [pltpu.VMEM(wide, jnp.float32)] * 2,
    )
    v_best = lax.ppermute(v_best, ALL, ahead)
    mine = jnp.maximum(mine, lax.ppermute(others, ALL, swap))
    own = jnp.maximum(mine[:Y], v_best)
    own = jnp.maximum(own, lax.ppermute(mine[Y:], ALL, behind))
    table = lax.all_to_all(
        jnp.broadcast_to(own[:, None], (Y, Z, CAP)).reshape(GROUPS, CAP),
        ("y", "z"), split_axis=0, concat_axis=0, tiled=True,
    )
    return answer(ids, slots, table).reshape(ROWS)


def solution(mesh):
    fine = Mesh(mesh.devices.reshape(Y, X, C, Z), ALL)
    clus = ("y", "x", "core")
    return jax.shard_map(
        shards,
        mesh=fine,
        in_specs=(P(clus, "z"), P(clus), P(clus)),
        out_specs=P(clus),
        check_vma=False,
    )
```

```python
import functools

import jax
import jax.numpy as jnp
from jax import lax
from jax.experimental import pallas as pl
from jax.experimental.pallas import tpu as pltpu
from jax.sharding import Mesh, PartitionSpec as P

never_order = 2.0**30
low = -3e38
Y, X, C, Z = 4, 4, 2, 8
ROWS = 3072
GROUPS = 32
CAP = 192
WIDTH = 128
PARTS = (128, 64)
SIZES = (Y * 128, Y * 64)
LINES = ROWS // 128
ALL = ("y", "x", "core", "z")
PARAMS = pltpu.CompilerParams(vmem_limit_bytes=40 * 2**20)
VMEM = pl.BlockSpec(memory_space=pltpu.VMEM)
SMEM = pl.BlockSpec(memory_space=pltpu.SMEM)


def routes(move):
    pairs = []
    for y in range(Y):
        for x in range(X):
            for c in range(C):
                for z in range(Z):
                    y2, x2, c2, z2 = move(y, x, c, z)
                    to = (((y2 % Y) * X + x2 % X) * C + c2 % C) * Z + z2 % Z
                    pairs.append((((y * X + x) * C + c) * Z + z, to))
    return pairs


def scatter_rows(spot_sm, wide_ref, out_ref, first, last):
    @pl.loop(first, last)
    def _(i):
        for lane in range(128):
            spot = spot_sm[i, lane]
            out_ref[pl.ds(spot, 1), :] = wide_ref[pl.ds(i * 128 + lane, 1), :]


def place_kernel(
    ids_any, rows_any, placed_ref, slot_ref,
    ids_ref, rows_ref, member_ref, wide_ref, out_ref, spot_ref, spot_sm, sems,
):
    ids_copy = pltpu.make_async_copy(ids_any, ids_ref, sems.at[0])
    rows_copy = pltpu.make_async_copy(rows_any, rows_ref, sems.at[1])
    ids_copy.start()
    rows_copy.start()
    out_ref[...] = jnp.zeros_like(out_ref)
    r = lax.broadcasted_iota(jnp.int32, (128, 256), 0)
    c = lax.broadcasted_iota(jnp.int32, (128, 256), 1)
    weights = ((r < c) | (c >= 128)).astype(jnp.float32).astype(jnp.bfloat16)
    group = lax.broadcasted_iota(jnp.int32, (GROUPS, 128), 0)
    ids_copy.wait()
    carry = jnp.zeros((GROUPS, 128), jnp.float32)
    copies = []
    for piece in range(LINES // 8):
        lines = range(piece * 8, piece * 8 + 8)
        for i in lines:
            hit = group == ids_ref[pl.ds(i, 1), :]
            member_ref[pl.ds(i * GROUPS, GROUPS), :] = hit.astype(jnp.float32).astype(jnp.bfloat16)
        members = member_ref[pl.ds(piece * 8 * GROUPS, 8 * GROUPS), :]
        counts = jnp.dot(members, weights, preferred_element_type=jnp.float32)
        for at, i in enumerate(lines):
            part = counts[at * GROUPS : (at + 1) * GROUPS]
            line = ids_ref[pl.ds(i, 1), :]
            within = jnp.sum(
                jnp.where(group == line, part[:, :128] + carry, 0.0), axis=0, keepdims=True
            ).astype(jnp.int32)
            slot_ref[pl.ds(i, 1), :] = line * CAP + within
            spot_ref[pl.ds(i, 1), :] = jnp.where(
                within < PARTS[0], line * PARTS[0] + within, GROUPS * PARTS[0]
            )
            carry = carry + part[:, 128:]
        rows = pl.ds(piece * 8, 8)
        copies.append(pltpu.make_async_copy(spot_ref.at[rows], spot_sm.at[rows], sems.at[2 + piece]))
        copies[piece].start()
    rows_copy.wait()
    wide_ref[...] = rows_ref[...].astype(jnp.float32)
    for piece, copy in enumerate(copies):
        copy.wait()
        scatter_rows(spot_sm, wide_ref, out_ref, piece * 8, piece * 8 + 8)
    placed_ref[...] = out_ref[pl.ds(0, GROUPS * PARTS[0]), :].astype(jnp.bfloat16)


def place(ids, rows):
    return pl.pallas_call(
        place_kernel,
        out_shape=(
            jax.ShapeDtypeStruct((GROUPS * PARTS[0], WIDTH), jnp.bfloat16),
            jax.ShapeDtypeStruct((LINES, 128), jnp.int32),
        ),
        in_specs=[pl.BlockSpec(memory_space=pltpu.HBM)] * 2,
        out_specs=(VMEM, VMEM),
        scratch_shapes=[
            pltpu.VMEM((LINES, 128), jnp.int32),
            pltpu.VMEM((ROWS, WIDTH), jnp.bfloat16),
            pltpu.VMEM((LINES * GROUPS, 128), jnp.bfloat16),
            pltpu.VMEM((ROWS, WIDTH), jnp.float32),
            pltpu.VMEM((GROUPS * PARTS[0] + 8, WIDTH), jnp.float32),
            pltpu.VMEM((LINES, 128), jnp.int32),
            pltpu.SMEM((LINES, 128), jnp.int32),
            pltpu.SemaphoreType.DMA((2 + LINES // 8,)),
        ],
        compiler_params=pltpu.CompilerParams(vmem_limit_bytes=60 * 2**20),
        name="place",
    )(ids, rows)


def place_rest_kernel(
    ids_ref, slot_ref, rows_ref, placed_ref, wide_ref, out_ref, spot_ref, spot_sm, sem
):
    ids = ids_ref[...]
    within = slot_ref[...] - ids * CAP
    spot_ref[...] = jnp.where(
        within < PARTS[0], GROUPS * PARTS[1], ids * PARTS[1] + within - PARTS[0]
    )
    copy = pltpu.make_async_copy(spot_ref, spot_sm, sem)
    copy.start()
    out_ref[...] = jnp.zeros_like(out_ref)
    wide_ref[...] = rows_ref[...].astype(jnp.float32)
    copy.wait()
    scatter_rows(spot_sm, wide_ref, out_ref, 0, LINES)
    placed_ref[...] = out_ref[pl.ds(0, GROUPS * PARTS[1]), :].astype(jnp.bfloat16)


def place_rest(ids, slots, rows):
    return pl.pallas_call(
        place_rest_kernel,
        out_shape=jax.ShapeDtypeStruct((GROUPS * PARTS[1], WIDTH), jnp.bfloat16),
        in_specs=[VMEM] * 3,
        out_specs=VMEM,
        scratch_shapes=[
            pltpu.VMEM((ROWS, WIDTH), jnp.float32),
            pltpu.VMEM((GROUPS * PARTS[1] + 8, WIDTH), jnp.float32),
            pltpu.VMEM((LINES, 128), jnp.int32),
            pltpu.SMEM((LINES, 128), jnp.int32),
            pltpu.SemaphoreType.DMA,
        ],
        compiler_params=PARAMS,
        name="place_rest",
    )(ids, slots, rows)


def ranks_kernel(ids_ref, slot_ref, orders_ref, table_ref):
    group = lax.broadcasted_iota(jnp.int32, (GROUPS, 128), 0)
    spot = lax.broadcasted_iota(jnp.int32, (CAP, 128), 0)
    total = jnp.zeros((3 * GROUPS, CAP), jnp.float32)
    for i in range(LINES):
        ids = ids_ref[pl.ds(i, 1), :]
        within = slot_ref[pl.ds(i, 1), :] - ids * CAP
        value = orders_ref[pl.ds(i, 1), :] + 1
        hit = group == ids
        digits = [
            jnp.where(hit, digit.astype(jnp.float32), 0.0)
            for digit in (value & 255, (value >> 8) & 255, value >> 16)
        ]
        left = jnp.concatenate(digits, axis=0).astype(jnp.bfloat16)
        right = (spot == within).astype(jnp.float32).astype(jnp.bfloat16)
        total = total + dot_rows(left, right)
    value = total[:GROUPS] + 256.0 * total[GROUPS : 2 * GROUPS] + 65536.0 * total[2 * GROUPS :]
    table_ref[...] = value


def ranks(ids, slots, orders):
    return pl.pallas_call(
        ranks_kernel,
        out_shape=jax.ShapeDtypeStruct((GROUPS, CAP), jnp.float32),
        in_specs=[VMEM] * 3,
        out_specs=VMEM,
        compiler_params=PARAMS,
        name="ranks",
    )(ids, slots, orders)


def dot_rows(p, q):
    return lax.dot_general(p, q, (((1,), (1,)), ((), ())), preferred_element_type=jnp.float32)


def eye():
    r = lax.broadcasted_iota(jnp.int32, (128, 128), 0)
    return r == lax.broadcasted_iota(jnp.int32, (128, 128), 1)


def to_row(col):
    pieces = []
    for i in range(col.shape[0] // 128):
        piece = jnp.broadcast_to(col[i * 128 : (i + 1) * 128], (128, 128))
        pieces.append(jnp.max(jnp.where(eye(), piece, low), axis=0, keepdims=True))
    return jnp.concatenate(pieces, axis=1)


def to_col(row):
    pieces = []
    for i in range(row.shape[1] // 128):
        piece = jnp.broadcast_to(row[:, i * 128 : (i + 1) * 128], (128, 128))
        pieces.append(jnp.max(jnp.where(eye(), piece, low), axis=1, keepdims=True))
    return jnp.concatenate(pieces, axis=0)


def part_of(ref):
    return ref.shape[0] // GROUPS


def size_of(ref):
    return Y * part_of(ref)


def rows_of(ref, start, count):
    part = part_of(ref)
    lines = []
    for y in range(start // part, (start + count) // part):
        pieces = [ref[pl.ds((y * Z + z) * part, part), :] for z in range(Z)]
        lines.append(jnp.concatenate(pieces, axis=1))
    return jnp.concatenate(lines, axis=0)


def note(inverses, name, ref):
    part = part_of(ref)
    cols = []
    for y in range(Y):
        total = jnp.zeros((part, WIDTH), jnp.float32)
        for z in range(Z):
            wide = ref[pl.ds((y * Z + z) * part, part), :].astype(jnp.float32)
            total = total + wide * wide
        cols.append(lax.rsqrt(jnp.sum(total, axis=1, keepdims=True) + 1e-06))
    inverses[pl.ds(name, 1), pl.ds(0, Y * part)] = to_row(jnp.concatenate(cols, axis=0))


def meet(best, inverses, ranks, ps, others):
    sizes = [size_of(ref) for _, ref in ps]
    inv_p, rank_p = (
        jnp.concatenate(
            [to_col(rows[pl.ds(name, 1), pl.ds(0, size)]) for (name, _), size in zip(ps, sizes)]
        )
        for rows in (inverses, ranks)
    )
    p_best = jnp.full((sum(sizes), 128), low, jnp.float32)
    for q_name, q_ref in others:
        q_best = []
        for j in range(0, size_of(q_ref), 256):
            at = (pl.ds(q_name, 1), pl.ds(j, 256))
            p = jnp.concatenate([rows_of(ref, 0, size) for (_, ref), size in zip(ps, sizes)])
            s = dot_rows(p, rows_of(q_ref, j, 256))
            s = s * inv_p * inverses[at]
            earlier = ranks[at] < rank_p
            mine = jnp.where(earlier, s, low)
            p_best = jnp.maximum(p_best, jnp.maximum(mine[:, :128], mine[:, 128:]))
            if q_name != ps[0][0]:
                q_best.append(jnp.max(jnp.where(earlier, low, s), axis=0, keepdims=True))
        if q_best:
            record(best, q_name, jnp.concatenate(q_best, axis=1))
    start = 0
    for (name, _), size in zip(ps, sizes):
        record(best, name, to_row(jnp.max(p_best[start : start + size], axis=1, keepdims=True)))
        start += size


def by_place(spots, run):
    for core in range(2):
        for side in range(2):

            @pl.when((spots[0] == core) & (spots[1] == side))
            def _():
                run(core, side)


def record(best, name, row):
    at = (pl.ds(name, 1), pl.ds(0, row.shape[1]))
    best[at] = jnp.maximum(best[at], row)


O1, O2, U1, U2, V1, V2, E1, E2, W1, W2 = range(10)


def own_kernel(spots, ranks, o1, e1, best, inverses):
    best[...] = jnp.full_like(best, -1.0)
    inverses[...] = jnp.zeros_like(inverses)
    note(inverses, O1, o1)
    note(inverses, E1, e1)

    @pl.when(spots[0] == 0)
    def _():
        meet(best, inverses, ranks, [(O1, o1)], [(O1, o1), (E1, e1)])

    @pl.when(spots[0] != 0)
    def _():
        meet(best, inverses, ranks, [(O1, o1)], [(O1, o1)])


def near_kernel(spots, ranks, o1, u1, before, known, best, inverses):
    best[...] = before[...]
    inverses[...] = known[...]
    note(inverses, U1, u1)
    meet(best, inverses, ranks, [(U1, u1)], [(O1, o1)])


def second_kernel(spots, ranks, o1, o2, u1, v1, e1, e2, w1, before, known, best, inverses):
    best[...] = before[...]
    inverses[...] = known[...]
    note(inverses, V1, v1)
    note(inverses, W1, w1)
    note(inverses, O2, o2)
    note(inverses, E2, e2)
    meet(best, inverses, ranks, [(O2, o2), (E2, e2)], [(O1, o1), (U1, u1), (V1, v1)])

    def run(core, side):
        meet(best, inverses, ranks, [(O2, o2)], [(O2, o2)] + [(E2, e2)] * core)
        if core:
            others = [(V1, v1) if side else (W1, w1), (E1, e1)]
            meet(best, inverses, ranks, [(U1, u1)], others)
        elif side:
            meet(best, inverses, ranks, [(V1, v1)], [(E1, e1), (U1, u1)])
        else:
            meet(best, inverses, ranks, [(V1, v1)], [(E1, e1)])
            meet(best, inverses, ranks, [(W1, w1)], [(U1, u1)])

    by_place(spots, run)


def third_kernel(spots, ranks, o2, u2, e2, v1, w1, before, known, best, inverses):
    best[...] = before[...]
    inverses[...] = known[...]
    note(inverses, U2, u2)

    def run(core, side):
        others = [(O2, o2), (V1, v1) if side else (W1, w1)] + [(E2, e2)] * core
        meet(best, inverses, ranks, [(U2, u2)], others)

    by_place(spots, run)


def give(best, name, out, start):
    for y in range(Y):
        at = pl.ds(start + y, 1)
        out[at, pl.ds(0, PARTS[0])] = best[pl.ds(name, 1), pl.ds(y * PARTS[0], PARTS[0])]
        pair = best[pl.ds(name + 1, 1), pl.ds(y // 2 * 128, 128)]
        pair = pltpu.roll(pair, 64, 1) if y % 2 else pair
        out[at, pl.ds(PARTS[0], PARTS[1])] = pair[:, : PARTS[1]]


def fourth_kernel(
    spots, ranks, u1, u2, v2, e2, w2, before, known, mine, others, v_best, best, inverses
):
    best[...] = before[...]
    inverses[...] = known[...]
    note(inverses, V2, v2)

    def run(core, side):
        if side:
            others = [(E2, e2)] * (1 - core) + [(U1, u1), (U2, u2)]
            meet(best, inverses, ranks, [(V2, v2)], others)
        else:
            note(inverses, W2, w2)
            if core == 0:
                meet(best, inverses, ranks, [(V2, v2)], [(E2, e2)])
            meet(best, inverses, ranks, [(W2, w2)], [(U1, u1), (U2, u2)])

    by_place(spots, run)

    give(best, O1, mine, 0)
    give(best, U1, mine, Y)
    give(best, E1, others, 0)
    give(best, W1, others, Y)
    give(best, V1, v_best, 0)


def is_dims(item):
    return isinstance(item, tuple) and isinstance(item[0], int)


def scores_call(kernel, units, inputs, out, scratch, name):
    return pl.pallas_call(
        kernel,
        out_shape=jax.tree.map(lambda dims: jax.ShapeDtypeStruct(dims, jnp.float32), out, is_leaf=is_dims),
        in_specs=[SMEM] + [VMEM] * (len(inputs) - 1),
        out_specs=jax.tree.map(lambda _: VMEM, out, is_leaf=is_dims),
        scratch_shapes=scratch,
        compiler_params=PARAMS,
        cost_estimate=pl.CostEstimate(
            flops=int(units * 2 * 256 * 256 * 1024), bytes_accessed=4 * 2**20, transcendentals=0
        ),
        name=name,
    )(*inputs)


def answer_kernel(ids_ref, slot_ref, table_ref, out_ref):
    table = table_ref[...]
    high = table.astype(jnp.bfloat16)
    rest = table - high.astype(jnp.float32)
    middle = rest.astype(jnp.bfloat16)
    small = (rest - middle.astype(jnp.float32)).astype(jnp.bfloat16)
    pieces = jnp.concatenate([high, middle, small], axis=0)
    group = lax.broadcasted_iota(jnp.int32, (3 * GROUPS, 128), 0) & (GROUPS - 1)
    place_in = lax.broadcasted_iota(jnp.int32, (CAP, 128), 0)
    for first in range(0, LINES, 4):
        lines = range(first, first + 4)
        member = jnp.concatenate(
            [(group == ids_ref[pl.ds(i, 1), :]).astype(jnp.float32) for i in lines], axis=1
        ).astype(jnp.bfloat16)
        found = lax.dot_general(
            pieces, member, (((0,), (0,)), ((), ())), preferred_element_type=jnp.float32
        )
        for at, i in enumerate(lines):
            within = slot_ref[pl.ds(i, 1), :] - ids_ref[pl.ds(i, 1), :] * CAP
            out_ref[pl.ds(i, 1), :] = jnp.sum(
                jnp.where(place_in == within, found[:, at * 128 : (at + 1) * 128], 0.0),
                axis=0,
                keepdims=True,
            )


def answer(ids, slots, table):
    return pl.pallas_call(
        answer_kernel,
        out_shape=jax.ShapeDtypeStruct((LINES, 128), jnp.float32),
        in_specs=[VMEM] * 3,
        out_specs=VMEM,
        compiler_params=PARAMS,
        name="answer",
    )(ids, slots, table)


def shards(embeds, cluster_ids, orders):
    y, x, core, z = (lax.axis_index(name) for name in ALL)
    swap = routes(lambda y, x, c, z: (y, x, 1 - c, z))
    ahead = routes(lambda y, x, c, z: (y, x + 1 - 2 * c, c, z))
    behind = routes(lambda y, x, c, z: (y, x - 1 + 2 * c, c, z))

    def bring(rows):
        part = rows.shape[0] // GROUPS
        return lax.all_to_all(
            rows.reshape(GROUPS, part, WIDTH), ("y", "z"), split_axis=0, concat_axis=0, tiled=True
        ).reshape(GROUPS * part, WIDTH)

    ids = cluster_ids.reshape(LINES, 128)
    placed1, slots = place(ids, embeds)
    o1 = bring(placed1)
    placed2 = place_rest(ids, slots, embeds)

    table = ranks(ids, slots, orders.reshape(LINES, 128)).reshape(Y, Z, CAP)
    table = lax.dynamic_index_in_dim(table, z, 1, keepdims=False)
    rank_parts = []
    for j in range(Y):
        row = lax.dynamic_slice_in_dim(table, (y + j) % Y, 1, 0)
        if j:
            row = lax.ppermute(row, ALL, routes(lambda y, x, c, z: (y + j, x, c, z)))
        rank_parts.append(row)
    own_ranks = jnp.concatenate(rank_parts)[(y - jnp.arange(Y)) % Y]
    own_ranks = jnp.where(own_ranks > 0, own_ranks, never_order)
    own_ranks = jnp.stack(
        [
            own_ranks[:, : PARTS[0]].reshape(SIZES[0]),
            jnp.pad(own_ranks[:, PARTS[0] :].reshape(SIZES[1]), (0, SIZES[0] - SIZES[1])),
        ]
    )
    near_ranks = lax.ppermute(own_ranks, ALL, ahead)
    member_ranks = jnp.concatenate(
        [
            own_ranks,
            near_ranks,
            lax.ppermute(own_ranks, ALL, behind),
            lax.ppermute(own_ranks, ALL, swap),
            lax.ppermute(near_ranks, ALL, swap),
            jnp.zeros((6, SIZES[0]), jnp.float32),
        ]
    )
    spots = jnp.stack([core, ((x < X // 2) == (core == 0)).astype(jnp.int32)]).astype(jnp.int32)
    o1, placed2, member_ranks, spots = lax.optimization_barrier((o1, placed2, member_ranks, spots))
    o2 = bring(placed2)

    wide = (16, SIZES[0])

    def score(kernel, units, blocks, state, name, out=(wide, wide), scratch=()):
        inputs = (spots, member_ranks, *blocks, *state)
        return scores_call(kernel, units, inputs, list(out), list(scratch), name)

    u1 = lax.ppermute(o1, ALL, ahead)
    v1 = lax.ppermute(o1, ALL, behind)
    e1 = lax.ppermute(o1, ALL, swap)
    state = score(own_kernel, 8, (o1, e1), (), "own")
    u1, *state = lax.optimization_barrier((u1, *state))
    w1 = lax.ppermute(u1, ALL, swap)
    o2, *state = lax.optimization_barrier((o2, *state))

    u2 = lax.ppermute(o2, ALL, ahead)
    e2 = lax.ppermute(o2, ALL, swap)
    state = score(near_kernel, 4, (o1, u1), state, "near")
    o2, *state = lax.optimization_barrier((o2, *state))
    v2 = lax.ppermute(o2, ALL, behind)
    state = score(second_kernel, 20, (o1, o2, u1, v1, e1, e2, w1), state, "second")
    u2, *state = lax.optimization_barrier((u2, *state))
    w2 = lax.ppermute(u2, ALL, swap)
    state = score(third_kernel, 4, (o2, u2, e2, v1, w1), state, "third")
    v2, *state = lax.optimization_barrier((v2, *state))
    mine, others, v_best = score(
        fourth_kernel, 4, (u1, u2, v2, e2, w2), state, "fourth",
        [(2 * Y, CAP), (2 * Y, CAP), (Y, CAP)], [pltpu.VMEM(wide, jnp.float32)] * 2,
    )
    v_best = lax.ppermute(v_best, ALL, ahead)
    mine = jnp.maximum(mine, lax.ppermute(others, ALL, swap))
    own = jnp.maximum(mine[:Y], v_best)
    own = jnp.maximum(own, lax.ppermute(mine[Y:], ALL, behind))
    table = lax.all_to_all(
        jnp.broadcast_to(own[:, None], (Y, Z, CAP)).reshape(GROUPS, CAP),
        ("y", "z"), split_axis=0, concat_axis=0, tiled=True,
    )
    return answer(ids, slots, table).reshape(ROWS)


def solution(mesh):
    fine = Mesh(mesh.devices.reshape(Y, X, C, Z), ALL)
    clus = ("y", "x", "core")
    return jax.shard_map(
        shards,
        mesh=fine,
        in_specs=(P(clus, "z"), P(clus), P(clus)),
        out_specs=P(clus),
        check_vma=False,
    )
```

```python
import functools

import jax
import jax.numpy as jnp
from jax import lax
from jax.experimental import pallas as pl
from jax.experimental.pallas import tpu as pltpu
from jax.sharding import Mesh, PartitionSpec as P

never_order = 2.0**30
low = -3e38
Y, X, C, Z = 4, 4, 2, 8
ROWS = 3072
GROUPS = 32
CAP = 192
WIDTH = 128
PARTS = (128, 64)
SIZES = (Y * 128, Y * 64)
LINES = ROWS // 128
ALL = ("y", "x", "core", "z")
PARAMS = pltpu.CompilerParams(vmem_limit_bytes=40 * 2**20)
VMEM = pl.BlockSpec(memory_space=pltpu.VMEM)
SMEM = pl.BlockSpec(memory_space=pltpu.SMEM)


def routes(move):
    pairs = []
    for y in range(Y):
        for x in range(X):
            for c in range(C):
                for z in range(Z):
                    y2, x2, c2, z2 = move(y, x, c, z)
                    to = (((y2 % Y) * X + x2 % X) * C + c2 % C) * Z + z2 % Z
                    pairs.append((((y * X + x) * C + c) * Z + z, to))
    return pairs


def scatter_rows(spot_sm, wide_ref, out_ref, first, last):
    @pl.loop(first, last)
    def _(i):
        for lane in range(128):
            spot = spot_sm[i, lane]
            out_ref[pl.ds(spot, 1), :] = wide_ref[pl.ds(i * 128 + lane, 1), :]


def place_kernel(
    ids_any, rows_any, placed_ref, slot_ref,
    ids_ref, rows_ref, member_ref, wide_ref, out_ref, spot_ref, spot_sm, sems,
):
    ids_copy = pltpu.make_async_copy(ids_any, ids_ref, sems.at[0])
    rows_copy = pltpu.make_async_copy(rows_any, rows_ref, sems.at[1])
    ids_copy.start()
    rows_copy.start()
    out_ref[...] = jnp.zeros_like(out_ref)
    r = lax.broadcasted_iota(jnp.int32, (128, 256), 0)
    c = lax.broadcasted_iota(jnp.int32, (128, 256), 1)
    weights = ((r < c) | (c >= 128)).astype(jnp.float32).astype(jnp.bfloat16)
    group = lax.broadcasted_iota(jnp.int32, (GROUPS, 128), 0)
    ids_copy.wait()
    carry = jnp.zeros((GROUPS, 128), jnp.float32)
    copies = []
    for piece in range(LINES // 8):
        lines = range(piece * 8, piece * 8 + 8)
        for i in lines:
            hit = group == ids_ref[pl.ds(i, 1), :]
            member_ref[pl.ds(i * GROUPS, GROUPS), :] = hit.astype(jnp.float32).astype(jnp.bfloat16)
        members = member_ref[pl.ds(piece * 8 * GROUPS, 8 * GROUPS), :]
        counts = jnp.dot(members, weights, preferred_element_type=jnp.float32)
        for at, i in enumerate(lines):
            part = counts[at * GROUPS : (at + 1) * GROUPS]
            line = ids_ref[pl.ds(i, 1), :]
            within = jnp.sum(
                jnp.where(group == line, part[:, :128] + carry, 0.0), axis=0, keepdims=True
            ).astype(jnp.int32)
            slot_ref[pl.ds(i, 1), :] = line * CAP + within
            spot_ref[pl.ds(i, 1), :] = jnp.where(
                within < PARTS[0], line * PARTS[0] + within, GROUPS * PARTS[0]
            )
            carry = carry + part[:, 128:]
        rows = pl.ds(piece * 8, 8)
        copies.append(pltpu.make_async_copy(spot_ref.at[rows], spot_sm.at[rows], sems.at[2 + piece]))
        copies[piece].start()
    rows_copy.wait()
    wide_ref[...] = rows_ref[...].astype(jnp.float32)
    for piece, copy in enumerate(copies):
        copy.wait()
        scatter_rows(spot_sm, wide_ref, out_ref, piece * 8, piece * 8 + 8)
    placed_ref[...] = out_ref[pl.ds(0, GROUPS * PARTS[0]), :].astype(jnp.bfloat16)


def place(ids, rows):
    return pl.pallas_call(
        place_kernel,
        out_shape=(
            jax.ShapeDtypeStruct((GROUPS * PARTS[0], WIDTH), jnp.bfloat16),
            jax.ShapeDtypeStruct((LINES, 128), jnp.int32),
        ),
        in_specs=[pl.BlockSpec(memory_space=pltpu.HBM)] * 2,
        out_specs=(VMEM, VMEM),
        scratch_shapes=[
            pltpu.VMEM((LINES, 128), jnp.int32),
            pltpu.VMEM((ROWS, WIDTH), jnp.bfloat16),
            pltpu.VMEM((LINES * GROUPS, 128), jnp.bfloat16),
            pltpu.VMEM((ROWS, WIDTH), jnp.float32),
            pltpu.VMEM((GROUPS * PARTS[0] + 8, WIDTH), jnp.float32),
            pltpu.VMEM((LINES, 128), jnp.int32),
            pltpu.SMEM((LINES, 128), jnp.int32),
            pltpu.SemaphoreType.DMA((2 + LINES // 8,)),
        ],
        compiler_params=pltpu.CompilerParams(vmem_limit_bytes=60 * 2**20),
        name="place",
    )(ids, rows)


def place_rest_kernel(
    ids_ref, slot_ref, rows_ref, placed_ref, wide_ref, out_ref, spot_ref, spot_sm, sem
):
    ids = ids_ref[...]
    within = slot_ref[...] - ids * CAP
    spot_ref[...] = jnp.where(
        within < PARTS[0], GROUPS * PARTS[1], ids * PARTS[1] + within - PARTS[0]
    )
    copy = pltpu.make_async_copy(spot_ref, spot_sm, sem)
    copy.start()
    out_ref[...] = jnp.zeros_like(out_ref)
    wide_ref[...] = rows_ref[...].astype(jnp.float32)
    copy.wait()
    scatter_rows(spot_sm, wide_ref, out_ref, 0, LINES)
    placed_ref[...] = out_ref[pl.ds(0, GROUPS * PARTS[1]), :].astype(jnp.bfloat16)


def place_rest(ids, slots, rows):
    return pl.pallas_call(
        place_rest_kernel,
        out_shape=jax.ShapeDtypeStruct((GROUPS * PARTS[1], WIDTH), jnp.bfloat16),
        in_specs=[VMEM] * 3,
        out_specs=VMEM,
        scratch_shapes=[
            pltpu.VMEM((ROWS, WIDTH), jnp.float32),
            pltpu.VMEM((GROUPS * PARTS[1] + 8, WIDTH), jnp.float32),
            pltpu.VMEM((LINES, 128), jnp.int32),
            pltpu.SMEM((LINES, 128), jnp.int32),
            pltpu.SemaphoreType.DMA,
        ],
        compiler_params=PARAMS,
        name="place_rest",
    )(ids, slots, rows)


def ranks_kernel(ids_ref, slot_ref, orders_ref, table_ref):
    group = lax.broadcasted_iota(jnp.int32, (GROUPS, 128), 0)
    spot = lax.broadcasted_iota(jnp.int32, (CAP, 128), 0)
    total = jnp.zeros((3 * GROUPS, CAP), jnp.float32)
    for i in range(LINES):
        ids = ids_ref[pl.ds(i, 1), :]
        within = slot_ref[pl.ds(i, 1), :] - ids * CAP
        value = orders_ref[pl.ds(i, 1), :] + 1
        hit = group == ids
        digits = [
            jnp.where(hit, digit.astype(jnp.float32), 0.0)
            for digit in (value & 255, (value >> 8) & 255, value >> 16)
        ]
        left = jnp.concatenate(digits, axis=0).astype(jnp.bfloat16)
        right = (spot == within).astype(jnp.float32).astype(jnp.bfloat16)
        total = total + dot_rows(left, right)
    value = total[:GROUPS] + 256.0 * total[GROUPS : 2 * GROUPS] + 65536.0 * total[2 * GROUPS :]
    table_ref[...] = value


def ranks(ids, slots, orders):
    return pl.pallas_call(
        ranks_kernel,
        out_shape=jax.ShapeDtypeStruct((GROUPS, CAP), jnp.float32),
        in_specs=[VMEM] * 3,
        out_specs=VMEM,
        compiler_params=PARAMS,
        name="ranks",
    )(ids, slots, orders)


def dot_rows(p, q):
    return lax.dot_general(p, q, (((1,), (1,)), ((), ())), preferred_element_type=jnp.float32)


def eye():
    r = lax.broadcasted_iota(jnp.int32, (128, 128), 0)
    return r == lax.broadcasted_iota(jnp.int32, (128, 128), 1)


def to_row(col):
    pieces = []
    for i in range(col.shape[0] // 128):
        piece = jnp.broadcast_to(col[i * 128 : (i + 1) * 128], (128, 128))
        pieces.append(jnp.max(jnp.where(eye(), piece, low), axis=0, keepdims=True))
    return jnp.concatenate(pieces, axis=1)


def to_col(row):
    pieces = []
    for i in range(row.shape[1] // 128):
        piece = jnp.broadcast_to(row[:, i * 128 : (i + 1) * 128], (128, 128))
        pieces.append(jnp.max(jnp.where(eye(), piece, low), axis=1, keepdims=True))
    return jnp.concatenate(pieces, axis=0)


def part_of(ref):
    return ref.shape[0] // GROUPS


def size_of(ref):
    return Y * part_of(ref)


def rows_of(ref, start, count):
    part = part_of(ref)
    lines = []
    for y in range(start // part, (start + count) // part):
        pieces = [ref[pl.ds((y * Z + z) * part, part), :] for z in range(Z)]
        lines.append(jnp.concatenate(pieces, axis=1))
    return jnp.concatenate(lines, axis=0)


def note(inverses, name, ref):
    part = part_of(ref)
    cols = []
    for y in range(Y):
        total = jnp.zeros((part, WIDTH), jnp.float32)
        for z in range(Z):
            wide = ref[pl.ds((y * Z + z) * part, part), :].astype(jnp.float32)
            total = total + wide * wide
        cols.append(lax.rsqrt(jnp.sum(total, axis=1, keepdims=True) + 1e-06))
    inverses[pl.ds(name, 1), pl.ds(0, Y * part)] = to_row(jnp.concatenate(cols, axis=0))


def meet(best, inverses, ranks, ps, others):
    sizes = [size_of(ref) for _, ref in ps]
    inv_p, rank_p = (
        jnp.concatenate(
            [to_col(rows[pl.ds(name, 1), pl.ds(0, size)]) for (name, _), size in zip(ps, sizes)]
        )
        for rows in (inverses, ranks)
    )
    p_best = jnp.full((sum(sizes), 128), low, jnp.float32)
    for q_name, q_ref in others:
        q_best = []
        for j in range(0, size_of(q_ref), 256):
            at = (pl.ds(q_name, 1), pl.ds(j, 256))
            p = jnp.concatenate([rows_of(ref, 0, size) for (_, ref), size in zip(ps, sizes)])
            s = dot_rows(p, rows_of(q_ref, j, 256))
            s = s * inv_p * inverses[at]
            earlier = ranks[at] < rank_p
            mine = jnp.where(earlier, s, low)
            p_best = jnp.maximum(p_best, jnp.maximum(mine[:, :128], mine[:, 128:]))
            if q_name != ps[0][0]:
                q_best.append(jnp.max(jnp.where(earlier, low, s), axis=0, keepdims=True))
        if q_best:
            record(best, q_name, jnp.concatenate(q_best, axis=1))
    start = 0
    for (name, _), size in zip(ps, sizes):
        record(best, name, to_row(jnp.max(p_best[start : start + size], axis=1, keepdims=True)))
        start += size


def by_place(spots, run):
    for core in range(2):
        for side in range(2):

            @pl.when((spots[0] == core) & (spots[1] == side))
            def _():
                run(core, side)


def record(best, name, row):
    at = (pl.ds(name, 1), pl.ds(0, row.shape[1]))
    best[at] = jnp.maximum(best[at], row)


O1, O2, U1, U2, V1, V2, E1, E2, W1, W2 = range(10)


def own_kernel(spots, ranks, o1, e1, best, inverses):
    best[...] = jnp.full_like(best, -1.0)
    inverses[...] = jnp.zeros_like(inverses)
    note(inverses, O1, o1)
    note(inverses, E1, e1)

    meet(best, inverses, ranks, [(O1, o1)], [(O1, o1)])


def near_kernel(spots, ranks, o1, u1, e1, before, known, best, inverses):
    best[...] = before[...]
    inverses[...] = known[...]
    note(inverses, U1, u1)

    @pl.when(spots[0] == 0)
    def _():
        meet(best, inverses, ranks, [(O1, o1)], [(U1, u1), (E1, e1)])

    @pl.when(spots[0] != 0)
    def _():
        meet(best, inverses, ranks, [(U1, u1)], [(O1, o1), (E1, e1)])


def second_kernel(spots, ranks, o1, o2, u1, v1, e1, e2, w1, before, known, best, inverses):
    best[...] = before[...]
    inverses[...] = known[...]
    note(inverses, V1, v1)
    note(inverses, W1, w1)
    note(inverses, O2, o2)
    note(inverses, E2, e2)
    meet(best, inverses, ranks, [(O2, o2), (E2, e2)], [(O1, o1), (U1, u1), (V1, v1)])

    def run(core, side):
        meet(best, inverses, ranks, [(O2, o2)], [(O2, o2)] + [(E2, e2)] * core)
        if side:
            meet(best, inverses, ranks, [(V1, v1)], [(E1, e1)] * (1 - core) + [(U1, u1)])
        else:
            if core == 0:
                meet(best, inverses, ranks, [(V1, v1)], [(E1, e1)])
            meet(best, inverses, ranks, [(W1, w1)], [(U1, u1)])

    by_place(spots, run)


def third_kernel(spots, ranks, o2, u2, e2, v1, w1, before, known, best, inverses):
    best[...] = before[...]
    inverses[...] = known[...]
    note(inverses, U2, u2)

    def run(core, side):
        others = [(O2, o2), (V1, v1) if side else (W1, w1)] + [(E2, e2)] * core
        meet(best, inverses, ranks, [(U2, u2)], others)

    by_place(spots, run)


def give(best, name, out, start):
    for y in range(Y):
        at = pl.ds(start + y, 1)
        out[at, pl.ds(0, PARTS[0])] = best[pl.ds(name, 1), pl.ds(y * PARTS[0], PARTS[0])]
        pair = best[pl.ds(name + 1, 1), pl.ds(y // 2 * 128, 128)]
        pair = pltpu.roll(pair, 64, 1) if y % 2 else pair
        out[at, pl.ds(PARTS[0], PARTS[1])] = pair[:, : PARTS[1]]


def fourth_kernel(
    spots, ranks, u1, u2, v2, e2, w2, before, known, mine, others, v_best, best, inverses
):
    best[...] = before[...]
    inverses[...] = known[...]
    note(inverses, V2, v2)

    def run(core, side):
        if side:
            others = [(E2, e2)] * (1 - core) + [(U1, u1), (U2, u2)]
            meet(best, inverses, ranks, [(V2, v2)], others)
        else:
            note(inverses, W2, w2)
            if core == 0:
                meet(best, inverses, ranks, [(V2, v2)], [(E2, e2)])
            meet(best, inverses, ranks, [(W2, w2)], [(U1, u1), (U2, u2)])

    by_place(spots, run)

    give(best, O1, mine, 0)
    give(best, U1, mine, Y)
    give(best, E1, others, 0)
    give(best, W1, others, Y)
    give(best, V1, v_best, 0)


def is_dims(item):
    return isinstance(item, tuple) and isinstance(item[0], int)


def scores_call(kernel, units, inputs, out, scratch, name):
    return pl.pallas_call(
        kernel,
        out_shape=jax.tree.map(lambda dims: jax.ShapeDtypeStruct(dims, jnp.float32), out, is_leaf=is_dims),
        in_specs=[SMEM] + [VMEM] * (len(inputs) - 1),
        out_specs=jax.tree.map(lambda _: VMEM, out, is_leaf=is_dims),
        scratch_shapes=scratch,
        compiler_params=PARAMS,
        cost_estimate=pl.CostEstimate(
            flops=int(units * 2 * 256 * 256 * 1024), bytes_accessed=4 * 2**20, transcendentals=0
        ),
        name=name,
    )(*inputs)


def answer_kernel(ids_ref, slot_ref, table_ref, out_ref):
    table = table_ref[...]
    high = table.astype(jnp.bfloat16)
    rest = table - high.astype(jnp.float32)
    middle = rest.astype(jnp.bfloat16)
    small = (rest - middle.astype(jnp.float32)).astype(jnp.bfloat16)
    pieces = jnp.concatenate([high, middle, small], axis=0)
    group = lax.broadcasted_iota(jnp.int32, (3 * GROUPS, 128), 0) & (GROUPS - 1)
    place_in = lax.broadcasted_iota(jnp.int32, (CAP, 128), 0)
    for first in range(0, LINES, 4):
        lines = range(first, first + 4)
        member = jnp.concatenate(
            [(group == ids_ref[pl.ds(i, 1), :]).astype(jnp.float32) for i in lines], axis=1
        ).astype(jnp.bfloat16)
        found = lax.dot_general(
            pieces, member, (((0,), (0,)), ((), ())), preferred_element_type=jnp.float32
        )
        for at, i in enumerate(lines):
            within = slot_ref[pl.ds(i, 1), :] - ids_ref[pl.ds(i, 1), :] * CAP
            out_ref[pl.ds(i, 1), :] = jnp.sum(
                jnp.where(place_in == within, found[:, at * 128 : (at + 1) * 128], 0.0),
                axis=0,
                keepdims=True,
            )


def answer(ids, slots, table):
    return pl.pallas_call(
        answer_kernel,
        out_shape=jax.ShapeDtypeStruct((LINES, 128), jnp.float32),
        in_specs=[VMEM] * 3,
        out_specs=VMEM,
        compiler_params=PARAMS,
        name="answer",
    )(ids, slots, table)


def shards(embeds, cluster_ids, orders):
    y, x, core, z = (lax.axis_index(name) for name in ALL)
    swap = routes(lambda y, x, c, z: (y, x, 1 - c, z))
    ahead = routes(lambda y, x, c, z: (y, x + 1 - 2 * c, c, z))
    behind = routes(lambda y, x, c, z: (y, x - 1 + 2 * c, c, z))

    def bring(rows):
        part = rows.shape[0] // GROUPS
        return lax.all_to_all(
            rows.reshape(GROUPS, part, WIDTH), ("y", "z"), split_axis=0, concat_axis=0, tiled=True
        ).reshape(GROUPS * part, WIDTH)

    ids = cluster_ids.reshape(LINES, 128)
    placed1, slots = place(ids, embeds)
    o1 = bring(placed1)
    placed2 = place_rest(ids, slots, embeds)

    table = ranks(ids, slots, orders.reshape(LINES, 128)).reshape(Y, Z, CAP)
    table = lax.dynamic_index_in_dim(table, z, 1, keepdims=False)
    rank_parts = []
    for j in range(Y):
        row = lax.dynamic_slice_in_dim(table, (y + j) % Y, 1, 0)
        if j:
            row = lax.ppermute(row, ALL, routes(lambda y, x, c, z: (y + j, x, c, z)))
        rank_parts.append(row)
    own_ranks = jnp.concatenate(rank_parts)[(y - jnp.arange(Y)) % Y]
    own_ranks = jnp.where(own_ranks > 0, own_ranks, never_order)
    own_ranks = jnp.stack(
        [
            own_ranks[:, : PARTS[0]].reshape(SIZES[0]),
            jnp.pad(own_ranks[:, PARTS[0] :].reshape(SIZES[1]), (0, SIZES[0] - SIZES[1])),
        ]
    )
    near_ranks = lax.ppermute(own_ranks, ALL, ahead)
    member_ranks = jnp.concatenate(
        [
            own_ranks,
            near_ranks,
            lax.ppermute(own_ranks, ALL, behind),
            lax.ppermute(own_ranks, ALL, swap),
            lax.ppermute(near_ranks, ALL, swap),
            jnp.zeros((6, SIZES[0]), jnp.float32),
        ]
    )
    spots = jnp.stack([core, ((x < X // 2) == (core == 0)).astype(jnp.int32)]).astype(jnp.int32)
    o1, placed2, member_ranks, spots = lax.optimization_barrier((o1, placed2, member_ranks, spots))
    o2 = bring(placed2)

    wide = (16, SIZES[0])

    def score(kernel, units, blocks, state, name, out=(wide, wide), scratch=()):
        inputs = (spots, member_ranks, *blocks, *state)
        return scores_call(kernel, units, inputs, list(out), list(scratch), name)

    u1 = lax.ppermute(o1, ALL, ahead)
    v1 = lax.ppermute(o1, ALL, behind)
    e1 = lax.ppermute(o1, ALL, swap)
    state = score(own_kernel, 8, (o1, e1), (), "own")
    u1, *state = lax.optimization_barrier((u1, *state))
    w1 = lax.ppermute(u1, ALL, swap)
    o2, *state = lax.optimization_barrier((o2, *state))

    u2 = lax.ppermute(o2, ALL, ahead)
    e2 = lax.ppermute(o2, ALL, swap)
    state = score(near_kernel, 6, (o1, u1, e1), state, "near")
    o2, *state = lax.optimization_barrier((o2, *state))
    v2 = lax.ppermute(o2, ALL, behind)
    state = score(second_kernel, 20, (o1, o2, u1, v1, e1, e2, w1), state, "second")
    u2, *state = lax.optimization_barrier((u2, *state))
    w2 = lax.ppermute(u2, ALL, swap)
    state = score(third_kernel, 4, (o2, u2, e2, v1, w1), state, "third")
    v2, *state = lax.optimization_barrier((v2, *state))
    mine, others, v_best = score(
        fourth_kernel, 4, (u1, u2, v2, e2, w2), state, "fourth",
        [(2 * Y, CAP), (2 * Y, CAP), (Y, CAP)], [pltpu.VMEM(wide, jnp.float32)] * 2,
    )
    v_best = lax.ppermute(v_best, ALL, ahead)
    mine = jnp.maximum(mine, lax.ppermute(others, ALL, swap))
    own = jnp.maximum(mine[:Y], v_best)
    own = jnp.maximum(own, lax.ppermute(mine[Y:], ALL, behind))
    table = lax.all_to_all(
        jnp.broadcast_to(own[:, None], (Y, Z, CAP)).reshape(GROUPS, CAP),
        ("y", "z"), split_axis=0, concat_axis=0, tiled=True,
    )
    return answer(ids, slots, table).reshape(ROWS)


def solution(mesh):
    fine = Mesh(mesh.devices.reshape(Y, X, C, Z), ALL)
    clus = ("y", "x", "core")
    return jax.shard_map(
        shards,
        mesh=fine,
        in_specs=(P(clus, "z"), P(clus), P(clus)),
        out_specs=P(clus),
        check_vma=False,
    )
```
